32 devices in a mesh: slab: 4 (over y, x), energy: 8 (over z, core).
Axes of the slice: x: 2, y: 2, z: 4, core: 2. Of those that a mesh axis runs over, the one named last changes fastest.
Arguments:
- link_p: float32 [12, 2, 64, 64], P('slab'), may hold values from -1 to 2, as said below
- link_q: float32 [12, 2, 64, 64], P('slab'), may hold values from -1 to 2, as said below
- shift: float32 [64, 12, 64], P('energy', 'slab'), may hold values from 0.01 to 0.3
- lesser_gain: float32 [64, 12, 64], P('energy', 'slab'), may hold values from 0.1 to 2
- sources: float32 [12, 2, 64, 128], P('slab'), may hold values from -1.8 to 1.8
Outputs:
- polar: float32 [2, 64, 12, 64, 128], P(None, None, 'slab', 'energy')
The draws below stay inside these ranges and needn't reach their ends.
Inputs may be any that keep to these rules, and one draw needn't show every extreme that they name: `link_p`: real and imaginary parts of complex link factors. `link_q`: real and imaginary parts of complex link factors.
All inputs are finite; a program needn't handle non-finite values.
Results may differ from the reference program's by a relative error of at most 0.0003.
Values sent between devices are 32-bit elements; how exact they have to be, the bound alone decides.
No kernel may reach another device: no remote copies, remote signals or barrier semaphores. Data moves between devices by JAX's collectives and lax.ppermute only.
A program may use at most 128 MiB of HBM per device.

```python
import math
import jax
import jax.numpy as jnp
from jax import lax

ORB = 64
R = 128
NE = 64
NSLAB = 12


def link_factor(key):
    noise = jnp.clip(jax.random.normal(key, (NSLAB, 2, ORB, ORB), jnp.float32), -4.0, 4.0)
    noise = noise * (0.35 / math.sqrt(ORB))
    identity = jnp.eye(ORB, dtype=jnp.float32)
    return noise.at[:, 0].add(identity)


def draw_link_p(key, part):
    return link_factor(jax.random.fold_in(key, 11))


def draw_link_q(key, part):
    return link_factor(jax.random.fold_in(key, 23))


def level_of(key, extent, split, least, top_value):
    loudness = 1.0
    for dim, shards_of in split:
        steps = jax.random.uniform(jax.random.fold_in(jax.random.fold_in(key, 6), dim), (shards_of,), jnp.float32, least / len(split), top_value / len(split))
        loudness = loudness * jnp.repeat(jnp.exp(steps), extent[dim] // shards_of).reshape((-1,) + (1,) * (len(extent) - 1 - dim))
    return loudness


def bell_draw(stream_key, extent, deviation, bound, cuts=(), kind=jnp.bfloat16):
    drawn = jax.random.normal(stream_key, extent, jnp.float32) * deviation
    if len(cuts) > 0:
        drawn = level_of(stream_key, extent, cuts, -0.22, 0.18) * drawn
    return jnp.clip(drawn, min=-bound, max=bound).astype(kind)


def setup_inputs(seed: int = 0) -> dict:
    arg_keys = jax.random.split(jax.random.key(seed), 6)
    link_p = draw_link_p(jax.random.fold_in(arg_keys[5], 71), 0)
    link_q = draw_link_q(jax.random.fold_in(arg_keys[5], 71), 0)
    shift = jnp.clip(jnp.exp(math.log(0.3) - 3.4011974 * jax.random.uniform(arg_keys[2], (NE, NSLAB, ORB), jnp.float32) ** level_of(arg_keys[2], (NE, NSLAB, ORB), ((0, 8), (1, 4)), -0.2, 0.2)), 0.01, 0.3)
    lesser_gain = jnp.clip(jnp.exp(math.log(2.0) - 2.9957323 * jax.random.uniform(arg_keys[3], (NE, NSLAB, ORB), jnp.float32) ** level_of(arg_keys[3], (NE, NSLAB, ORB), ((0, 8), (1, 4)), -0.2, 0.2)), 0.1, 2.0)
    sources = bell_draw(arg_keys[4], (NSLAB, 2, ORB, R), 0.3, 1.8, ((0, 4),), jnp.float32)
    return dict(link_p=link_p, link_q=link_q, shift=shift, lesser_gain=lesser_gain, sources=sources)


HIGHEST = lax.Precision.HIGHEST

def real_form(part):
    real = part[..., 0, :, :]
    imag = part[..., 1, :, :]
    upper_half = jnp.concatenate([real, -imag], axis=-1)
    lower_half = jnp.concatenate([imag, real], axis=-1)
    return jnp.concatenate([upper_half, lower_half], axis=-2)

def right_transposed(left, right):
    return jnp.einsum('...ij,...kj->...ik', left, right, precision=HIGHEST)

def left_transposed(left, right):
    return jnp.einsum('...ji,...jk->...ik', left, right, precision=HIGHEST)

def product(left, right):
    return jnp.einsum('...ij,...jk->...ik', left, right, precision=HIGHEST)

def solve_with(factor, rhs):
    return jax.scipy.linalg.cho_solve((factor, True), rhs)

def chain(diag, upper, sources_flat, gain_row):
    upper_full = jnp.concatenate([upper, jnp.zeros_like(upper[:1])], axis=0)

    def factor_step(carry, pieces):
        block, link_block = pieces
        factor = jnp.linalg.cholesky(block - carry)
        step = solve_with(factor, link_block)
        return (left_transposed(link_block, step), (factor, step))
    unused, stored = lax.scan(factor_step, jnp.zeros_like(diag[0]), (diag, upper_full))
    factors, steps = stored

    def solve(rhs):

        def down(carry, pieces):
            factor, link_block, rhs_row = pieces
            solved = solve_with(factor, rhs_row - carry)
            return (left_transposed(link_block, solved), solved)
        unused_down, partial_rows = lax.scan(down, jnp.zeros_like(rhs[0]), (factors, upper_full, rhs))

        def climb(carry, pieces):
            step, partial_row = pieces
            value = partial_row - product(step, carry)
            return (value, value)
        unused_up, values = lax.scan(climb, jnp.zeros_like(rhs[0]), (steps, partial_rows), reverse=True)
        return values
    retarded = solve(sources_flat)
    lesser = solve(gain_row[..., None] * retarded)
    return (retarded, lesser)

def reference(link_p, link_q, shift, lesser_gain, sources):
    width = 2 * ORB
    rp = real_form(link_p)
    rq = real_form(link_q)
    pp = right_transposed(rp, rp)
    qq = right_transposed(rq, rq)
    cc = -right_transposed(rp, rq)
    base = qq + jnp.concatenate([pp[1:], jnp.zeros_like(pp[:1])], axis=0)
    base = base.at[0].add(pp[0])
    upper = cc[1:]
    eye = jnp.eye(width, dtype=jnp.float32)
    shift_two = jnp.concatenate([shift, shift], axis=-1)
    gain_two = jnp.concatenate([lesser_gain, lesser_gain], axis=-1)
    sources_flat = sources.reshape(NSLAB, width, R)

    def per_energy(pieces):
        shift_row, gain_row = pieces
        diag = base + eye * shift_row[:, None, :]
        retarded, lesser = chain(diag, upper, sources_flat, gain_row)
        ret_real = retarded[:, :ORB]
        ret_imag = retarded[:, ORB:]
        les_real = lesser[:, :ORB]
        les_imag = lesser[:, ORB:]
        return (ret_real * les_real + ret_imag * les_imag, ret_real * les_imag - ret_imag * les_real, ret_real * ret_real + ret_imag * ret_imag)
    lesser_re, lesser_im, power = lax.map(per_energy, (shift_two, gain_two))
    padded_re = jnp.concatenate([lesser_re, jnp.zeros_like(lesser_re)], axis=0)
    padded_im = jnp.concatenate([lesser_im, jnp.zeros_like(lesser_im)], axis=0)

    def lag(offset):
        part_re = lax.dynamic_slice_in_dim(padded_re, offset, NE, 0)
        part_im = lax.dynamic_slice_in_dim(padded_im, offset, NE, 0)
        return (jnp.sum(part_re * power, axis=0), jnp.sum(part_im * power, axis=0))
    corr_re, corr_im = lax.map(lag, jnp.arange(NE, dtype=jnp.int32))
    return jnp.stack([corr_re, corr_im], axis=0) / NE
```

```python
import functools

import jax
import jax.numpy as jnp
from jax import lax
from jax.experimental import pallas as pl
from jax.experimental.pallas import tpu as pltpu
from jax.sharding import PartitionSpec as P

HIGHEST = lax.Precision.HIGHEST
F32 = jnp.float32
VMEM_LIMIT = 56 * 1024 * 1024
PANEL = 8


def elimination_levels(count):
    levels = []
    chain = list(range(count))
    while len(chain) > 1:
        level = []
        for place in range(0, len(chain), 2):
            left = chain[place - 1] if place > 0 else None
            right = chain[place + 1] if place + 1 < len(chain) else None
            level.append((chain[place], left, right))
        levels.append(level)
        chain = chain[1::2]
    return levels, chain[0]


def mm(a, b):
    return lax.dot_general(a, b, (((1,), (0,)), ((), ())), precision=HIGHEST, preferred_element_type=F32)


def mm_nt(a, b):
    return lax.dot_general(a, b, (((1,), (1,)), ((), ())), precision=HIGHEST, preferred_element_type=F32)


def half_roll(x):
    return pltpu.roll(x, x.shape[1] // 2, 1)


def invert_batch(mat_ref, members, orbits):
    width = 2 * orbits
    blocks = orbits // PANEL
    lane = lax.broadcasted_iota(jnp.int32, (PANEL, width), 1)
    sub = lax.broadcasted_iota(jnp.int32, (PANEL, width), 0)
    pivots = (lane < PANEL) | ((lane >= orbits) & (lane < orbits + PANEL))

    def panel(p, unused):
        rows = pl.ds(pl.multiple_of(p * PANEL, PANEL), PANEL)
        original = lax.rem(lane + p * PANEL, width)
        sign = jnp.where(original < orbits, -1.0, 1.0).astype(F32)
        tops = []
        for m in members:
            tops.append(mat_ref[m, rows, :])
        for k in range(PANEL):
            here = sub == k
            at_pivot = (lane == k) | (lane == orbits + k)
            unit = jnp.where(here & (lane == k), 1.0, 0.0).astype(F32)
            for n in range(len(tops)):
                r = tops[n]
                cr = jnp.broadcast_to(r[:, k : k + 1], r.shape)
                ci = jnp.broadcast_to(r[:, orbits + k : orbits + k + 1], r.shape)
                inv = 1.0 / cr[k : k + 1, :]
                r0 = jnp.where(at_pivot, unit, r)
                row = r0[k : k + 1, :] * inv
                hat = half_roll(r0)[k : k + 1, :] * (sign[k : k + 1, :] * inv)
                tops[n] = jnp.where(here, row, r0 - cr * row - ci * hat)
        for n, m in enumerate(members):
            r = tops[n]
            hat = half_roll(r) * sign
            for i in range(blocks):
                block = mat_ref[m, PANEL * i : PANEL * (i + 1), :]
                out = jnp.where(pivots, 0.0, block)
                for j in range(PANEL):
                    out = out - jnp.broadcast_to(block[:, j : j + 1], out.shape) * r[j : j + 1, :]
                    out = out - jnp.broadcast_to(block[:, orbits + j : orbits + j + 1], out.shape) * hat[j : j + 1, :]
                mat_ref[m, PANEL * i : PANEL * (i + 1), :] = pltpu.roll(out, width - PANEL, 1)
            mat_ref[m, rows, :] = pltpu.roll(r, width - PANEL, 1)
        return 0

    lax.fori_loop(0, blocks, panel, 0)


def solve_kernel(plan, first_ref, data_ref, out_ref, mat, rhs, inv, w1, w2, sol, up1, dn1, up2, dn2):
    (slabs, mine, orbits, groups, energy_groups, per, orb_per) = plan
    width = 2 * orbits
    levels, root = elimination_levels(slabs)
    lane = lax.broadcasted_iota(jnp.int32, (orbits, width), 1)
    sub = lax.broadcasted_iota(jnp.int32, (orbits, width), 0)
    low = lane < orbits
    diag_lane = lane == sub
    gain_lane = lane == sub + orbits
    first = first_ref[0]

    def real_rows(z):
        return jnp.concatenate([jnp.where(low, z, -z), half_roll(z)], axis=0)

    def trans_rows(z):
        return jnp.concatenate([z, jnp.where(low, -half_roll(z), half_roll(z))], axis=0)

    def real_left(t):
        top, bottom = t[:orbits], t[orbits:]
        return jnp.concatenate(
            [jnp.where(low, top, -half_roll(bottom)), jnp.where(low, bottom, half_roll(top))], axis=0
        )

    def real_right(t):
        top, bottom = t[:orbits], t[orbits:]
        return jnp.concatenate(
            [jnp.where(low, half_roll(top), -bottom), jnp.where(low, half_roll(bottom), top)], axis=0
        )

    def packed_left(t):
        return jnp.where(low, t[:orbits], half_roll(t[orbits:]))

    def packed_right(t):
        return jnp.where(low, half_roll(t[:orbits]), t[orbits:])

    def factor_p(s):
        return data_ref[s, 0:orbits, :]

    def factor_q(s):
        return data_ref[s, orbits : 2 * orbits, :]

    def settings(s, e):
        return data_ref[s, pl.ds(4 * orbits + first + e, 1), :]

    for s in range(slabs):
        zq = factor_q(s)
        base = mm_nt(zq, trans_rows(zq))
        if s + 1 < slabs:
            zp = factor_p(s + 1)
            base = base + mm_nt(zp, trans_rows(zp))
            rp = real_rows(zp)
            rq = real_rows(factor_q(s + 1))
            up1[s] = -mm_nt(rp, rq)
            dn1[s] = -mm_nt(rq, rp)
        if s == 0:
            zp = factor_p(0)
            base = base + mm_nt(zp, trans_rows(zp))
        for e in range(mine):
            mat[s * mine + e] = base + jnp.where(diag_lane, settings(s, e), 0.0)
            rhs[s * mine + e] = data_ref[s, 2 * orbits : 4 * orbits, :]

    links = {}
    for s in range(slabs - 1):
        for e in range(mine):
            links[(0, s, s + 1, e)] = (up1, dn1, s)
    spare = 0
    for depth, level in enumerate(levels):
        for node, left, right in level:
            if left is not None and right is not None:
                for e in range(mine):
                    links[(depth + 1, left, right, e)] = (up2, dn2, spare)
                    spare += 1

    def links_of(depth, node, left, right, e):
        from_left = from_right = None
        if left is not None:
            refs = links[(depth, left, node, e)]
            from_left = refs[0][refs[2]]
        if right is not None:
            refs = links[(depth, node, right, e)]
            from_right = refs[1][refs[2]]
        return from_left, from_right

    def couplings(depth, node, left, right, e):
        pieces = [None, None]
        if left is not None:
            refs = links[(depth, left, node, e)]
            pieces[0] = refs[1][refs[2]]
        if right is not None:
            refs = links[(depth, node, right, e)]
            pieces[1] = half_roll(refs[0][refs[2]])
        low_all = lax.broadcasted_iota(jnp.int32, (width, width), 1) < orbits
        if pieces[0] is None:
            return jnp.where(low_all, 0.0, pieces[1])
        if pieces[1] is None:
            return jnp.where(low_all, pieces[0], 0.0)
        return jnp.where(low_all, pieces[0], pieces[1])

    def expand_inverse(m):
        inv[m] = real_rows(half_roll(mat[m]))

    for depth, level in enumerate(levels):
        invert_batch(mat, [node * mine + e for node, _, _ in level for e in range(mine)], orbits)
        for node, left, right in level:
            for e in range(mine):
                m = node * mine + e
                expand_inverse(m)
                stacked = jnp.concatenate([couplings(depth, node, left, right, e), rhs[m]], axis=1)
                step = mm(inv[m], stacked)
                links_step, rhs_step = step[:, :width], step[:, width:]
                from_left, from_right = links_of(depth, node, left, right, e)
                sol[m] = rhs_step
                if left is not None:
                    w1[m] = real_left(links_step)
                    change = mm(from_left, step)
                    ml = left * mine + e
                    mat[ml] = mat[ml] - packed_left(change[:, :width])
                    rhs[ml] = rhs[ml] - change[:, width:]
                    if right is not None:
                        refs = links[(depth + 1, left, right, e)]
                        refs[0][refs[2]] = -real_right(change[:, :width])
                if right is not None:
                    w2[m] = real_right(links_step)
                    change = mm(from_right, step)
                    mr = right * mine + e
                    mat[mr] = mat[mr] - packed_right(change[:, :width])
                    rhs[mr] = rhs[mr] - change[:, width:]
                    if left is not None:
                        refs = links[(depth + 1, left, right, e)]
                        refs[1][refs[2]] = -real_left(change[:, :width])
    invert_batch(mat, [root * mine + e for e in range(mine)], orbits)
    for e in range(mine):
        m = root * mine + e
        expand_inverse(m)
        sol[m] = mm(inv[m], rhs[m])

    def climb():
        for level in reversed(levels):
            for node, left, right in level:
                for e in range(mine):
                    m = node * mine + e
                    if left is not None and right is not None:
                        both = jnp.concatenate([w1[m], w2[m]], axis=1)
                        sides = jnp.concatenate([sol[left * mine + e], sol[right * mine + e]], axis=0)
                        sol[m] = sol[m] - mm(both, sides)
                    elif left is not None:
                        sol[m] = sol[m] - mm(w1[m], sol[left * mine + e])
                    elif right is not None:
                        sol[m] = sol[m] - mm(w2[m], sol[right * mine + e])

    climb()

    def deliver(what, s, e, value):
        for j in range(energy_groups):
            out_ref[s // per, j, what, e, s % per, :, :] = value[j * orb_per : (j + 1) * orb_per, :]

    for s in range(slabs):
        for e in range(mine):
            m = s * mine + e
            gain = jnp.sum(jnp.where(gain_lane, settings(s, e), 0.0), axis=1, keepdims=True)
            x = sol[m]
            rhs[m] = x * jnp.concatenate([gain, gain], axis=0)
            inverse_left = x
            keep = inverse_left
            xr, xi = keep[:orbits], keep[orbits:]
            deliver(2, s, e, xr * xr + xi * xi)
    ret = {}
    for s in range(slabs):
        for e in range(mine):
            ret[(s, e)] = s * mine + e
    return (levels, root, ret, links_of, climb, deliver)


def kernel_body(plan, first_ref, data_ref, out_ref, mat, rhs, inv, w1, w2, sol, up1, dn1, up2, dn2, kept):
    (slabs, mine, orbits, groups, energy_groups, per, orb_per) = plan
    levels, root, _, links_of, climb, deliver = solve_kernel(
        plan, first_ref, data_ref, out_ref, mat, rhs, inv, w1, w2, sol, up1, dn1, up2, dn2
    )
    for m in range(slabs * mine):
        kept[m] = sol[m]
    for depth, level in enumerate(levels):
        for node, left, right in level:
            for e in range(mine):
                m = node * mine + e
                step = mm(inv[m], rhs[m])
                sol[m] = step
                from_left, from_right = links_of(depth, node, left, right, e)
                if left is not None:
                    ml = left * mine + e
                    rhs[ml] = rhs[ml] - mm(from_left, step)
                if right is not None:
                    mr = right * mine + e
                    rhs[mr] = rhs[mr] - mm(from_right, step)
    for e in range(mine):
        m = root * mine + e
        sol[m] = mm(inv[m], rhs[m])
    climb()
    for s in range(slabs):
        for e in range(mine):
            m = s * mine + e
            x, y = kept[m], sol[m]
            xr, xi, yr, yi = x[:orbits], x[orbits:], y[:orbits], y[orbits:]
            deliver(0, s, e, xr * yr + xi * yi)
            deliver(1, s, e, xr * yi - xi * yr)


def solve_slabs(first, data, plan):
    (slabs, mine, orbits, groups, energy_groups, per, orb_per) = plan
    width = 2 * orbits
    columns = data.shape[-1]
    nodes = slabs * mine
    levels, _ = elimination_levels(slabs)
    fills = mine * sum(1 for level in levels for _, a, b in level if a is not None and b is not None)
    square = (width, width)
    return pl.pallas_call(
        functools.partial(kernel_body, plan),
        out_shape=jax.ShapeDtypeStruct((groups, energy_groups, 3, mine, per, orb_per, columns), F32),
        in_specs=[
            pl.BlockSpec(memory_space=pltpu.SMEM),
            pl.BlockSpec(memory_space=pltpu.VMEM),
        ],
        out_specs=pl.BlockSpec(memory_space=pltpu.VMEM),
        scratch_shapes=[
            pltpu.VMEM((nodes, orbits, width), F32),
            pltpu.VMEM((nodes, width, columns), F32),
            pltpu.VMEM((nodes,) + square, F32),
            pltpu.VMEM((nodes,) + square, F32),
            pltpu.VMEM((nodes,) + square, F32),
            pltpu.VMEM((nodes, width, columns), F32),
            pltpu.VMEM((slabs - 1,) + square, F32),
            pltpu.VMEM((slabs - 1,) + square, F32),
            pltpu.VMEM((fills,) + square, F32),
            pltpu.VMEM((fills,) + square, F32),
            pltpu.VMEM((nodes, width, columns), F32),
        ],
        compiler_params=pltpu.CompilerParams(vmem_limit_bytes=VMEM_LIMIT),
        name="solve_slabs",
    )(first, data)


def correlate_kernel(order, got_ref, out_ref):
    count = len(order)
    window = 8
    scale = 1.0 / count
    for start in range(0, count, window):
        span = min(window, count - start)
        acc_re = [None] * span
        acc_im = [None] * span
        reach = count - start
        lead = {}
        for energy in range(reach):
            sender, place = order[energy]
            power = got_ref[sender, 2, place, 0]
            for w in range(span):
                at = energy + start + w
                if at >= count:
                    continue
                if at not in lead:
                    s2, p2 = order[at]
                    lead[at] = (got_ref[s2, 0, p2, 0], got_ref[s2, 1, p2, 0])
                re, im = lead[at]
                acc_re[w] = re * power if acc_re[w] is None else acc_re[w] + re * power
                acc_im[w] = im * power if acc_im[w] is None else acc_im[w] + im * power
        for w in range(span):
            out_ref[0, start + w, 0] = acc_re[w] * scale
            out_ref[1, start + w, 0] = acc_im[w] * scale


def correlate(got, order):
    senders, kinds, mine, per, rows, columns = got.shape
    count = len(order)
    return pl.pallas_call(
        functools.partial(correlate_kernel, order),
        grid=(per,),
        out_shape=jax.ShapeDtypeStruct((2, count, per, rows, columns), F32),
        in_specs=[pl.BlockSpec((senders, kinds, mine, 1, rows, columns), lambda i: (0, 0, 0, i, 0, 0))],
        out_specs=pl.BlockSpec((2, count, 1, rows, columns), lambda i: (0, 0, i, 0, 0)),
        compiler_params=pltpu.CompilerParams(vmem_limit_bytes=VMEM_LIMIT),
        name="correlate",
    )(got)


def per_device(link_p, link_q, shift, lesser_gain, sources):
    per, _, orbits, _ = link_p.shape
    width = 2 * orbits
    columns = sources.shape[-1]
    local = shift.shape[0]
    groups = lax.axis_size("slab")
    energy_groups = lax.axis_size("energy")
    slabs = per * groups
    mine = max(1, local // groups)
    owner = lax.axis_index("slab")
    packed = jnp.concatenate(
        [
            jnp.concatenate([link_p[:, 0], link_p[:, 1]], axis=-1),
            jnp.concatenate([link_q[:, 0], link_q[:, 1]], axis=-1),
            sources.reshape(per, width, columns),
            jnp.swapaxes(jnp.concatenate([shift, lesser_gain], axis=-1), 0, 1),
        ],
        axis=1,
    )
    data = lax.all_gather(packed, "slab", axis=0, tiled=True)
    first = (owner * local // groups).astype(jnp.int32).reshape(1)
    plan = (slabs, mine, orbits, groups, energy_groups, per, orbits // energy_groups)
    sent = solve_slabs(first, data, plan)
    sent = sent.reshape((groups * energy_groups,) + sent.shape[2:])
    got = lax.all_to_all(sent, ("slab", "energy"), split_axis=0, concat_axis=0, tiled=True)
    order = []
    for group in range(energy_groups):
        for row in range(local):
            if local >= groups:
                holder, place = row // mine, row % mine
            else:
                holder, place = -(-row * groups // local), 0
            order.append((holder * energy_groups + group, place))
    return correlate(got, tuple(order))


def solution(mesh):
    placed = (
        P("slab", None, None, None),
        P("slab", None, None, None),
        P("energy", "slab", None),
        P("energy", "slab", None),
        P("slab", None, None, None),
    )
    return jax.shard_map(
        per_device,
        mesh=mesh,
        in_specs=placed,
        out_specs=P(None, None, "slab", "energy", None),
        check_vma=False,
    )
```

```python
import functools

import jax
import jax.numpy as jnp
from jax import lax
from jax.experimental import pallas as pl
from jax.experimental.pallas import tpu as pltpu
from jax.sharding import PartitionSpec as P

F32 = jnp.float32
BF16 = jnp.bfloat16
VMEM_LIMIT = 56 * 1024 * 1024
PANEL = 8
BROADCAST_UP_TO = 6


def elimination_levels(count):
    levels = []
    chain = list(range(count))
    while len(chain) > 1:
        level = []
        for place in range(0, len(chain), 2):
            left = chain[place - 1] if place > 0 else None
            right = chain[place + 1] if place + 1 < len(chain) else None
            level.append((chain[place], left, right))
        levels.append(level)
        chain = chain[1::2]
    return levels, chain[0]


def thirds(x):
    one = x.astype(BF16)
    rest = x - one.astype(F32)
    two = rest.astype(BF16)
    three = (rest - two.astype(F32)).astype(BF16)
    return one, two, three


def mm(a, b):
    a1, a2, a3 = thirds(a)
    b1, b2, b3 = thirds(b)
    left = jnp.concatenate([a1, a2, a1, a2, a1, a3], axis=1)
    right = jnp.concatenate([b1, b1, b2, b2, b3, b1], axis=0)
    return lax.dot_general(left, right, (((1,), (0,)), ((), ())), preferred_element_type=F32)


def mm_nt(a, b):
    a1, a2, a3 = thirds(a)
    b1, b2, b3 = thirds(b)
    left = jnp.concatenate([a1, a2, a1, a2, a1, a3], axis=1)
    right = jnp.concatenate([b1, b1, b2, b2, b3, b1], axis=1)
    return lax.dot_general(left, right, (((1,), (1,)), ((), ())), preferred_element_type=F32)


def half_roll(x):
    return pltpu.roll(x, x.shape[1] // 2, 1)


def invert_batch(mat_ref, members, orbits):
    width = 2 * orbits
    blocks = orbits // PANEL
    lane = lax.broadcasted_iota(jnp.int32, (PANEL, width), 1)
    sub = lax.broadcasted_iota(jnp.int32, (PANEL, width), 0)
    pivots = (lane < PANEL) | ((lane >= orbits) & (lane < orbits + PANEL))

    def panel(p, unused):
        rows = pl.ds(pl.multiple_of(p * PANEL, PANEL), PANEL)
        original = lax.rem(lane + p * PANEL, width)
        sign = jnp.where(original < orbits, -1.0, 1.0).astype(F32)
        tops = []
        for m in members:
            tops.append(mat_ref[m, rows, :])
        hats = []
        if len(members) > BROADCAST_UP_TO:
            for k in range(PANEL):
                here = sub == k
                at_pivot = (lane == k) | (lane == orbits + k)
                unit = jnp.where(here & (lane == k), 1.0, 0.0).astype(F32)
                for n in range(len(tops)):
                    r = tops[n]
                    cr = jnp.broadcast_to(r[:, k : k + 1], r.shape)
                    ci = jnp.broadcast_to(r[:, orbits + k : orbits + k + 1], r.shape)
                    inv = 1.0 / cr[k : k + 1, :]
                    r0 = jnp.where(at_pivot, unit, r)
                    row = r0[k : k + 1, :] * inv
                    hat = half_roll(r0)[k : k + 1, :] * (sign[k : k + 1, :] * inv)
                    tops[n] = jnp.where(here, row, r0 - cr * row - ci * hat)
            for r in tops:
                hats.append(half_roll(r) * sign)
        else:
            eye = jnp.where(lane == sub, 1.0, 0.0).astype(F32)
            turned = jnp.where(lane == sub + orbits, 1.0, 0.0).astype(F32) * sign
            cols = []
            for n in range(len(tops)):
                r = tops[n]
                cols.append(
                    [
                        (
                            jnp.broadcast_to(r[:, j : j + 1], r.shape),
                            jnp.broadcast_to(r[:, orbits + j : orbits + j + 1], r.shape),
                        )
                        for j in range(PANEL)
                    ]
                )
                hats.append(jnp.where(pivots, turned, half_roll(r) * sign))
                tops[n] = jnp.where(pivots, eye, r)
            for k in range(PANEL):
                here = sub == k
                for n in range(len(tops)):
                    r, hat = tops[n], hats[n]
                    cr, ci = cols[n][k]
                    inv = 1.0 / cr[k : k + 1, :]
                    ur, ui = cr * inv, ci * inv
                    for j in range(k + 1, PANEL):
                        er, ei = cols[n][j]
                        fr, fi = er[k : k + 1, :], ei[k : k + 1, :]
                        cols[n][j] = (
                            jnp.where(here, fr * inv, er - ur * fr + ui * fi),
                            jnp.where(here, fi * inv, ei - ur * fi - ui * fr),
                        )
                    row, hat_row = r[k : k + 1, :], hat[k : k + 1, :]
                    tops[n] = jnp.where(here, row * inv, r - ur * row - ui * hat_row)
                    hats[n] = jnp.where(here, hat_row * inv, hat - ur * hat_row + ui * row)
        for n, m in enumerate(members):
            r, hat = tops[n], hats[n]
            for i in range(blocks):
                block = mat_ref[m, PANEL * i : PANEL * (i + 1), :]
                out = jnp.where(pivots, 0.0, block)
                for j in range(PANEL):
                    out = out - jnp.broadcast_to(block[:, j : j + 1], out.shape) * r[j : j + 1, :]
                    out = out - jnp.broadcast_to(block[:, orbits + j : orbits + j + 1], out.shape) * hat[j : j + 1, :]
                mat_ref[m, PANEL * i : PANEL * (i + 1), :] = pltpu.roll(out, width - PANEL, 1)
            mat_ref[m, rows, :] = pltpu.roll(r, width - PANEL, 1)
        return 0

    lax.fori_loop(0, blocks, panel, 0)


def link_places(slabs, mine, levels):
    places = {}
    for s in range(slabs - 1):
        for e in range(mine):
            places[(0, s, s + 1, e)] = (True, s)
    spare = 0
    for depth, level in enumerate(levels):
        for node, left, right in level:
            if left is not None and right is not None:
                for e in range(mine):
                    places[(depth + 1, left, right, e)] = (False, spare)
                    spare += 1
    return places, spare


def climb(levels, mine, w1, w2, sol):
    for level in reversed(levels):
        for node, left, right in level:
            for e in range(mine):
                m = node * mine + e
                if left is not None and right is not None:
                    both = jnp.concatenate([w1[m], w2[m]], axis=1)
                    sides = jnp.concatenate([sol[left * mine + e], sol[right * mine + e]], axis=0)
                    sol[m] = sol[m] - mm(both, sides)
                elif left is not None:
                    sol[m] = sol[m] - mm(w1[m], sol[left * mine + e])
                elif right is not None:
                    sol[m] = sol[m] - mm(w2[m], sol[right * mine + e])


def retarded_kernel(plan, where_ref, *refs):
    (slabs, mine, orbits, groups, energy_groups, per, orb_per) = plan
    pq_ref, src_ref, set_ref = refs[0], refs[1], refs[2]
    peers = refs[3 : 3 + 2 * (groups - 1)]
    power_ref, inv, w1, w2, up1, dn1, up2, dn2, sol, gains, data, mat, rhs = refs[3 + 2 * (groups - 1) :]
    width = 2 * orbits
    levels, root = elimination_levels(slabs)
    places, _ = link_places(slabs, mine, levels)
    lane = lax.broadcasted_iota(jnp.int32, (orbits, width), 1)
    sub = lax.broadcasted_iota(jnp.int32, (orbits, width), 0)
    low = lane < orbits
    low_all = lax.broadcasted_iota(jnp.int32, (width, width), 1) < orbits
    diag_lane = lane == sub
    first, owner, core = where_ref[0], where_ref[1], where_ref[2]

    local = set_ref.shape[1]
    for i in range(per):
        at = owner * per + i
        data[at, 0:width, :] = pq_ref[i]
        data[at, width : 2 * width, :] = src_ref[i]
        data[at, 2 * width : 2 * width + local, :] = set_ref[i]
    for k in range(1, groups):
        mine_half, other_half = peers[2 * (k - 1)], peers[2 * (k - 1) + 1]
        for i in range(per):
            at = (owner ^ k) * per + i
            data[at, pl.ds(pl.multiple_of(core * width, width), width), :] = mine_half[i, 0:width, :]
            data[at, pl.ds(pl.multiple_of((1 - core) * width, width), width), :] = other_half[i, 0:width, :]
            data[at, 2 * width : 2 * width + local, :] = mine_half[i, width : width + local, :]

    def real_rows(z):
        return jnp.concatenate([jnp.where(low, z, -z), half_roll(z)], axis=0)

    def trans_rows(z):
        return jnp.concatenate([z, jnp.where(low, -half_roll(z), half_roll(z))], axis=0)

    def real_left(t):
        top, bottom = t[:orbits], t[orbits:]
        return jnp.concatenate(
            [jnp.where(low, top, -half_roll(bottom)), jnp.where(low, bottom, half_roll(top))], axis=0
        )

    def real_right(t):
        top, bottom = t[:orbits], t[orbits:]
        return jnp.concatenate(
            [jnp.where(low, half_roll(top), -bottom), jnp.where(low, half_roll(bottom), top)], axis=0
        )

    def packed_left(t):
        return jnp.where(low, t[:orbits], half_roll(t[orbits:]))

    def packed_right(t):
        return jnp.where(low, half_roll(t[:orbits]), t[orbits:])

    def factor_p(s):
        return data[s, 0:orbits, :]

    def factor_q(s):
        return data[s, orbits : 2 * orbits, :]

    for s in range(slabs):
        zq = factor_q(s)
        base = mm_nt(zq, trans_rows(zq))
        if s + 1 < slabs:
            zp = factor_p(s + 1)
            base = base + mm_nt(zp, trans_rows(zp))
            rp = real_rows(zp)
            rq = real_rows(factor_q(s + 1))
            up1[s] = -mm_nt(rp, rq)
            dn1[s] = -mm_nt(rq, rp)
        if s == 0:
            zp = factor_p(0)
            base = base + mm_nt(zp, trans_rows(zp))
        for e in range(mine):
            settings = data[s, pl.ds(2 * width + first + e, 1), :]
            gains[s * mine + e] = settings
            mat[s * mine + e] = base + jnp.where(diag_lane, settings, 0.0)
            rhs[s * mine + e] = data[s, width : 2 * width, :]

    def held(key):
        basic, place = places[key]
        return (up1, dn1, place) if basic else (up2, dn2, place)

    def couplings(depth, node, left, right, e):
        if left is None:
            to_left = 0.0
        else:
            _, downs, place = held((depth, left, node, e))
            to_left = downs[place]
        if right is None:
            to_right = 0.0
        else:
            ups, _, place = held((depth, node, right, e))
            to_right = half_roll(ups[place])
        return jnp.where(low_all, to_left, to_right)

    for depth, level in enumerate(levels):
        invert_batch(mat, [node * mine + e for node, _, _ in level for e in range(mine)], orbits)
        for node, left, right in level:
            for e in range(mine):
                m = node * mine + e
                full = real_rows(half_roll(mat[m]))
                inv[m] = full
                stacked = jnp.concatenate([couplings(depth, node, left, right, e), rhs[m]], axis=1)
                step = mm(full, stacked)
                links_step, rhs_step = step[:, :width], step[:, width:]
                sol[m] = rhs_step
                if left is not None:
                    w1[m] = real_left(links_step)
                    ups, _, place = held((depth, left, node, e))
                    change = mm(ups[place], step)
                    ml = left * mine + e
                    mat[ml] = mat[ml] - packed_left(change[:, :width])
                    rhs[ml] = rhs[ml] - change[:, width:]
                    if right is not None:
                        ups, _, place = held((depth + 1, left, right, e))
                        ups[place] = -real_right(change[:, :width])
                if right is not None:
                    w2[m] = real_right(links_step)
                    _, downs, place = held((depth, node, right, e))
                    change = mm(downs[place], step)
                    mr = right * mine + e
                    mat[mr] = mat[mr] - packed_right(change[:, :width])
                    rhs[mr] = rhs[mr] - change[:, width:]
                    if left is not None:
                        _, downs, place = held((depth + 1, left, right, e))
                        downs[place] = -real_left(change[:, :width])
    invert_batch(mat, [root * mine + e for e in range(mine)], orbits)
    for e in range(mine):
        m = root * mine + e
        full = real_rows(half_roll(mat[m]))
        inv[m] = full
        sol[m] = mm(full, rhs[m])
    climb(levels, mine, w1, w2, sol)
    for s in range(slabs):
        for e in range(mine):
            x = sol[s * mine + e]
            xr, xi = x[:orbits], x[orbits:]
            power = xr * xr + xi * xi
            for j in range(energy_groups):
                power_ref[s // per, j, e, s % per, :, :] = power[j * orb_per : (j + 1) * orb_per, :]


def lesser_kernel(plan, inv, w1, w2, up1, dn1, up2, dn2, ret, gains, out_ref, rhs, sol):
    (slabs, mine, orbits, groups, energy_groups, per, orb_per) = plan
    width = 2 * orbits
    levels, root = elimination_levels(slabs)
    places, _ = link_places(slabs, mine, levels)
    lane = lax.broadcasted_iota(jnp.int32, (orbits, width), 1)
    sub = lax.broadcasted_iota(jnp.int32, (orbits, width), 0)
    gain_lane = lane == sub + orbits
    for m in range(slabs * mine):
        gain = jnp.sum(jnp.where(gain_lane, gains[m], 0.0), axis=1, keepdims=True)
        rhs[m] = ret[m] * jnp.concatenate([gain, gain], axis=0)
    for depth, level in enumerate(levels):
        for node, left, right in level:
            for e in range(mine):
                m = node * mine + e
                step = mm(inv[m], rhs[m])
                sol[m] = step
                if left is not None:
                    basic, place = places[(depth, left, node, e)]
                    ml = left * mine + e
                    rhs[ml] = rhs[ml] - mm((up1 if basic else up2)[place], step)
                if right is not None:
                    basic, place = places[(depth, node, right, e)]
                    mr = right * mine + e
                    rhs[mr] = rhs[mr] - mm((dn1 if basic else dn2)[place], step)
    for e in range(mine):
        m = root * mine + e
        sol[m] = mm(inv[m], rhs[m])
    climb(levels, mine, w1, w2, sol)
    for s in range(slabs):
        for e in range(mine):
            m = s * mine + e
            x, y = ret[m], sol[m]
            xr, xi, yr, yi = x[:orbits], x[orbits:], y[:orbits], y[orbits:]
            re = xr * yr + xi * yi
            im = xr * yi - xi * yr
            for j in range(energy_groups):
                rows = slice(j * orb_per, (j + 1) * orb_per)
                out_ref[s // per, j, 0, e, s % per, :, :] = re[rows, :]
                out_ref[s // per, j, 1, e, s % per, :, :] = im[rows, :]


def vmem_specs(count):
    return [pl.BlockSpec(memory_space=pltpu.VMEM)] * count


def solve_retarded(where, pieces, plan, columns):
    (slabs, mine, orbits, groups, energy_groups, per, orb_per) = plan
    width = 2 * orbits
    nodes = slabs * mine
    levels, _ = elimination_levels(slabs)
    _, fills = link_places(slabs, mine, levels)
    local = pieces[2].shape[1]
    shapes = [
        (groups, energy_groups, mine, per, orb_per, columns),
        (nodes, width, width),
        (nodes, width, width),
        (nodes, width, width),
        (slabs - 1, width, width),
        (slabs - 1, width, width),
        (fills, width, width),
        (fills, width, width),
        (nodes, width, columns),
        (nodes, 1, width),
    ]
    return pl.pallas_call(
        functools.partial(retarded_kernel, plan),
        out_shape=[jax.ShapeDtypeStruct(shape, F32) for shape in shapes],
        in_specs=[pl.BlockSpec(memory_space=pltpu.SMEM)] + vmem_specs(len(pieces)),
        out_specs=vmem_specs(len(shapes)),
        scratch_shapes=[
            pltpu.VMEM((slabs, 2 * width + local, columns), F32),
            pltpu.VMEM((nodes, orbits, width), F32),
            pltpu.VMEM((nodes, width, columns), F32),
        ],
        compiler_params=pltpu.CompilerParams(vmem_limit_bytes=VMEM_LIMIT),
        name="solve_retarded",
    )(where, *pieces)


def solve_lesser(stored, plan):
    (slabs, mine, orbits, groups, energy_groups, per, orb_per) = plan
    solved = stored[7].shape
    return pl.pallas_call(
        functools.partial(lesser_kernel, plan),
        out_shape=jax.ShapeDtypeStruct((groups, energy_groups, 2, mine, per, orb_per, solved[-1]), F32),
        in_specs=vmem_specs(len(stored)),
        out_specs=pl.BlockSpec(memory_space=pltpu.VMEM),
        scratch_shapes=[pltpu.VMEM(solved, F32), pltpu.VMEM(solved, F32)],
        compiler_params=pltpu.CompilerParams(vmem_limit_bytes=VMEM_LIMIT),
        name="solve_lesser",
    )(*stored)


def correlate_kernel(order, power_ref, got_ref, out_ref):
    count = len(order)
    window = 8
    scale = 1.0 / count
    for start in range(0, count, window):
        span = min(window, count - start)
        acc_re = [None] * span
        acc_im = [None] * span
        reach = count - start
        lead = {}
        for energy in range(reach):
            sender, place = order[energy]
            power = power_ref[sender, place, 0]
            for w in range(span):
                at = energy + start + w
                if at >= count:
                    continue
                if at not in lead:
                    s2, p2 = order[at]
                    lead[at] = (got_ref[s2, 0, p2, 0], got_ref[s2, 1, p2, 0])
                re, im = lead[at]
                acc_re[w] = re * power if acc_re[w] is None else acc_re[w] + re * power
                acc_im[w] = im * power if acc_im[w] is None else acc_im[w] + im * power
        for w in range(span):
            out_ref[0, start + w, 0] = acc_re[w] * scale
            out_ref[1, start + w, 0] = acc_im[w] * scale


def correlate(power, got, order):
    senders, kinds, mine, per, rows, columns = got.shape
    count = len(order)
    return pl.pallas_call(
        functools.partial(correlate_kernel, order),
        grid=(per,),
        out_shape=jax.ShapeDtypeStruct((2, count, per, rows, columns), F32),
        in_specs=[
            pl.BlockSpec((senders, mine, 1, rows, columns), lambda i: (0, 0, i, 0, 0)),
            pl.BlockSpec((senders, kinds, mine, 1, rows, columns), lambda i: (0, 0, 0, i, 0, 0)),
        ],
        out_specs=pl.BlockSpec((2, count, 1, rows, columns), lambda i: (0, 0, i, 0, 0)),
        compiler_params=pltpu.CompilerParams(vmem_limit_bytes=VMEM_LIMIT),
        name="correlate",
    )(power, got)


def per_device(link_p, link_q, shift, lesser_gain, sources):
    per, _, orbits, _ = link_p.shape
    width = 2 * orbits
    columns = sources.shape[-1]
    local = shift.shape[0]
    groups = lax.axis_size("slab")
    energy_groups = lax.axis_size("energy")
    slabs = per * groups
    mine = max(1, local // groups)
    owner = lax.axis_index("slab")
    factors = jnp.concatenate(
        [
            jnp.concatenate([link_p[:, 0], link_p[:, 1]], axis=-1),
            jnp.concatenate([link_q[:, 0], link_q[:, 1]], axis=-1),
        ],
        axis=1,
    )
    columns_in = sources.reshape(per, width, columns)
    settings = jnp.swapaxes(jnp.concatenate([shift, lesser_gain], axis=-1), 0, 1)
    place = lax.axis_index("energy")
    core = place % 2
    parcel = jnp.concatenate([jnp.where(core == 0, factors, columns_in), settings], axis=1)
    siblings = [(j, j ^ 1) for j in range(energy_groups)]
    pieces = [factors, columns_in, settings]
    fetched = [lax.ppermute(parcel, "slab", [(g, g ^ k) for g in range(groups)]) for k in range(1, groups)]
    for piece in fetched:
        pieces.append(piece)
        pieces.append(lax.ppermute(piece, "energy", siblings))
    where = jnp.stack([owner * local // groups, owner, core]).astype(jnp.int32)
    plan = (slabs, mine, orbits, groups, energy_groups, per, orbits // energy_groups)
    power, *stored = solve_retarded(where, pieces, plan, columns)

    def spread(array):
        array = array.reshape((groups * energy_groups,) + array.shape[2:])
        return lax.all_to_all(array, ("slab", "energy"), split_axis=0, concat_axis=0, tiled=True)

    power = spread(power)
    got = spread(solve_lesser(stored, plan))
    order = []
    for group in range(energy_groups):
        for row in range(local):
            if local >= groups:
                holder, place = row // mine, row % mine
            else:
                holder, place = -(-row * groups // local), 0
            order.append((holder * energy_groups + group, place))
    return correlate(power, got, tuple(order))


def solution(mesh):
    placed = (
        P("slab", None, None, None),
        P("slab", None, None, None),
        P("energy", "slab", None),
        P("energy", "slab", None),
        P("slab", None, None, None),
    )
    return jax.shard_map(
        per_device,
        mesh=mesh,
        in_specs=placed,
        out_specs=P(None, None, "slab", "energy", None),
        check_vma=False,
    )
```

```python
import functools

import jax
import jax.numpy as jnp
from jax import lax
from jax.experimental import pallas as pl
from jax.experimental.pallas import tpu as pltpu
from jax.sharding import PartitionSpec as P

F32 = jnp.float32
BF16 = jnp.bfloat16
VMEM_LIMIT = 56 * 1024 * 1024
LEAST = 0.0095
CLOSE = 1e-3


def elimination_levels(count):
    levels = []
    chain = list(range(count))
    while len(chain) > 1:
        level = []
        for place in range(0, len(chain), 2):
            left = chain[place - 1] if place > 0 else None
            right = chain[place + 1] if place + 1 < len(chain) else None
            level.append((chain[place], left, right))
        levels.append(level)
        chain = chain[1::2]
    return levels, chain[0]


def thirds(x):
    one = x.astype(BF16)
    rest = x - one.astype(F32)
    two = rest.astype(BF16)
    three = (rest - two.astype(F32)).astype(BF16)
    return one, two, three


def mm(a, b):
    a1, a2, a3 = thirds(a)
    b1, b2, b3 = thirds(b)
    left = jnp.concatenate([a1, a2, a1, a2, a1, a3], axis=1)
    right = jnp.concatenate([b1, b1, b2, b2, b3, b1], axis=0)
    return lax.dot_general(left, right, (((1,), (0,)), ((), ())), preferred_element_type=F32)


def mm_nt(a, b):
    a1, a2, a3 = thirds(a)
    b1, b2, b3 = thirds(b)
    left = jnp.concatenate([a1, a2, a1, a2, a1, a3], axis=1)
    right = jnp.concatenate([b1, b1, b2, b2, b3, b1], axis=1)
    return lax.dot_general(left, right, (((1,), (1,)), ((), ())), preferred_element_type=F32)


def half_roll(x):
    return pltpu.roll(x, x.shape[1] // 2, 1)


def turn_rows(z):
    low = lax.broadcasted_iota(jnp.int32, z.shape, 1) < z.shape[1] // 2
    turned = half_roll(z)
    return jnp.concatenate([z, jnp.where(low, -turned, turned)], axis=0)


def packed_mm(a, b):
    full = turn_rows(b)
    a1 = a.astype(BF16)
    a2 = (a - a1.astype(F32)).astype(BF16)
    b1 = full.astype(BF16)
    b2 = (full - b1.astype(F32)).astype(BF16)
    left = jnp.concatenate([a1, a2, a1], axis=1)
    right = jnp.concatenate([b1, b1, b2], axis=0)
    return lax.dot_general(left, right, (((1,), (0,)), ((), ())), preferred_element_type=F32)


def invert_batch(mat_ref, inv_ref, members, top):
    shape = mat_ref.shape[1:]
    lane = lax.broadcasted_iota(jnp.int32, shape, 1)
    sub = lax.broadcasted_iota(jnp.int32, shape, 0)
    eye = jnp.where(lane == sub, 1.0, 0.0).astype(F32)
    total = top + LEAST
    for m in members:
        inv_ref[m] = eye * (2.0 / total)

    def body(reach):
        squared = reach * reach
        gain = 2.0 / (2.0 - squared)
        after = squared * gain * 0.5
        squared_after = after * after
        gain_after = 2.0 / (2.0 - squared_after)
        mats = [mat_ref[m] for m in members]
        guesses = [inv_ref[m] for m in members]
        closeness = [packed_mm(a, x) for a, x in zip(mats, guesses)]
        pairs = [
            packed_mm(jnp.concatenate([x, t], axis=0), (2.0 * eye - t) * gain) for x, t in zip(guesses, closeness)
        ]
        count = shape[0]
        for m, pair in zip(members, pairs):
            inv_ref[m] = packed_mm(pair[:count], (2.0 * eye - pair[count:]) * gain_after)
        return squared_after * gain_after * 0.5

    lax.while_loop(lambda reach: reach > CLOSE, body, (top - LEAST) / total)
    guesses = [inv_ref[m] for m in members]
    rests = [eye - mm(mat_ref[m], turn_rows(x)) for m, x in zip(members, guesses)]
    for m, x, rest in zip(members, guesses, rests):
        inv_ref[m] = x + packed_mm(x, rest)


def link_places(slabs, mine, levels):
    places = {}
    for s in range(slabs - 1):
        for e in range(mine):
            places[(0, s, s + 1, e)] = (True, s)
    spare = 0
    for depth, level in enumerate(levels):
        for node, left, right in level:
            if left is not None and right is not None:
                for e in range(mine):
                    places[(depth + 1, left, right, e)] = (False, spare)
                    spare += 1
    return places, spare


def climb(levels, mine, w1, w2, sol):
    for level in reversed(levels):
        for node, left, right in level:
            for e in range(mine):
                m = node * mine + e
                if left is not None and right is not None:
                    both = jnp.concatenate([w1[m], w2[m]], axis=1)
                    sides = jnp.concatenate([sol[left * mine + e], sol[right * mine + e]], axis=0)
                    sol[m] = sol[m] - mm(both, sides)
                elif left is not None:
                    sol[m] = sol[m] - mm(w1[m], sol[left * mine + e])
                elif right is not None:
                    sol[m] = sol[m] - mm(w2[m], sol[right * mine + e])


def retarded_kernel(plan, where_ref, *refs):
    (slabs, mine, orbits, groups, energy_groups, per, orb_per) = plan
    pq_ref, src_ref, set_ref = refs[0], refs[1], refs[2]
    peers = refs[3 : 3 + 2 * (groups - 1)]
    power_ref, inv, w1, w2, up1, dn1, up2, dn2, sol, gains, data, mat, rhs, near = refs[3 + 2 * (groups - 1) :]
    width = 2 * orbits
    levels, root = elimination_levels(slabs)
    places, _ = link_places(slabs, mine, levels)
    lane = lax.broadcasted_iota(jnp.int32, (orbits, width), 1)
    sub = lax.broadcasted_iota(jnp.int32, (orbits, width), 0)
    low = lane < orbits
    low_all = lax.broadcasted_iota(jnp.int32, (width, width), 1) < orbits
    diag_lane = lane == sub
    first, owner, core = where_ref[0], where_ref[1], where_ref[2]

    local = set_ref.shape[1]
    for i in range(per):
        at = owner * per + i
        data[at, 0:width, :] = pq_ref[i]
        data[at, width : 2 * width, :] = src_ref[i]
        data[at, 2 * width : 2 * width + local, :] = set_ref[i]
    for k in range(1, groups):
        mine_half, other_half = peers[2 * (k - 1)], peers[2 * (k - 1) + 1]
        for i in range(per):
            at = (owner ^ k) * per + i
            data[at, pl.ds(pl.multiple_of(core * width, width), width), :] = mine_half[i, 0:width, :]
            data[at, pl.ds(pl.multiple_of((1 - core) * width, width), width), :] = other_half[i, 0:width, :]
            data[at, 2 * width : 2 * width + local, :] = mine_half[i, width : width + local, :]

    def real_rows(z):
        return jnp.concatenate([jnp.where(low, z, -z), half_roll(z)], axis=0)

    def real_left(t):
        top, bottom = t[:orbits], t[orbits:]
        return jnp.concatenate(
            [jnp.where(low, top, -half_roll(bottom)), jnp.where(low, bottom, half_roll(top))], axis=0
        )

    def real_right(t):
        top, bottom = t[:orbits], t[orbits:]
        return jnp.concatenate(
            [jnp.where(low, half_roll(top), -bottom), jnp.where(low, half_roll(bottom), top)], axis=0
        )

    def packed_left(t):
        return jnp.where(low, t[:orbits], half_roll(t[orbits:]))

    def packed_right(t):
        return jnp.where(low, half_roll(t[:orbits]), t[orbits:])

    def factor_p(s):
        return data[s, 0:orbits, :]

    def factor_q(s):
        return data[s, orbits : 2 * orbits, :]

    largest = None
    for s in range(slabs):
        zq = factor_q(s)
        base = mm_nt(zq, turn_rows(zq))
        if s + 1 < slabs:
            zp = factor_p(s + 1)
            base = base + mm_nt(zp, turn_rows(zp))
            rp = real_rows(zp)
            rq = real_rows(factor_q(s + 1))
            up1[s] = -mm_nt(rp, rq)
            dn1[s] = -mm_nt(rq, rp)
        if s == 0:
            zp = factor_p(0)
            base = base + mm_nt(zp, turn_rows(zp))
        for e in range(mine):
            settings = data[s, pl.ds(2 * width + first + e, 1), :]
            gains[s * mine + e] = settings
            block = base + jnp.where(diag_lane, settings, 0.0)
            mat[s * mine + e] = block
            rhs[s * mine + e] = data[s, width : 2 * width, :]
            sums = jnp.sum(jnp.abs(block), axis=0, keepdims=True)
            largest = sums if largest is None else jnp.maximum(largest, sums)
    top = 1.01 * jnp.max(largest + half_roll(largest))

    def held(key):
        basic, place = places[key]
        return (up1, dn1, place) if basic else (up2, dn2, place)

    def couplings(depth, node, left, right, e):
        if left is None:
            to_left = 0.0
        else:
            _, downs, place = held((depth, left, node, e))
            to_left = downs[place]
        if right is None:
            to_right = 0.0
        else:
            ups, _, place = held((depth, node, right, e))
            to_right = half_roll(ups[place])
        return jnp.where(low_all, to_left, to_right)

    for depth, level in enumerate(levels):
        invert_batch(mat, near, [node * mine + e for node, _, _ in level for e in range(mine)], top)
        for node, left, right in level:
            for e in range(mine):
                m = node * mine + e
                full = real_rows(near[m])
                inv[m] = full
                stacked = jnp.concatenate([couplings(depth, node, left, right, e), rhs[m]], axis=1)
                step = mm(full, stacked)
                links_step, rhs_step = step[:, :width], step[:, width:]
                sol[m] = rhs_step
                if left is not None:
                    w1[m] = real_left(links_step)
                    ups, _, place = held((depth, left, node, e))
                    change = mm(ups[place], step)
                    ml = left * mine + e
                    mat[ml] = mat[ml] - packed_left(change[:, :width])
                    rhs[ml] = rhs[ml] - change[:, width:]
                    if right is not None:
                        ups, _, place = held((depth + 1, left, right, e))
                        ups[place] = -real_right(change[:, :width])
                if right is not None:
                    w2[m] = real_right(links_step)
                    _, downs, place = held((depth, node, right, e))
                    change = mm(downs[place], step)
                    mr = right * mine + e
                    mat[mr] = mat[mr] - packed_right(change[:, :width])
                    rhs[mr] = rhs[mr] - change[:, width:]
                    if left is not None:
                        _, downs, place = held((depth + 1, left, right, e))
                        downs[place] = -real_left(change[:, :width])
    invert_batch(mat, near, [root * mine + e for e in range(mine)], top)
    for e in range(mine):
        m = root * mine + e
        full = real_rows(near[m])
        inv[m] = full
        sol[m] = mm(full, rhs[m])
    climb(levels, mine, w1, w2, sol)
    for s in range(slabs):
        for e in range(mine):
            x = sol[s * mine + e]
            xr, xi = x[:orbits], x[orbits:]
            power = xr * xr + xi * xi
            for j in range(energy_groups):
                power_ref[s // per, j, e, s % per, :, :] = power[j * orb_per : (j + 1) * orb_per, :]


def lesser_kernel(plan, inv, w1, w2, up1, dn1, up2, dn2, ret, gains, out_ref, rhs, sol):
    (slabs, mine, orbits, groups, energy_groups, per, orb_per) = plan
    width = 2 * orbits
    levels, root = elimination_levels(slabs)
    places, _ = link_places(slabs, mine, levels)
    lane = lax.broadcasted_iota(jnp.int32, (orbits, width), 1)
    sub = lax.broadcasted_iota(jnp.int32, (orbits, width), 0)
    gain_lane = lane == sub + orbits
    for m in range(slabs * mine):
        gain = jnp.sum(jnp.where(gain_lane, gains[m], 0.0), axis=1, keepdims=True)
        rhs[m] = ret[m] * jnp.concatenate([gain, gain], axis=0)
    for depth, level in enumerate(levels):
        for node, left, right in level:
            for e in range(mine):
                m = node * mine + e
                step = mm(inv[m], rhs[m])
                sol[m] = step
                if left is not None:
                    basic, place = places[(depth, left, node, e)]
                    ml = left * mine + e
                    rhs[ml] = rhs[ml] - mm((up1 if basic else up2)[place], step)
                if right is not None:
                    basic, place = places[(depth, node, right, e)]
                    mr = right * mine + e
                    rhs[mr] = rhs[mr] - mm((dn1 if basic else dn2)[place], step)
    for e in range(mine):
        m = root * mine + e
        sol[m] = mm(inv[m], rhs[m])
    climb(levels, mine, w1, w2, sol)
    for s in range(slabs):
        for e in range(mine):
            m = s * mine + e
            x, y = ret[m], sol[m]
            xr, xi, yr, yi = x[:orbits], x[orbits:], y[:orbits], y[orbits:]
            re = xr * yr + xi * yi
            im = xr * yi - xi * yr
            for j in range(energy_groups):
                rows = slice(j * orb_per, (j + 1) * orb_per)
                out_ref[s // per, j, 0, e, s % per, :, :] = re[rows, :]
                out_ref[s // per, j, 1, e, s % per, :, :] = im[rows, :]


def vmem_specs(count):
    return [pl.BlockSpec(memory_space=pltpu.VMEM)] * count


def solve_retarded(where, pieces, plan, columns):
    (slabs, mine, orbits, groups, energy_groups, per, orb_per) = plan
    width = 2 * orbits
    nodes = slabs * mine
    levels, _ = elimination_levels(slabs)
    _, fills = link_places(slabs, mine, levels)
    local = pieces[2].shape[1]
    shapes = [
        (groups, energy_groups, mine, per, orb_per, columns),
        (nodes, width, width),
        (nodes, width, width),
        (nodes, width, width),
        (slabs - 1, width, width),
        (slabs - 1, width, width),
        (fills, width, width),
        (fills, width, width),
        (nodes, width, columns),
        (nodes, 1, width),
    ]
    return pl.pallas_call(
        functools.partial(retarded_kernel, plan),
        out_shape=[jax.ShapeDtypeStruct(shape, F32) for shape in shapes],
        in_specs=[pl.BlockSpec(memory_space=pltpu.SMEM)] + vmem_specs(len(pieces)),
        out_specs=vmem_specs(len(shapes)),
        scratch_shapes=[
            pltpu.VMEM((slabs, 2 * width + local, columns), F32),
            pltpu.VMEM((nodes, orbits, width), F32),
            pltpu.VMEM((nodes, width, columns), F32),
            pltpu.VMEM((nodes, orbits, width), F32),
        ],
        compiler_params=pltpu.CompilerParams(vmem_limit_bytes=VMEM_LIMIT),
        name="solve_retarded",
    )(where, *pieces)


def solve_lesser(stored, plan):
    (slabs, mine, orbits, groups, energy_groups, per, orb_per) = plan
    solved = stored[7].shape
    return pl.pallas_call(
        functools.partial(lesser_kernel, plan),
        out_shape=jax.ShapeDtypeStruct((groups, energy_groups, 2, mine, per, orb_per, solved[-1]), F32),
        in_specs=vmem_specs(len(stored)),
        out_specs=pl.BlockSpec(memory_space=pltpu.VMEM),
        scratch_shapes=[pltpu.VMEM(solved, F32), pltpu.VMEM(solved, F32)],
        compiler_params=pltpu.CompilerParams(vmem_limit_bytes=VMEM_LIMIT),
        name="solve_lesser",
    )(*stored)


def correlate_kernel(order, power_ref, got_ref, out_ref):
    count = len(order)
    window = 8
    scale = 1.0 / count
    for start in range(0, count, window):
        span = min(window, count - start)
        acc_re = [None] * span
        acc_im = [None] * span
        reach = count - start
        lead = {}
        for energy in range(reach):
            sender, place = order[energy]
            power = power_ref[sender, place, 0]
            for w in range(span):
                at = energy + start + w
                if at >= count:
                    continue
                if at not in lead:
                    s2, p2 = order[at]
                    lead[at] = (got_ref[s2, 0, p2, 0], got_ref[s2, 1, p2, 0])
                re, im = lead[at]
                acc_re[w] = re * power if acc_re[w] is None else acc_re[w] + re * power
                acc_im[w] = im * power if acc_im[w] is None else acc_im[w] + im * power
        for w in range(span):
            out_ref[0, start + w, 0] = acc_re[w] * scale
            out_ref[1, start + w, 0] = acc_im[w] * scale


def correlate(power, got, order):
    senders, kinds, mine, per, rows, columns = got.shape
    count = len(order)
    return pl.pallas_call(
        functools.partial(correlate_kernel, order),
        grid=(per,),
        out_shape=jax.ShapeDtypeStruct((2, count, per, rows, columns), F32),
        in_specs=[
            pl.BlockSpec((senders, mine, 1, rows, columns), lambda i: (0, 0, i, 0, 0)),
            pl.BlockSpec((senders, kinds, mine, 1, rows, columns), lambda i: (0, 0, 0, i, 0, 0)),
        ],
        out_specs=pl.BlockSpec((2, count, 1, rows, columns), lambda i: (0, 0, i, 0, 0)),
        compiler_params=pltpu.CompilerParams(vmem_limit_bytes=VMEM_LIMIT),
        name="correlate",
    )(power, got)


def per_device(link_p, link_q, shift, lesser_gain, sources):
    per, _, orbits, _ = link_p.shape
    width = 2 * orbits
    columns = sources.shape[-1]
    local = shift.shape[0]
    groups = lax.axis_size("slab")
    energy_groups = lax.axis_size("energy")
    slabs = per * groups
    mine = max(1, local // groups)
    owner = lax.axis_index("slab")
    factors = jnp.concatenate(
        [
            jnp.concatenate([link_p[:, 0], link_p[:, 1]], axis=-1),
            jnp.concatenate([link_q[:, 0], link_q[:, 1]], axis=-1),
        ],
        axis=1,
    )
    columns_in = sources.reshape(per, width, columns)
    settings = jnp.swapaxes(jnp.concatenate([shift, lesser_gain], axis=-1), 0, 1)
    place = lax.axis_index("energy")
    core = place % 2
    parcel = jnp.concatenate([jnp.where(core == 0, factors, columns_in), settings], axis=1)
    siblings = [(j, j ^ 1) for j in range(energy_groups)]
    pieces = [factors, columns_in, settings]
    fetched = [lax.ppermute(parcel, "slab", [(g, g ^ k) for g in range(groups)]) for k in range(1, groups)]
    for piece in fetched:
        pieces.append(piece)
        pieces.append(lax.ppermute(piece, "energy", siblings))
    where = jnp.stack([owner * local // groups, owner, core]).astype(jnp.int32)
    plan = (slabs, mine, orbits, groups, energy_groups, per, orbits // energy_groups)
    power, *stored = solve_retarded(where, pieces, plan, columns)

    def spread(array):
        array = array.reshape((groups * energy_groups,) + array.shape[2:])
        return lax.all_to_all(array, ("slab", "energy"), split_axis=0, concat_axis=0, tiled=True)

    power = spread(power)
    got = spread(solve_lesser(stored, plan))
    order = []
    for group in range(energy_groups):
        for row in range(local):
            if local >= groups:
                holder, place = row // mine, row % mine
            else:
                holder, place = -(-row * groups // local), 0
            order.append((holder * energy_groups + group, place))
    return correlate(power, got, tuple(order))


def solution(mesh):
    placed = (
        P("slab", None, None, None),
        P("slab", None, None, None),
        P("energy", "slab", None),
        P("energy", "slab", None),
        P("slab", None, None, None),
    )
    return jax.shard_map(
        per_device,
        mesh=mesh,
        in_specs=placed,
        out_specs=P(None, None, "slab", "energy", None),
        check_vma=False,
    )
```

```python
import functools

import jax
import jax.numpy as jnp
from jax import lax
from jax.experimental import pallas as pl
from jax.experimental.pallas import tpu as pltpu
from jax.sharding import PartitionSpec as P

F32 = jnp.float32
BF16 = jnp.bfloat16
VMEM_LIMIT = 56 * 1024 * 1024
SMALL_LIMIT = 16 * 1024 * 1024
LEAST = 0.0095
CLOSE = 1e-3
STRIDE = 4


def elimination_levels(count):
    levels = []
    chain = list(range(count))
    while len(chain) > 1:
        level = []
        for place in range(0, len(chain), 2):
            left = chain[place - 1] if place > 0 else None
            right = chain[place + 1] if place + 1 < len(chain) else None
            level.append((chain[place], left, right))
        levels.append(level)
        chain = chain[1::2]
    return levels, chain[0]


def thirds(x):
    one = x.astype(BF16)
    rest = x - one.astype(F32)
    two = rest.astype(BF16)
    three = (rest - two.astype(F32)).astype(BF16)
    return one, two, three


def mm(a, b):
    a1, a2, a3 = thirds(a)
    b1, b2, b3 = thirds(b)
    left = jnp.concatenate([a1, a2, a1, a2, a1, a3], axis=1)
    right = jnp.concatenate([b1, b1, b2, b2, b3, b1], axis=0)
    return lax.dot_general(left, right, (((1,), (0,)), ((), ())), preferred_element_type=F32)


def mm_three(a, b):
    a1 = a.astype(BF16)
    a2 = (a - a1.astype(F32)).astype(BF16)
    b1 = b.astype(BF16)
    b2 = (b - b1.astype(F32)).astype(BF16)
    left = jnp.concatenate([a1, a2, a1], axis=1)
    right = jnp.concatenate([b1, b1, b2], axis=0)
    return lax.dot_general(left, right, (((1,), (0,)), ((), ())), preferred_element_type=F32)


def mm_nt(a, b):
    a1, a2, a3 = thirds(a)
    b1, b2, b3 = thirds(b)
    left = jnp.concatenate([a1, a2, a1, a2, a1, a3], axis=1)
    right = jnp.concatenate([b1, b1, b2, b2, b3, b1], axis=1)
    return lax.dot_general(left, right, (((1,), (1,)), ((), ())), preferred_element_type=F32)


def half_roll(x):
    return pltpu.roll(x, x.shape[1] // 2, 1)


def turn_rows(z):
    low = lax.broadcasted_iota(jnp.int32, z.shape, 1) < z.shape[1] // 2
    turned = half_roll(z)
    return jnp.concatenate([z, jnp.where(low, -turned, turned)], axis=0)


def packed_mm(a, b):
    return mm_three(a, turn_rows(b))


def invert_batch(mat_ref, inv_ref, members, top):
    shape = mat_ref.shape[1:]
    count = shape[0]
    lane = lax.broadcasted_iota(jnp.int32, shape, 1)
    sub = lax.broadcasted_iota(jnp.int32, shape, 0)
    eye = jnp.where(lane == sub, 1.0, 0.0).astype(F32)
    total = top + LEAST

    def factor_of(reach):
        squared = reach * reach
        gain = 2.0 / (2.0 - squared)
        return gain, 0.5 * squared * gain

    def steps(xs, ts, reach, number):
        for step in range(number):
            gain, reach = factor_of(reach)
            bases = [(2.0 * eye - t) * gain for t in ts]
            if step + 1 < number:
                pairs = [packed_mm(jnp.concatenate([x, t], axis=0), base) for x, t, base in zip(xs, ts, bases)]
                xs = [pair[:count] for pair in pairs]
                ts = [pair[count:] for pair in pairs]
            else:
                xs = [packed_mm(x, base) for x, base in zip(xs, bases)]
        for m, x in zip(members, xs):
            inv_ref[m] = x
        return reach

    reach = (top - LEAST) / total
    start = 2.0 / total
    gain, reach = factor_of(reach)
    ts = [mat_ref[m] * start for m in members]
    bases = [(2.0 * eye - t) * gain for t in ts]
    xs = [base * start for base in bases]
    ts = [packed_mm(t, base) for t, base in zip(ts, bases)]
    reach = steps(xs, ts, reach, STRIDE - 1)

    def body(reach):
        xs = [inv_ref[m] for m in members]
        ts = [packed_mm(mat_ref[m], x) for m, x in zip(members, xs)]
        return steps(xs, ts, reach, STRIDE)

    lax.while_loop(lambda reach: reach > CLOSE, body, reach)
    xs = [inv_ref[m] for m in members]
    rests = [eye - mm(mat_ref[m], turn_rows(x)) for m, x in zip(members, xs)]
    for m, x, rest in zip(members, xs, rests):
        inv_ref[m] = x + packed_mm(x, rest)


def slots(levels, root):
    order = [node for level in levels for node, _, _ in level] + [root]
    return {node: place for place, node in enumerate(order)}


def link_places(slabs, mine, levels):
    places = {}
    for s in range(slabs - 1):
        for e in range(mine):
            places[(0, s, s + 1, e)] = (True, s)
    spare = 0
    for depth, level in enumerate(levels):
        for node, left, right in level:
            if left is not None and right is not None:
                for e in range(mine):
                    places[(depth + 1, left, right, e)] = (False, spare)
                    spare += 1
    return places, spare


def climb(levels, spot, mine, w1, w2, sol, finished):
    for level in reversed(levels):
        for node, left, right in level:
            for e in range(mine):
                m = spot[node] * mine + e
                if left is not None and right is not None:
                    both = jnp.concatenate([w1[m], w2[m]], axis=1)
                    sides = jnp.concatenate([sol[spot[left] * mine + e], sol[spot[right] * mine + e]], axis=0)
                    sol[m] = sol[m] - mm_three(both, sides)
                elif left is not None:
                    sol[m] = sol[m] - mm_three(w1[m], sol[spot[left] * mine + e])
                elif right is not None:
                    sol[m] = sol[m] - mm_three(w2[m], sol[spot[right] * mine + e])
        finished([node for node, _, _ in level])


def retarded_kernel(plan, where_ref, *refs):
    (slabs, mine, orbits, groups, energy_groups, per, orb_per) = plan
    pq_ref, src_ref, set_ref = refs[0], refs[1], refs[2]
    peers = refs[3 : 3 + 2 * (groups - 1)]
    power_ref, gains = refs[3 + 2 * (groups - 1) : 5 + 2 * (groups - 1)]
    outs = refs[5 + 2 * (groups - 1) : 13 + 2 * (groups - 1)]
    inv, w1, w2, up1, dn1, up2, dn2, sol, data, mat, rhs, near, sems = refs[13 + 2 * (groups - 1) :]
    stores = (inv, w1, w2, up1, dn1, up2, dn2, sol)
    copies = []

    def copy_out(which, low_place, high_place):
        part = pl.ds(low_place, high_place - low_place)
        copy = pltpu.make_async_copy(stores[which].at[part], outs[which].at[part], sems.at[len(copies)])
        copy.start()
        copies.append(copy)

    width = 2 * orbits
    levels, root = elimination_levels(slabs)
    spot = slots(levels, root)
    places, _ = link_places(slabs, mine, levels)
    lane = lax.broadcasted_iota(jnp.int32, (orbits, width), 1)
    sub = lax.broadcasted_iota(jnp.int32, (orbits, width), 0)
    low = lane < orbits
    low_all = lax.broadcasted_iota(jnp.int32, (width, width), 1) < orbits
    diag_lane = lane == sub
    first, owner, core = where_ref[0], where_ref[1], where_ref[2]

    local = set_ref.shape[1]
    for i in range(per):
        at = owner * per + i
        data[at, 0:width, :] = pq_ref[i]
        data[at, width : 2 * width, :] = src_ref[i]
        data[at, 2 * width : 2 * width + local, :] = set_ref[i]
    for k in range(1, groups):
        mine_half, other_half = peers[2 * (k - 1)], peers[2 * (k - 1) + 1]
        for i in range(per):
            at = (owner ^ k) * per + i
            data[at, pl.ds(pl.multiple_of(core * width, width), width), :] = mine_half[i, 0:width, :]
            data[at, pl.ds(pl.multiple_of((1 - core) * width, width), width), :] = other_half[i, 0:width, :]
            data[at, 2 * width : 2 * width + local, :] = mine_half[i, width : width + local, :]

    def real_rows(z):
        return jnp.concatenate([jnp.where(low, z, -z), half_roll(z)], axis=0)

    def real_left(t):
        top, bottom = t[:orbits], t[orbits:]
        return jnp.concatenate(
            [jnp.where(low, top, -half_roll(bottom)), jnp.where(low, bottom, half_roll(top))], axis=0
        )

    def real_right(t):
        top, bottom = t[:orbits], t[orbits:]
        return jnp.concatenate(
            [jnp.where(low, half_roll(top), -bottom), jnp.where(low, half_roll(bottom), top)], axis=0
        )

    def packed_left(t):
        return jnp.where(low, t[:orbits], half_roll(t[orbits:]))

    def packed_right(t):
        return jnp.where(low, half_roll(t[:orbits]), t[orbits:])

    largest = None
    pps, qqs = [], []
    for s in range(slabs):
        both = data[s, 0:width, :]
        zp, zq = both[:orbits], both[orbits:]
        with_p = mm_nt(both, turn_rows(zp))
        with_q = mm_nt(both, turn_rows(zq))
        pps.append(with_p[:orbits])
        qqs.append(with_q[orbits:])
        if s > 0:
            up1[s - 1] = -real_rows(with_q[:orbits])
            dn1[s - 1] = -real_rows(with_p[orbits:])
    for s in range(slabs):
        base = qqs[s]
        if s + 1 < slabs:
            base = base + pps[s + 1]
        if s == 0:
            base = base + pps[0]
        for e in range(mine):
            settings = data[s, pl.ds(2 * width + first + e, 1), :]
            m = spot[s] * mine + e
            gains[m] = settings
            block = base + jnp.where(diag_lane, settings, 0.0)
            mat[m] = block
            rhs[m] = data[s, width : 2 * width, :]
            sums = jnp.sum(jnp.abs(block), axis=0, keepdims=True)
            largest = sums if largest is None else jnp.maximum(largest, sums)
    top = 1.01 * jnp.max(largest + half_roll(largest))
    copy_out(3, 0, slabs - 1)
    copy_out(4, 0, slabs - 1)

    def held(key):
        basic, place = places[key]
        return (up1, dn1, place) if basic else (up2, dn2, place)

    def couplings(depth, node, left, right, e):
        if left is None:
            to_left = 0.0
        else:
            _, downs, place = held((depth, left, node, e))
            to_left = downs[place]
        if right is None:
            to_right = 0.0
        else:
            ups, _, place = held((depth, node, right, e))
            to_right = half_roll(ups[place])
        return jnp.where(low_all, to_left, to_right)

    for depth, level in enumerate(levels):
        invert_batch(mat, near, [spot[node] * mine + e for node, _, _ in level for e in range(mine)], top)
        for node, left, right in level:
            for e in range(mine):
                m = spot[node] * mine + e
                full = real_rows(near[m])
                inv[m] = full
                stacked = jnp.concatenate([couplings(depth, node, left, right, e), rhs[m]], axis=1)
                step = mm(full, stacked)
                links_step, rhs_step = step[:, :width], step[:, width:]
                sol[m] = rhs_step
                sides = []
                if left is not None:
                    w1[m] = real_left(links_step)
                    ups, _, place = held((depth, left, node, e))
                    sides.append(ups[place])
                if right is not None:
                    w2[m] = real_right(links_step)
                    _, downs, place = held((depth, node, right, e))
                    sides.append(downs[place])
                change = mm(sides[0] if len(sides) == 1 else jnp.concatenate(sides, axis=0), step)
                if left is not None:
                    ml = spot[left] * mine + e
                    mat[ml] = mat[ml] - packed_left(change[:width, :width])
                    rhs[ml] = rhs[ml] - change[:width, width:]
                if right is not None:
                    mr = spot[right] * mine + e
                    mat[mr] = mat[mr] - packed_right(change[-width:, :width])
                    rhs[mr] = rhs[mr] - change[-width:, width:]
                if left is not None and right is not None:
                    ups, downs, place = held((depth + 1, left, right, e))
                    ups[place] = -real_right(change[:width, :width])
                    downs[place] = -real_left(change[-width:, :width])
        span = [spot[node] * mine for node, _, _ in level]
        for which in range(3):
            copy_out(which, span[0], span[-1] + mine)
        made = [places[(depth + 1, l, r, e)][1] for _, l, r in level if l is not None and r is not None for e in range(mine)]
        if made:
            copy_out(5, made[0], made[-1] + 1)
            copy_out(6, made[0], made[-1] + 1)
    invert_batch(mat, near, [spot[root] * mine + e for e in range(mine)], top)
    for e in range(mine):
        m = spot[root] * mine + e
        full = real_rows(near[m])
        inv[m] = full
        sol[m] = mm(full, rhs[m])
    copy_out(0, spot[root] * mine, (spot[root] + 1) * mine)

    def finished(nodes):
        copy_out(7, spot[nodes[0]] * mine, (spot[nodes[-1]] + 1) * mine)
        for s in nodes:
            for e in range(mine):
                x = sol[spot[s] * mine + e]
                xr, xi = x[:orbits], x[orbits:]
                power = xr * xr + xi * xi
                for j in range(energy_groups):
                    power_ref[s // per, j, e, s % per, :, :] = power[j * orb_per : (j + 1) * orb_per, :]

    finished([root])
    climb(levels, spot, mine, w1, w2, sol, finished)
    for copy in copies:
        copy.wait()


def lesser_kernel(plan, gains, inv, w1, w2, up1, dn1, up2, dn2, ret, out_ref, rhs, sol):
    (slabs, mine, orbits, groups, energy_groups, per, orb_per) = plan
    width = 2 * orbits
    levels, root = elimination_levels(slabs)
    spot = slots(levels, root)
    places, _ = link_places(slabs, mine, levels)
    lane = lax.broadcasted_iota(jnp.int32, (orbits, width), 1)
    sub = lax.broadcasted_iota(jnp.int32, (orbits, width), 0)
    gain_lane = lane == sub + orbits
    for m in range(slabs * mine):
        gain = jnp.sum(jnp.where(gain_lane, gains[m], 0.0), axis=1, keepdims=True)
        rhs[m] = ret[m] * jnp.concatenate([gain, gain], axis=0)
    for depth, level in enumerate(levels):
        for node, left, right in level:
            for e in range(mine):
                m = spot[node] * mine + e
                step = mm(inv[m], rhs[m])
                sol[m] = step
                sides = []
                if left is not None:
                    basic, place = places[(depth, left, node, e)]
                    sides.append((up1 if basic else up2)[place])
                if right is not None:
                    basic, place = places[(depth, node, right, e)]
                    sides.append((dn1 if basic else dn2)[place])
                change = mm(sides[0] if len(sides) == 1 else jnp.concatenate(sides, axis=0), step)
                if left is not None:
                    ml = spot[left] * mine + e
                    rhs[ml] = rhs[ml] - change[:width]
                if right is not None:
                    mr = spot[right] * mine + e
                    rhs[mr] = rhs[mr] - change[-width:]
    for e in range(mine):
        m = spot[root] * mine + e
        sol[m] = mm(inv[m], rhs[m])
    climb(levels, spot, mine, w1, w2, sol, lambda nodes: None)
    for s in range(slabs):
        for e in range(mine):
            m = spot[s] * mine + e
            x, y = ret[m], sol[m]
            xr, xi, yr, yi = x[:orbits], x[orbits:], y[:orbits], y[orbits:]
            re = xr * yr + xi * yi
            im = xr * yi - xi * yr
            for j in range(energy_groups):
                rows = slice(j * orb_per, (j + 1) * orb_per)
                out_ref[s // per, j, 0, e, s % per, :, :] = re[rows, :]
                out_ref[s // per, j, 1, e, s % per, :, :] = im[rows, :]


def pack_kernel(where_ref, p_ref, q_ref, src_ref, shift_ref, gain_ref, factors_ref, settings_ref, parcel_ref):
    per, _, orbits, _ = p_ref.shape
    width = 2 * orbits
    local = shift_ref.shape[0]
    core = where_ref[2]
    for i in range(per):
        rows = [
            jnp.concatenate([shift_ref[e, i : i + 1, :], gain_ref[e, i : i + 1, :]], axis=1) for e in range(local)
        ]
        settings = jnp.concatenate(rows, axis=0)
        settings_ref[i] = settings
        parcel_ref[i, width : width + local, :] = settings
        factors_ref[i, 0:orbits, :] = jnp.concatenate([p_ref[i, 0], p_ref[i, 1]], axis=1)
        factors_ref[i, orbits:width, :] = jnp.concatenate([q_ref[i, 0], q_ref[i, 1]], axis=1)

    @pl.when(core == 0)
    def _():
        parcel_ref[:, 0:width, :] = factors_ref[...]

    @pl.when(core != 0)
    def _():
        for i in range(per):
            parcel_ref[i, 0:orbits, :] = src_ref[i, 0]
            parcel_ref[i, orbits:width, :] = src_ref[i, 1]


def pack(where, link_p, link_q, sources, shift, lesser_gain):
    per, _, orbits, _ = link_p.shape
    width = 2 * orbits
    columns = sources.shape[-1]
    local = shift.shape[0]
    shapes = [(per, width, width), (per, local, width), (per, width + local, columns)]
    return pl.pallas_call(
        pack_kernel,
        out_shape=[jax.ShapeDtypeStruct(shape, F32) for shape in shapes],
        in_specs=[pl.BlockSpec(memory_space=pltpu.SMEM)] + vmem_specs(5),
        out_specs=vmem_specs(3),
        compiler_params=pltpu.CompilerParams(vmem_limit_bytes=SMALL_LIMIT),
        name="pack_parcel",
    )(where, link_p, link_q, sources, shift, lesser_gain)


def vmem_specs(count):
    return [pl.BlockSpec(memory_space=pltpu.VMEM)] * count


def solve_retarded(where, pieces, plan, columns):
    (slabs, mine, orbits, groups, energy_groups, per, orb_per) = plan
    width = 2 * orbits
    nodes = slabs * mine
    levels, _ = elimination_levels(slabs)
    _, fills = link_places(slabs, mine, levels)
    local = pieces[2].shape[1]
    kept = [
        (nodes, width, width),
        (nodes, width, width),
        (nodes, width, width),
        (slabs - 1, width, width),
        (slabs - 1, width, width),
        (fills, width, width),
        (fills, width, width),
        (nodes, width, columns),
    ]
    shapes = [(groups, energy_groups, mine, per, orb_per, columns), (nodes, 1, width)] + kept
    return pl.pallas_call(
        functools.partial(retarded_kernel, plan),
        out_shape=[jax.ShapeDtypeStruct(shape, F32) for shape in shapes],
        in_specs=[pl.BlockSpec(memory_space=pltpu.SMEM)] + vmem_specs(len(pieces)),
        out_specs=vmem_specs(2) + [pl.BlockSpec(memory_space=pl.ANY)] * len(kept),
        scratch_shapes=[pltpu.VMEM(shape, F32) for shape in kept]
        + [
            pltpu.VMEM((slabs, 2 * width + local, columns), F32),
            pltpu.VMEM((nodes, orbits, width), F32),
            pltpu.VMEM((nodes, width, columns), F32),
            pltpu.VMEM((nodes, orbits, width), F32),
            pltpu.SemaphoreType.DMA((6 * len(levels) + 4,)),
        ],
        compiler_params=pltpu.CompilerParams(vmem_limit_bytes=VMEM_LIMIT),
        name="solve_retarded",
    )(where, *pieces)


def solve_lesser(stored, plan):
    (slabs, mine, orbits, groups, energy_groups, per, orb_per) = plan
    solved = stored[8].shape
    return pl.pallas_call(
        functools.partial(lesser_kernel, plan),
        out_shape=jax.ShapeDtypeStruct((groups, energy_groups, 2, mine, per, orb_per, solved[-1]), F32),
        in_specs=vmem_specs(len(stored)),
        out_specs=pl.BlockSpec(memory_space=pltpu.VMEM),
        scratch_shapes=[pltpu.VMEM(solved, F32), pltpu.VMEM(solved, F32)],
        compiler_params=pltpu.CompilerParams(vmem_limit_bytes=VMEM_LIMIT),
        name="solve_lesser",
    )(*stored)


def correlate_kernel(order, power_ref, got_ref, out_ref):
    count = len(order)
    window = 8
    scale = 1.0 / count
    for start in range(0, count, window):
        span = min(window, count - start)
        acc_re = [None] * span
        acc_im = [None] * span
        reach = count - start
        lead = {}
        for energy in range(reach):
            sender, place = order[energy]
            power = power_ref[sender, place, 0]
            for w in range(span):
                at = energy + start + w
                if at >= count:
                    continue
                if at not in lead:
                    s2, p2 = order[at]
                    lead[at] = (got_ref[s2, 0, p2, 0], got_ref[s2, 1, p2, 0])
                re, im = lead[at]
                acc_re[w] = re * power if acc_re[w] is None else acc_re[w] + re * power
                acc_im[w] = im * power if acc_im[w] is None else acc_im[w] + im * power
        for w in range(span):
            out_ref[0, start + w, 0] = acc_re[w] * scale
            out_ref[1, start + w, 0] = acc_im[w] * scale


def correlate(power, got, order):
    senders, kinds, mine, per, rows, columns = got.shape
    count = len(order)
    return pl.pallas_call(
        functools.partial(correlate_kernel, order),
        grid=(per,),
        out_shape=jax.ShapeDtypeStruct((2, count, per, rows, columns), F32),
        in_specs=[
            pl.BlockSpec((senders, mine, 1, rows, columns), lambda i: (0, 0, i, 0, 0)),
            pl.BlockSpec((senders, kinds, mine, 1, rows, columns), lambda i: (0, 0, 0, i, 0, 0)),
        ],
        out_specs=pl.BlockSpec((2, count, 1, rows, columns), lambda i: (0, 0, i, 0, 0)),
        compiler_params=pltpu.CompilerParams(vmem_limit_bytes=VMEM_LIMIT),
        name="correlate",
    )(power, got)


def per_device(link_p, link_q, shift, lesser_gain, sources):
    per, _, orbits, _ = link_p.shape
    width = 2 * orbits
    columns = sources.shape[-1]
    local = shift.shape[0]
    groups = lax.axis_size("slab")
    energy_groups = lax.axis_size("energy")
    slabs = per * groups
    mine = max(1, local // groups)
    owner = lax.axis_index("slab")
    columns_in = sources.reshape(per, width, columns)
    core = lax.axis_index("energy") & 1
    where = jnp.stack([owner * local // groups, owner, core]).astype(jnp.int32)
    factors, settings, parcel = pack(where, link_p, link_q, sources, shift, lesser_gain)
    siblings = [(j, j ^ 1) for j in range(energy_groups)]
    pieces = [factors, columns_in, settings]
    fetched = [lax.ppermute(parcel, "slab", [(g, g ^ k) for g in range(groups)]) for k in range(1, groups)]
    for piece in fetched:
        pieces.append(piece)
        pieces.append(lax.ppermute(piece, "energy", siblings))
    plan = (slabs, mine, orbits, groups, energy_groups, per, orbits // energy_groups)
    power, *stored = solve_retarded(where, pieces, plan, columns)

    def spread(array):
        array = array.reshape((groups * energy_groups,) + array.shape[2:])
        return lax.all_to_all(array, ("slab", "energy"), split_axis=0, concat_axis=0, tiled=True)

    power = spread(power)
    got = spread(solve_lesser(stored, plan))
    order = []
    for group in range(energy_groups):
        for row in range(local):
            if local >= groups:
                holder, place = row // mine, row % mine
            else:
                holder, place = -(-row * groups // local), 0
            order.append((holder * energy_groups + group, place))
    return correlate(power, got, tuple(order))


def solution(mesh):
    placed = (
        P("slab", None, None, None),
        P("slab", None, None, None),
        P("energy", "slab", None),
        P("energy", "slab", None),
        P("slab", None, None, None),
    )
    return jax.shard_map(
        per_device,
        mesh=mesh,
        in_specs=placed,
        out_specs=P(None, None, "slab", "energy", None),
        check_vma=False,
    )
```

```python
import functools

import jax
import jax.numpy as jnp
from jax import lax
from jax.experimental import pallas as pl
from jax.experimental.pallas import tpu as pltpu
from jax.sharding import PartitionSpec as P

F32 = jnp.float32
BF16 = jnp.bfloat16
VMEM_LIMIT = 56 * 1024 * 1024
LEAST = 0.0095
CLOSE = 1e-3
STRIDE = 4
HALVES = 2


def elimination_levels(count):
    levels = []
    chain = list(range(count))
    while len(chain) > 1:
        level = []
        for place in range(0, len(chain), 2):
            left = chain[place - 1] if place > 0 else None
            right = chain[place + 1] if place + 1 < len(chain) else None
            level.append((chain[place], left, right))
        levels.append(level)
        chain = chain[1::2]
    return levels, chain[0]


def thirds(x):
    one = x.astype(BF16)
    rest = x - one.astype(F32)
    two = rest.astype(BF16)
    three = (rest - two.astype(F32)).astype(BF16)
    return one, two, three


def mm(a, b):
    a1, a2, a3 = thirds(a)
    b1, b2, b3 = thirds(b)
    left = jnp.concatenate([a1, a2, a1, a2, a1, a3], axis=1)
    right = jnp.concatenate([b1, b1, b2, b2, b3, b1], axis=0)
    return lax.dot_general(left, right, (((1,), (0,)), ((), ())), preferred_element_type=F32)


def mm_three(a, b):
    a1 = a.astype(BF16)
    a2 = (a - a1.astype(F32)).astype(BF16)
    b1 = b.astype(BF16)
    b2 = (b - b1.astype(F32)).astype(BF16)
    left = jnp.concatenate([a1, a2, a1], axis=1)
    right = jnp.concatenate([b1, b1, b2], axis=0)
    return lax.dot_general(left, right, (((1,), (0,)), ((), ())), preferred_element_type=F32)


def mm_nt(a, b):
    a1, a2, a3 = thirds(a)
    b1, b2, b3 = thirds(b)
    left = jnp.concatenate([a1, a2, a1, a2, a1, a3], axis=1)
    right = jnp.concatenate([b1, b1, b2, b2, b3, b1], axis=1)
    return lax.dot_general(left, right, (((1,), (1,)), ((), ())), preferred_element_type=F32)


def half_roll(x):
    return pltpu.roll(x, x.shape[1] // 2, 1)


def turn_rows(z):
    low = lax.broadcasted_iota(jnp.int32, z.shape, 1) < z.shape[1] // 2
    turned = half_roll(z)
    return jnp.concatenate([z, jnp.where(low, -turned, turned)], axis=0)


def packed_mm(a, b):
    return mm_three(a, turn_rows(b))


def invert_batch(mat_ref, inv_ref, members, top):
    shape = mat_ref.shape[1:]
    count = shape[0]
    lane = lax.broadcasted_iota(jnp.int32, shape, 1)
    sub = lax.broadcasted_iota(jnp.int32, shape, 0)
    eye = jnp.where(lane == sub, 1.0, 0.0).astype(F32)
    total = top + LEAST

    def factor_of(reach):
        squared = reach * reach
        gain = 2.0 / (2.0 - squared)
        return gain, 0.5 * squared * gain

    def steps(xs, ts, reach, number):
        for step in range(number):
            gain, reach = factor_of(reach)
            bases = [(2.0 * eye - t) * gain for t in ts]
            if step + 1 < number:
                pairs = [packed_mm(jnp.concatenate([x, t], axis=0), base) for x, t, base in zip(xs, ts, bases)]
                xs = [pair[:count] for pair in pairs]
                ts = [pair[count:] for pair in pairs]
            else:
                xs = [packed_mm(x, base) for x, base in zip(xs, bases)]
        for m, x in zip(members, xs):
            inv_ref[m] = x
        return reach

    reach = (top - LEAST) / total
    start = 2.0 / total
    gain, reach = factor_of(reach)
    ts = [mat_ref[m] * start for m in members]
    bases = [(2.0 * eye - t) * gain for t in ts]
    xs = [base * start for base in bases]
    ts = [packed_mm(t, base) for t, base in zip(ts, bases)]
    reach = steps(xs, ts, reach, STRIDE - 1)

    def body(reach):
        xs = [inv_ref[m] for m in members]
        ts = [packed_mm(mat_ref[m], x) for m, x in zip(members, xs)]
        return steps(xs, ts, reach, STRIDE)

    lax.while_loop(lambda reach: reach > CLOSE, body, reach)
    xs = [inv_ref[m] for m in members]
    rests = [eye - mm(mat_ref[m], turn_rows(x)) for m, x in zip(members, xs)]
    for m, x, rest in zip(members, xs, rests):
        inv_ref[m] = x + packed_mm(x, rest)


def slots(levels, root):
    order = [node for level in levels for node, _, _ in level] + [root]
    return {node: place for place, node in enumerate(order)}


def link_places(slabs, mine, levels):
    places = {}
    for s in range(slabs - 1):
        for e in range(mine):
            places[(0, s, s + 1, e)] = (True, s)
    spare = 0
    for depth, level in enumerate(levels):
        for node, left, right in level:
            if left is not None and right is not None:
                for e in range(mine):
                    places[(depth + 1, left, right, e)] = (False, spare)
                    spare += 1
    return places, spare


def climb(levels, spot, mine, w1, w2, sol, finished):
    for level in reversed(levels):
        for node, left, right in level:
            for e in range(mine):
                m = spot[node] * mine + e
                if left is not None and right is not None:
                    both = jnp.concatenate([w1[m], w2[m]], axis=1)
                    sides = jnp.concatenate([sol[spot[left] * mine + e], sol[spot[right] * mine + e]], axis=0)
                    sol[m] = sol[m] - mm_three(both, sides)
                elif left is not None:
                    sol[m] = sol[m] - mm_three(w1[m], sol[spot[left] * mine + e])
                elif right is not None:
                    sol[m] = sol[m] - mm_three(w2[m], sol[spot[right] * mine + e])
        finished([node for node, _, _ in level])


def orbitals_of(ref, m, half, halves, orbits):
    count = orbits // halves
    found = [ref[m, 0:count, :], ref[m, orbits : orbits + count, :]]
    for h in range(1, halves):
        found = [
            jnp.where(half == h, ref[m, low + h * count : low + (h + 1) * count, :], kept)
            for low, kept in zip((0, orbits), found)
        ]
    return found


def retarded_kernel(plan, where_ref, *refs):
    (slabs, mine, orbits, groups, halves, lines, per, orb_per) = plan
    pq_ref, src_ref, set_ref = refs[0], refs[1], refs[2]
    peers = refs[3 : 3 + 2 * (groups - 1)]
    refs = refs[3 + 2 * (groups - 1) :]
    others = refs[: (halves - 1) * groups]
    refs = refs[(halves - 1) * groups :]
    power_ref, gains = refs[:2]
    outs = refs[2:10]
    inv, w1, w2, up1, dn1, up2, dn2, sol, data, mat, rhs, near, sems = refs[10:]
    stores = (inv, w1, w2, up1, dn1, up2, dn2, sol)
    copies = []

    def copy_out(which, low_place, high_place):
        part = pl.ds(low_place, high_place - low_place)
        copy = pltpu.make_async_copy(stores[which].at[part], outs[which].at[part], sems.at[len(copies)])
        copy.start()
        copies.append(copy)

    width = 2 * orbits
    levels, root = elimination_levels(slabs)
    spot = slots(levels, root)
    places, _ = link_places(slabs, mine, levels)
    lane = lax.broadcasted_iota(jnp.int32, (orbits, width), 1)
    sub = lax.broadcasted_iota(jnp.int32, (orbits, width), 0)
    low = lane < orbits
    low_all = lax.broadcasted_iota(jnp.int32, (width, width), 1) < orbits
    diag_lane = lane == sub
    first, owner, core, half = where_ref[0], where_ref[1], where_ref[2], where_ref[3]

    local = set_ref.shape[1]
    for i in range(per):
        at = owner * per + i
        data[at, 0:width, :] = pq_ref[i]
        data[at, width : 2 * width, :] = src_ref[i]
        data[at, 2 * width : 2 * width + local, :] = set_ref[i]
    for k in range(1, groups):
        mine_half, other_half = peers[2 * (k - 1)], peers[2 * (k - 1) + 1]
        for i in range(per):
            at = (owner ^ k) * per + i
            data[at, pl.ds(pl.multiple_of(core * width, width), width), :] = mine_half[i, 0:width, :]
            data[at, pl.ds(pl.multiple_of((1 - core) * width, width), width), :] = other_half[i, 0:width, :]
            data[at, 2 * width : 2 * width + local, :] = mine_half[i, width : width + local, :]

    for h in range(1, halves):
        for k in range(groups):
            for i in range(per):
                at = (owner ^ k) * per + i
                low_row = 2 * width + h * local
                data[at, low_row : low_row + local, :] = others[(h - 1) * groups + k][i]

    def real_rows(z):
        return jnp.concatenate([jnp.where(low, z, -z), half_roll(z)], axis=0)

    def real_left(t):
        top, bottom = t[:orbits], t[orbits:]
        return jnp.concatenate(
            [jnp.where(low, top, -half_roll(bottom)), jnp.where(low, bottom, half_roll(top))], axis=0
        )

    def real_right(t):
        top, bottom = t[:orbits], t[orbits:]
        return jnp.concatenate(
            [jnp.where(low, half_roll(top), -bottom), jnp.where(low, half_roll(bottom), top)], axis=0
        )

    def packed_left(t):
        return jnp.where(low, t[:orbits], half_roll(t[orbits:]))

    def packed_right(t):
        return jnp.where(low, half_roll(t[:orbits]), t[orbits:])

    largest = None
    pps, qqs = [], []
    for s in range(slabs):
        both = data[s, 0:width, :]
        zp, zq = both[:orbits], both[orbits:]
        with_p = mm_nt(both, turn_rows(zp))
        with_q = mm_nt(both, turn_rows(zq))
        pps.append(with_p[:orbits])
        qqs.append(with_q[orbits:])
        if s > 0:
            up1[s - 1] = -real_rows(with_q[:orbits])
            dn1[s - 1] = -real_rows(with_p[orbits:])
    for s in range(slabs):
        base = qqs[s]
        if s + 1 < slabs:
            base = base + pps[s + 1]
        if s == 0:
            base = base + pps[0]
        for e in range(mine):
            share = mine // halves
            row = 2 * width + ((e // share) ^ half) * local + first + e % share
            settings = data[s, pl.ds(row, 1), :]
            m = spot[s] * mine + e
            gains[m] = settings
            block = base + jnp.where(diag_lane, settings, 0.0)
            mat[m] = block
            rhs[m] = data[s, width : 2 * width, :]
            sums = jnp.sum(jnp.abs(block), axis=0, keepdims=True)
            largest = sums if largest is None else jnp.maximum(largest, sums)
    top = 1.01 * jnp.max(largest + half_roll(largest))
    copy_out(3, 0, slabs - 1)
    copy_out(4, 0, slabs - 1)

    def held(key):
        basic, place = places[key]
        return (up1, dn1, place) if basic else (up2, dn2, place)

    def couplings(depth, node, left, right, e):
        if left is None:
            to_left = 0.0
        else:
            _, downs, place = held((depth, left, node, e))
            to_left = downs[place]
        if right is None:
            to_right = 0.0
        else:
            ups, _, place = held((depth, node, right, e))
            to_right = half_roll(ups[place])
        return jnp.where(low_all, to_left, to_right)

    for depth, level in enumerate(levels):
        invert_batch(mat, near, [spot[node] * mine + e for node, _, _ in level for e in range(mine)], top)
        for node, left, right in level:
            for e in range(mine):
                m = spot[node] * mine + e
                full = real_rows(near[m])
                inv[m] = full
                stacked = jnp.concatenate([couplings(depth, node, left, right, e), rhs[m]], axis=1)
                step = mm(full, stacked)
                links_step, rhs_step = step[:, :width], step[:, width:]
                sol[m] = rhs_step
                sides = []
                if left is not None:
                    w1[m] = real_left(links_step)
                    ups, _, place = held((depth, left, node, e))
                    sides.append(ups[place])
                if right is not None:
                    w2[m] = real_right(links_step)
                    _, downs, place = held((depth, node, right, e))
                    sides.append(downs[place])
                change = mm(sides[0] if len(sides) == 1 else jnp.concatenate(sides, axis=0), step)
                if left is not None:
                    ml = spot[left] * mine + e
                    mat[ml] = mat[ml] - packed_left(change[:width, :width])
                    rhs[ml] = rhs[ml] - change[:width, width:]
                if right is not None:
                    mr = spot[right] * mine + e
                    mat[mr] = mat[mr] - packed_right(change[-width:, :width])
                    rhs[mr] = rhs[mr] - change[-width:, width:]
                if left is not None and right is not None:
                    ups, downs, place = held((depth + 1, left, right, e))
                    ups[place] = -real_right(change[:width, :width])
                    downs[place] = -real_left(change[-width:, :width])
        span = [spot[node] * mine for node, _, _ in level]
        for which in range(3):
            copy_out(which, span[0], span[-1] + mine)
        made = [places[(depth + 1, l, r, e)][1] for _, l, r in level if l is not None and r is not None for e in range(mine)]
        if made:
            copy_out(5, made[0], made[-1] + 1)
            copy_out(6, made[0], made[-1] + 1)
    invert_batch(mat, near, [spot[root] * mine + e for e in range(mine)], top)
    for e in range(mine):
        m = spot[root] * mine + e
        full = real_rows(near[m])
        inv[m] = full
        sol[m] = mm(full, rhs[m])
    copy_out(0, spot[root] * mine, (spot[root] + 1) * mine)

    def finished(nodes):
        copy_out(7, spot[nodes[0]] * mine, (spot[nodes[-1]] + 1) * mine)
        for s in nodes:
            for e in range(mine):
                m = spot[s] * mine + e
                xr, xi = orbitals_of(sol, m, half, halves, orbits)
                power = xr * xr + xi * xi
                for j in range(lines):
                    power_ref[s // per, j, e, s % per, :, :] = power[j * orb_per : (j + 1) * orb_per, :]

    finished([root])
    climb(levels, spot, mine, w1, w2, sol, finished)
    for copy in copies:
        copy.wait()


def lesser_kernel(plan, where_ref, gains, *refs):
    (slabs, mine, orbits, groups, halves, lines, per, orb_per) = plan
    stores, out_ref = refs[:8], refs[8]
    inv, w1, w2, up1, dn1, up2, dn2, ret, rhs, sol, sems = refs[9:]
    held = (inv, w1, w2, up1, dn1, up2, dn2, ret)
    half = where_ref[3]
    width = 2 * orbits
    levels, root = elimination_levels(slabs)
    spot = slots(levels, root)
    places, _ = link_places(slabs, mine, levels)
    fetches = {}

    def fetch(which, depth, low_place, high_place):
        part = pl.ds(low_place, high_place - low_place)
        copy = pltpu.make_async_copy(stores[which].at[part], held[which].at[part], sems.at[len(fetches)])
        copy.start()
        fetches[(which, depth)] = copy

    spans = []
    for level in levels:
        span = [spot[node] * mine for node, _, _ in level]
        spans.append((span[0], span[-1] + mine))
    spans.append((spot[root] * mine, (spot[root] + 1) * mine))
    for depth, span in enumerate(spans):
        fetch(7, depth, *span)
        fetch(0, depth, *span)
        if depth == 0:
            fetch(3, 0, 0, slabs - 1)
            fetch(4, 0, 0, slabs - 1)
        elif depth < len(levels):
            level = levels[depth - 1]
            made = [places[(depth, l, r, e)][1] for _, l, r in level if l is not None and r is not None for e in range(mine)]
            if made:
                fetch(5, depth, made[0], made[-1] + 1)
                fetch(6, depth, made[0], made[-1] + 1)
    for depth in range(len(levels) - 1, -1, -1):
        fetch(1, depth, *spans[depth])
        fetch(2, depth, *spans[depth])
    for depth in range(len(spans)):
        fetches[(7, depth)].wait()
    lane = lax.broadcasted_iota(jnp.int32, (orbits, width), 1)
    sub = lax.broadcasted_iota(jnp.int32, (orbits, width), 0)
    gain_lane = lane == sub + orbits
    for m in range(slabs * mine):
        gain = jnp.sum(jnp.where(gain_lane, gains[m], 0.0), axis=1, keepdims=True)
        rhs[m] = ret[m] * jnp.concatenate([gain, gain], axis=0)
    for depth, level in enumerate(levels):
        for which in (0, 3, 4, 5, 6):
            if (which, depth) in fetches:
                fetches[(which, depth)].wait()
        for node, left, right in level:
            for e in range(mine):
                m = spot[node] * mine + e
                step = mm(inv[m], rhs[m])
                sol[m] = step
                sides = []
                if left is not None:
                    basic, place = places[(depth, left, node, e)]
                    sides.append((up1 if basic else up2)[place])
                if right is not None:
                    basic, place = places[(depth, node, right, e)]
                    sides.append((dn1 if basic else dn2)[place])
                change = mm(sides[0] if len(sides) == 1 else jnp.concatenate(sides, axis=0), step)
                if left is not None:
                    ml = spot[left] * mine + e
                    rhs[ml] = rhs[ml] - change[:width]
                if right is not None:
                    mr = spot[right] * mine + e
                    rhs[mr] = rhs[mr] - change[-width:]
    fetches[(0, len(levels))].wait()
    for e in range(mine):
        m = spot[root] * mine + e
        sol[m] = mm(inv[m], rhs[m])
    for depth in range(len(levels)):
        fetches[(1, depth)].wait()
        fetches[(2, depth)].wait()
    climb(levels, spot, mine, w1, w2, sol, lambda nodes: None)
    for s in range(slabs):
        for e in range(mine):
            m = spot[s] * mine + e
            xr, xi = orbitals_of(ret, m, half, halves, orbits)
            yr, yi = orbitals_of(sol, m, half, halves, orbits)
            re = xr * yr + xi * yi
            im = xr * yi - xi * yr
            for j in range(lines):
                rows = slice(j * orb_per, (j + 1) * orb_per)
                out_ref[s // per, j, 0, e, s % per, :, :] = re[rows, :]
                out_ref[s // per, j, 1, e, s % per, :, :] = im[rows, :]


def pack_kernel(where_ref, p_ref, q_ref, src_ref, shift_ref, gain_ref, factors_ref, settings_ref, parcel_ref):
    per, _, orbits, _ = p_ref.shape
    width = 2 * orbits
    local = shift_ref.shape[1]
    core = where_ref[2]
    for i in range(per):
        settings = jnp.concatenate([shift_ref[i], gain_ref[i]], axis=1)
        settings_ref[i] = settings
        parcel_ref[i, width : width + local, :] = settings
        factors_ref[i, 0:orbits, :] = jnp.concatenate([p_ref[i, 0], p_ref[i, 1]], axis=1)
        factors_ref[i, orbits:width, :] = jnp.concatenate([q_ref[i, 0], q_ref[i, 1]], axis=1)

    @pl.when(core == 0)
    def _():
        parcel_ref[:, 0:width, :] = factors_ref[...]

    @pl.when(core != 0)
    def _():
        for i in range(per):
            parcel_ref[i, 0:orbits, :] = src_ref[i, 0]
            parcel_ref[i, orbits:width, :] = src_ref[i, 1]


def pack(where, link_p, link_q, sources, shift, lesser_gain):
    per, _, orbits, _ = link_p.shape
    width = 2 * orbits
    columns = sources.shape[-1]
    local = shift.shape[1]
    shapes = [(per, width, width), (per, local, width), (per, width + local, columns)]
    return pl.pallas_call(
        pack_kernel,
        out_shape=[jax.ShapeDtypeStruct(shape, F32) for shape in shapes],
        in_specs=[pl.BlockSpec(memory_space=pltpu.SMEM)] + vmem_specs(5),
        out_specs=vmem_specs(3),
        compiler_params=pltpu.CompilerParams(vmem_limit_bytes=VMEM_LIMIT),
        name="pack_parcel",
    )(where, link_p, link_q, sources, shift, lesser_gain)


def vmem_specs(count):
    return [pl.BlockSpec(memory_space=pltpu.VMEM)] * count


def solve_retarded(where, pieces, plan, columns):
    (slabs, mine, orbits, groups, halves, lines, per, orb_per) = plan
    width = 2 * orbits
    nodes = slabs * mine
    levels, _ = elimination_levels(slabs)
    _, fills = link_places(slabs, mine, levels)
    local = halves * pieces[2].shape[1]
    kept = [
        (nodes, width, width),
        (nodes, width, width),
        (nodes, width, width),
        (slabs - 1, width, width),
        (slabs - 1, width, width),
        (fills, width, width),
        (fills, width, width),
        (nodes, width, columns),
    ]
    shapes = [(groups, lines, mine, per, orb_per, columns), (nodes, 1, width)] + kept
    return pl.pallas_call(
        functools.partial(retarded_kernel, plan),
        out_shape=[jax.ShapeDtypeStruct(shape, F32) for shape in shapes],
        in_specs=[pl.BlockSpec(memory_space=pltpu.SMEM)] + vmem_specs(len(pieces)),
        out_specs=vmem_specs(2) + [pl.BlockSpec(memory_space=pl.ANY)] * len(kept),
        scratch_shapes=[pltpu.VMEM(shape, F32) for shape in kept]
        + [
            pltpu.VMEM((slabs, 2 * width + local, columns), F32),
            pltpu.VMEM((nodes, orbits, width), F32),
            pltpu.VMEM((nodes, width, columns), F32),
            pltpu.VMEM((nodes, orbits, width), F32),
            pltpu.SemaphoreType.DMA((6 * len(levels) + 4,)),
        ],
        compiler_params=pltpu.CompilerParams(vmem_limit_bytes=VMEM_LIMIT),
        name="solve_retarded",
    )(where, *pieces)


def solve_lesser(where, stored, plan):
    (slabs, mine, orbits, groups, halves, lines, per, orb_per) = plan
    levels, _ = elimination_levels(slabs)
    gains, kept = stored[0], stored[1:]
    solved = kept[7].shape
    return pl.pallas_call(
        functools.partial(lesser_kernel, plan),
        out_shape=jax.ShapeDtypeStruct((groups, lines, 2, mine, per, orb_per, solved[-1]), F32),
        in_specs=[pl.BlockSpec(memory_space=pltpu.SMEM)]
        + vmem_specs(1)
        + [pl.BlockSpec(memory_space=pl.ANY)] * len(kept),
        out_specs=pl.BlockSpec(memory_space=pltpu.VMEM),
        scratch_shapes=[pltpu.VMEM(array.shape, F32) for array in kept]
        + [pltpu.VMEM(solved, F32), pltpu.VMEM(solved, F32), pltpu.SemaphoreType.DMA((6 * len(levels) + 4,))],
        compiler_params=pltpu.CompilerParams(vmem_limit_bytes=VMEM_LIMIT),
        name="solve_lesser",
    )(where, gains, *kept)


def correlate_kernel(order, power_ref, got_ref, out_ref):
    count = len(order)
    window = 8
    scale = 1.0 / count
    for start in range(0, count, window):
        span = min(window, count - start)
        acc_re = [None] * span
        acc_im = [None] * span
        reach = count - start
        lead = {}
        for energy in range(reach):
            sender, place = order[energy]
            power = power_ref[sender, place, 0]
            for w in range(span):
                at = energy + start + w
                if at >= count:
                    continue
                if at not in lead:
                    s2, p2 = order[at]
                    lead[at] = (got_ref[s2, 0, p2, 0], got_ref[s2, 1, p2, 0])
                re, im = lead[at]
                acc_re[w] = re * power if acc_re[w] is None else acc_re[w] + re * power
                acc_im[w] = im * power if acc_im[w] is None else acc_im[w] + im * power
        for w in range(span):
            out_ref[0, start + w, 0] = acc_re[w] * scale
            out_ref[1, start + w, 0] = acc_im[w] * scale


def correlate(power, got, order):
    senders, kinds, mine, per, rows, columns = got.shape
    count = len(order)
    return pl.pallas_call(
        functools.partial(correlate_kernel, order),
        grid=(per,),
        out_shape=jax.ShapeDtypeStruct((2, count, per, rows, columns), F32),
        in_specs=[
            pl.BlockSpec((senders, mine, 1, rows, columns), lambda i: (0, 0, i, 0, 0)),
            pl.BlockSpec((senders, kinds, mine, 1, rows, columns), lambda i: (0, 0, 0, i, 0, 0)),
        ],
        out_specs=pl.BlockSpec((2, count, 1, rows, columns), lambda i: (0, 0, i, 0, 0)),
        compiler_params=pltpu.CompilerParams(vmem_limit_bytes=VMEM_LIMIT),
        name="correlate",
    )(power, got)


def per_device(link_p, link_q, shift, lesser_gain, sources):
    per, _, orbits, _ = link_p.shape
    width = 2 * orbits
    columns = sources.shape[-1]
    local = shift.shape[0]
    groups = lax.axis_size("slab")
    halves = lax.axis_size("half")
    lines = lax.axis_size("line")
    slabs = per * groups
    share = max(1, local // groups)
    mine = halves * share
    owner = lax.axis_index("slab")
    half = lax.axis_index("half")
    core = lax.axis_index("line") & 1
    where = jnp.stack([owner * local // groups, owner, core, half]).astype(jnp.int32)
    factors, settings, parcel = pack(
        where, link_p, link_q, sources, jnp.swapaxes(shift, 0, 1), jnp.swapaxes(lesser_gain, 0, 1)
    )
    pieces = [factors, sources.reshape(per, width, columns), settings]
    fetched = [lax.ppermute(parcel, "slab", [(g, g ^ k) for g in range(groups)]) for k in range(1, groups)]
    siblings = [(j, j ^ 1) for j in range(lines)]
    for piece in fetched:
        pieces.append(piece)
        pieces.append(lax.ppermute(piece, "line", siblings))
    for h in range(1, halves):
        for k in range(groups):
            moves = [(g * halves + a, (g ^ k) * halves + (a ^ h)) for g in range(groups) for a in range(halves)]
            pieces.append(lax.ppermute(settings, ("slab", "half"), moves))
    plan = (slabs, mine, orbits, groups, halves, lines, per, orbits // (halves * lines))
    power, *stored = solve_retarded(where, pieces, plan, columns)

    def spread(array):
        array = array.reshape((groups * lines,) + array.shape[2:])
        return lax.all_to_all(array, ("slab", "line"), split_axis=0, concat_axis=0, tiled=True)

    power = spread(power)
    got = spread(solve_lesser(where, stored, plan))
    order = []
    for energy in range(halves * lines * local):
        group, row = energy // local, energy % local
        if local >= groups:
            holder, place = row // share, row % share
        else:
            holder, place = -(-row * groups // local), 0
        order.append((holder * lines + group % lines, (group // lines) * share + place))
    return correlate(power, got, tuple(order))


def solution(mesh):
    slab_size, energy_size = mesh.devices.shape
    halves = HALVES if energy_size % (2 * HALVES) == 0 else 1
    split = jax.sharding.Mesh(
        mesh.devices.reshape(slab_size, halves, energy_size // halves), ("slab", "half", "line")
    )
    placed = (
        P("slab", None, None, None),
        P("slab", None, None, None),
        P(("half", "line"), "slab", None),
        P(("half", "line"), "slab", None),
        P("slab", None, None, None),
    )
    return jax.shard_map(
        per_device,
        mesh=split,
        in_specs=placed,
        out_specs=P(None, None, "slab", ("half", "line"), None),
        check_vma=False,
    )
```

```python
import functools

import jax
import jax.numpy as jnp
from jax import lax
from jax.experimental import pallas as pl
from jax.experimental.pallas import tpu as pltpu
from jax.sharding import PartitionSpec as P

F32 = jnp.float32
BF16 = jnp.bfloat16
VMEM_LIMIT = 56 * 1024 * 1024
LEAST = 0.0095
CLOSE = 1e-3
STRIDE = 4
HALVES = 2


def elimination_levels(count):
    levels = []
    chain = list(range(count))
    while len(chain) > 1:
        level = []
        for place in range(0, len(chain), 2):
            left = chain[place - 1] if place > 0 else None
            right = chain[place + 1] if place + 1 < len(chain) else None
            level.append((chain[place], left, right))
        levels.append(level)
        chain = chain[1::2]
    return levels, chain[0]


def split(x, count):
    parts = []
    for place in range(count):
        part = x.astype(BF16)
        parts.append(part)
        if place + 1 < count:
            x = x - part.astype(F32)
    return parts


def half_roll(x):
    return pltpu.roll(x, x.shape[1] // 2, 1)


def turned(block, count):
    half = block.shape[1] // 2
    top = split(block, count)
    if half % 128 == 0:
        bottom = [jnp.concatenate([-part[:, half:], part[:, :half]], axis=1) for part in top]
    else:
        low = lax.broadcasted_iota(jnp.int32, block.shape, 1) < half
        rolled = half_roll(block)
        bottom = split(jnp.where(low, -rolled, rolled), count)
    return [jnp.concatenate([one, two], axis=0) for one, two in zip(top, bottom)]


def beside(blocks, count):
    parts = [turned(block, count) for block in blocks]
    if len(parts) == 1:
        return parts[0]
    return [jnp.concatenate([part[k] for part in parts], axis=1) for k in range(count)]


def above(blocks, count):
    parts = [turned(block, count) for block in blocks]
    if len(parts) == 1:
        return parts[0]
    return [jnp.concatenate([part[k] for part in parts], axis=0) for k in range(count)]


def times(a, right, contract=0):
    left = split(a, len(right))
    if len(right) == 3:
        left = [left[0], left[1], left[0], left[1], left[0], left[2]]
        right = [right[0], right[0], right[1], right[1], right[2], right[0]]
    else:
        left = [left[0], left[1], left[0]]
        right = [right[0], right[0], right[1]]
    return lax.dot_general(
        jnp.concatenate(left, axis=1),
        jnp.concatenate(right, axis=contract),
        (((1,), (contract,)), ((), ())),
        preferred_element_type=F32,
    )


def invert_batch(mat_ref, inv_ref, members, top):
    shape = mat_ref.shape[1:]
    width = shape[1]
    lane = lax.broadcasted_iota(jnp.int32, shape, 1)
    sub = lax.broadcasted_iota(jnp.int32, shape, 0)
    eye = jnp.where(lane == sub, 1.0, 0.0).astype(F32)
    total = top + LEAST

    def factor_of(reach):
        squared = reach * reach
        gain = 2.0 / (2.0 - squared)
        return gain, 0.5 * squared * gain

    def steps(xs, ts, reach, number):
        for step in range(number):
            gain, reach = factor_of(reach)
            bases = [(2.0 * eye - t) * gain for t in ts]
            if step + 1 < number:
                pairs = [times(base, beside([x, t], 2)) for x, t, base in zip(xs, ts, bases)]
                xs = [pair[:, :width] for pair in pairs]
                ts = [pair[:, width:] for pair in pairs]
            else:
                xs = [times(base, turned(x, 2)) for x, base in zip(xs, bases)]
        for m, x in zip(members, xs):
            inv_ref[m] = x
        return reach

    reach = (top - LEAST) / total
    start = 2.0 / total
    gain, reach = factor_of(reach)
    ts = [mat_ref[m] * start for m in members]
    bases = [(2.0 * eye - t) * gain for t in ts]
    xs = [base * start for base in bases]
    ts = [times(base, turned(t, 2)) for t, base in zip(ts, bases)]
    reach = steps(xs, ts, reach, STRIDE - 1)

    def body(reach):
        xs = [inv_ref[m] for m in members]
        ts = [times(mat_ref[m], turned(x, 2)) for m, x in zip(members, xs)]
        return steps(xs, ts, reach, STRIDE)

    lax.while_loop(lambda reach: reach > CLOSE, body, reach)
    xs = [inv_ref[m] for m in members]
    rests = [eye - times(mat_ref[m], turned(x, 3)) for m, x in zip(members, xs)]
    for m, x, rest in zip(members, xs, rests):
        inv_ref[m] = x + times(x, turned(rest, 2))


def slots(levels, root):
    order = [node for level in levels for node, _, _ in level] + [root]
    return {node: place for place, node in enumerate(order)}


def link_places(slabs, mine, levels):
    places = {}
    for s in range(slabs - 1):
        for e in range(mine):
            places[(0, s, s + 1, e)] = (True, s)
    spare = 0
    for depth, level in enumerate(levels):
        for node, left, right in level:
            if left is not None and right is not None:
                for e in range(mine):
                    places[(depth + 1, left, right, e)] = (False, spare)
                    spare += 1
    return places, spare


def climb(levels, spot, mine, w1, w2, sol, finished):
    for level in reversed(levels):
        for node, left, right in level:
            for e in range(mine):
                m = spot[node] * mine + e
                steps, sides = [], []
                if left is not None:
                    steps.append(w1[m])
                    sides.append(sol[spot[left] * mine + e])
                if right is not None:
                    steps.append(w2[m])
                    sides.append(sol[spot[right] * mine + e])
                steps = steps[0] if len(steps) == 1 else jnp.concatenate(steps, axis=1)
                sol[m] = sol[m] - times(steps, above(sides, 2))
        finished([node for node, _, _ in level])


def orbitals_of(ref, m, half, halves, orbits):
    count = orbits // halves
    found = ref[m, 0:count, :]
    for h in range(1, halves):
        found = jnp.where(half == h, ref[m, h * count : (h + 1) * count, :], found)
    columns = found.shape[1] // 2
    return found[:, :columns], found[:, columns:]


def retarded_kernel(plan, where_ref, *refs):
    (slabs, mine, orbits, groups, halves, lines, per, orb_per) = plan
    factors_ref, src_ref, settings_ref = refs[:3]
    peers = refs[3 : 3 + 2 * (groups - 1)]
    refs = refs[3 + 2 * (groups - 1) :]
    power_ref, gains, outs = refs[0], refs[1], refs[2:10]
    inv, w1, w2, up1, dn1, up2, dn2, sol, data, mat, rhs, sems = refs[10:]
    stores = (inv, w1, w2, up1, dn1, up2, dn2, sol)
    copies = []

    def copy_out(which, low_place, high_place):
        part = pl.ds(low_place, high_place - low_place)
        copy = pltpu.make_async_copy(stores[which].at[part], outs[which].at[part], sems.at[len(copies)])
        copy.start()
        copies.append(copy)

    width = 2 * orbits
    columns = src_ref.shape[-1]
    share = mine // halves
    levels, root = elimination_levels(slabs)
    spot = slots(levels, root)
    places, _ = link_places(slabs, mine, levels)
    lane = lax.broadcasted_iota(jnp.int32, (orbits, width), 1)
    sub = lax.broadcasted_iota(jnp.int32, (orbits, width), 0)
    diag_lane = lane == sub
    first, owner, core, half = where_ref[0], where_ref[1], where_ref[2], where_ref[3]

    for i in range(per):
        at = owner * per + i
        data[at, 0:width, :] = factors_ref[i]
        data[at, width : width + orbits, :] = src_ref[i, 0]
        data[at, width + orbits : 2 * width, :] = src_ref[i, 1]
    for k in range(1, groups):
        mine_half, other_half = peers[2 * (k - 1)], peers[2 * (k - 1) + 1]
        for i in range(per):
            at = (owner ^ k) * per + i
            data[at, pl.ds(pl.multiple_of(core * width, width), width), :] = mine_half[i]
            data[at, pl.ds(pl.multiple_of((1 - core) * width, width), width), :] = other_half[i]

    pps, qqs = [], []
    for s in range(slabs):
        both = data[s, 0:width, :]
        with_p = times(both, turned(both[:orbits], 3), 1)
        with_q = times(both, turned(both[orbits:], 3), 1)
        pps.append(with_p[:orbits])
        qqs.append(with_q[orbits:])
        if s > 0:
            up1[s - 1] = -with_q[:orbits]
            dn1[s - 1] = -with_p[orbits:]
    largest = None
    for s in range(slabs):
        base = qqs[s]
        if s + 1 < slabs:
            base = base + pps[s + 1]
        if s == 0:
            base = base + pps[0]
        source = jnp.concatenate([data[s, width : width + orbits, :], data[s, width + orbits : 2 * width, :]], axis=1)
        for e in range(mine):
            settings = settings_ref[(s // per * halves + e // share) * per + s % per, pl.ds(first + e % share, 1), :]
            m = spot[s] * mine + e
            gains[m] = settings
            block = base + jnp.where(diag_lane, settings, 0.0)
            mat[m] = block
            rhs[m] = source
            sums = jnp.sum(jnp.abs(block), axis=0, keepdims=True)
            largest = sums if largest is None else jnp.maximum(largest, sums)
    top = 1.01 * jnp.max(largest + half_roll(largest))
    copy_out(3, 0, slabs - 1)
    copy_out(4, 0, slabs - 1)

    def held(key):
        basic, place = places[key]
        return (up1, dn1, place) if basic else (up2, dn2, place)

    for depth, level in enumerate(levels):
        invert_batch(mat, inv, [spot[node] * mine + e for node, _, _ in level for e in range(mine)], top)
        for node, left, right in level:
            for e in range(mine):
                m = spot[node] * mine + e
                outward, inward = [], []
                if left is not None:
                    ups, downs, place = held((depth, left, node, e))
                    outward.append(downs[place])
                    inward.append(ups[place])
                if right is not None:
                    ups, downs, place = held((depth, node, right, e))
                    outward.append(ups[place])
                    inward.append(downs[place])
                step = times(inv[m], beside(outward + [rhs[m]], 3))
                links_step = [step[:, n * width : (n + 1) * width] for n in range(len(outward))]
                rhs_step = step[:, len(outward) * width :]
                sol[m] = rhs_step
                if left is not None:
                    w1[m] = links_step[0]
                if right is not None:
                    w2[m] = links_step[-1]
                inward = inward[0] if len(inward) == 1 else jnp.concatenate(inward, axis=0)
                change = times(inward, beside(links_step + [rhs_step], 3))
                at_rhs = len(outward) * width
                if left is not None:
                    ml = spot[left] * mine + e
                    mat[ml] = mat[ml] - change[:orbits, :width]
                    rhs[ml] = rhs[ml] - change[:orbits, at_rhs:]
                if right is not None:
                    mr = spot[right] * mine + e
                    mat[mr] = mat[mr] - change[-orbits:, at_rhs - width : at_rhs]
                    rhs[mr] = rhs[mr] - change[-orbits:, at_rhs:]
                if left is not None and right is not None:
                    ups, downs, place = held((depth + 1, left, right, e))
                    ups[place] = -change[:orbits, width : 2 * width]
                    downs[place] = -change[orbits:, :width]
        span = [spot[node] * mine for node, _, _ in level]
        for which in range(3):
            copy_out(which, span[0], span[-1] + mine)
        made = [places[(depth + 1, l, r, e)][1] for _, l, r in level if l is not None and r is not None for e in range(mine)]
        if made:
            copy_out(5, made[0], made[-1] + 1)
            copy_out(6, made[0], made[-1] + 1)
    invert_batch(mat, inv, [spot[root] * mine + e for e in range(mine)], top)
    for e in range(mine):
        m = spot[root] * mine + e
        sol[m] = times(inv[m], turned(rhs[m], 3))
    copy_out(0, spot[root] * mine, (spot[root] + 1) * mine)

    def finished(nodes):
        copy_out(7, spot[nodes[0]] * mine, (spot[nodes[-1]] + 1) * mine)
        for s in nodes:
            for e in range(mine):
                xr, xi = orbitals_of(sol, spot[s] * mine + e, half, halves, orbits)
                power = xr * xr + xi * xi
                for j in range(lines):
                    power_ref[s // per, j, e, s % per, :, :] = power[j * orb_per : (j + 1) * orb_per, :]

    finished([root])
    climb(levels, spot, mine, w1, w2, sol, finished)
    for copy in copies:
        copy.wait()


def lesser_kernel(plan, where_ref, gains, *refs):
    (slabs, mine, orbits, groups, halves, lines, per, orb_per) = plan
    stores, out_ref = refs[:8], refs[8]
    inv, w1, w2, up1, dn1, up2, dn2, ret, rhs, sol, sems = refs[9:]
    held = (inv, w1, w2, up1, dn1, up2, dn2, ret)
    half = where_ref[3]
    width = 2 * orbits
    levels, root = elimination_levels(slabs)
    spot = slots(levels, root)
    places, _ = link_places(slabs, mine, levels)
    fetches = {}

    def fetch(which, depth, low_place, high_place):
        part = pl.ds(low_place, high_place - low_place)
        copy = pltpu.make_async_copy(stores[which].at[part], held[which].at[part], sems.at[len(fetches)])
        copy.start()
        fetches[(which, depth)] = copy

    spans = []
    for level in levels:
        span = [spot[node] * mine for node, _, _ in level]
        spans.append((span[0], span[-1] + mine))
    spans.append((spot[root] * mine, (spot[root] + 1) * mine))
    for depth, span in enumerate(spans):
        fetch(7, depth, *span)
        fetch(0, depth, *span)
        if depth == 0:
            fetch(3, 0, 0, slabs - 1)
            fetch(4, 0, 0, slabs - 1)
        elif depth < len(levels):
            level = levels[depth - 1]
            made = [places[(depth, l, r, e)][1] for _, l, r in level if l is not None and r is not None for e in range(mine)]
            if made:
                fetch(5, depth, made[0], made[-1] + 1)
                fetch(6, depth, made[0], made[-1] + 1)
    for depth in range(len(levels) - 1, -1, -1):
        fetch(1, depth, *spans[depth])
        fetch(2, depth, *spans[depth])
    for depth in range(len(spans)):
        fetches[(7, depth)].wait()
    lane = lax.broadcasted_iota(jnp.int32, (orbits, width), 1)
    sub = lax.broadcasted_iota(jnp.int32, (orbits, width), 0)
    gain_lane = lane == sub + orbits
    for m in range(slabs * mine):
        gain = jnp.sum(jnp.where(gain_lane, gains[m], 0.0), axis=1, keepdims=True)
        rhs[m] = ret[m] * gain
    for depth, level in enumerate(levels):
        for which in (0, 3, 4, 5, 6):
            if (which, depth) in fetches:
                fetches[(which, depth)].wait()
        for node, left, right in level:
            for e in range(mine):
                m = spot[node] * mine + e
                step = times(inv[m], turned(rhs[m], 3))
                sol[m] = step
                sides = []
                if left is not None:
                    basic, place = places[(depth, left, node, e)]
                    sides.append((up1 if basic else up2)[place])
                if right is not None:
                    basic, place = places[(depth, node, right, e)]
                    sides.append((dn1 if basic else dn2)[place])
                change = times(sides[0] if len(sides) == 1 else jnp.concatenate(sides, axis=0), turned(step, 3))
                if left is not None:
                    ml = spot[left] * mine + e
                    rhs[ml] = rhs[ml] - change[:orbits]
                if right is not None:
                    mr = spot[right] * mine + e
                    rhs[mr] = rhs[mr] - change[-orbits:]
    fetches[(0, len(levels))].wait()
    for e in range(mine):
        m = spot[root] * mine + e
        sol[m] = times(inv[m], turned(rhs[m], 3))
    for depth in range(len(levels)):
        fetches[(1, depth)].wait()
        fetches[(2, depth)].wait()
    climb(levels, spot, mine, w1, w2, sol, lambda nodes: None)
    for s in range(slabs):
        for e in range(mine):
            m = spot[s] * mine + e
            xr, xi = orbitals_of(ret, m, half, halves, orbits)
            yr, yi = orbitals_of(sol, m, half, halves, orbits)
            re = xr * yr + xi * yi
            im = xr * yi - xi * yr
            for j in range(lines):
                rows = slice(j * orb_per, (j + 1) * orb_per)
                out_ref[s // per, j, 0, e, s % per, :, :] = re[rows, :]
                out_ref[s // per, j, 1, e, s % per, :, :] = im[rows, :]


def pack_kernel(where_ref, p_ref, q_ref, src_ref, factors_ref, parcel_ref):
    per, _, orbits, _ = p_ref.shape
    width = 2 * orbits
    core = where_ref[2]
    for i in range(per):
        factors_ref[i, 0:orbits, :] = jnp.concatenate([p_ref[i, 0], p_ref[i, 1]], axis=1)
        factors_ref[i, orbits:width, :] = jnp.concatenate([q_ref[i, 0], q_ref[i, 1]], axis=1)

    @pl.when(core == 0)
    def _():
        parcel_ref[...] = factors_ref[...]

    @pl.when(core != 0)
    def _():
        for i in range(per):
            parcel_ref[i, 0:orbits, :] = src_ref[i, 0]
            parcel_ref[i, orbits:width, :] = src_ref[i, 1]


def pack(where, link_p, link_q, sources):
    per, _, orbits, _ = link_p.shape
    shape = jax.ShapeDtypeStruct((per, 2 * orbits, 2 * orbits), F32)
    return pl.pallas_call(
        pack_kernel,
        out_shape=[shape, shape],
        in_specs=[pl.BlockSpec(memory_space=pltpu.SMEM)] + vmem_specs(3),
        out_specs=vmem_specs(2),
        compiler_params=pltpu.CompilerParams(vmem_limit_bytes=VMEM_LIMIT),
        name="pack_parcel",
    )(where, link_p, link_q, sources)


def vmem_specs(count):
    return [pl.BlockSpec(memory_space=pltpu.VMEM)] * count


def solve_retarded(where, pieces, plan, columns):
    (slabs, mine, orbits, groups, halves, lines, per, orb_per) = plan
    width = 2 * orbits
    nodes = slabs * mine
    levels, _ = elimination_levels(slabs)
    _, fills = link_places(slabs, mine, levels)
    kept = [
        (nodes, orbits, width),
        (nodes, orbits, width),
        (nodes, orbits, width),
        (slabs - 1, orbits, width),
        (slabs - 1, orbits, width),
        (fills, orbits, width),
        (fills, orbits, width),
        (nodes, orbits, 2 * columns),
    ]
    shapes = [(groups, lines, mine, per, orb_per, columns), (nodes, 1, width)] + kept
    return pl.pallas_call(
        functools.partial(retarded_kernel, plan),
        out_shape=[jax.ShapeDtypeStruct(shape, F32) for shape in shapes],
        in_specs=[pl.BlockSpec(memory_space=pltpu.SMEM)] + vmem_specs(len(pieces)),
        out_specs=vmem_specs(2) + [pl.BlockSpec(memory_space=pl.ANY)] * len(kept),
        scratch_shapes=[pltpu.VMEM(shape, F32) for shape in kept]
        + [
            pltpu.VMEM((slabs, 2 * width, columns), F32),
            pltpu.VMEM((nodes, orbits, width), F32),
            pltpu.VMEM((nodes, orbits, 2 * columns), F32),
            pltpu.SemaphoreType.DMA((6 * len(levels) + 4,)),
        ],
        compiler_params=pltpu.CompilerParams(vmem_limit_bytes=VMEM_LIMIT),
        name="solve_retarded",
    )(where, *pieces)


def solve_lesser(where, stored, plan):
    (slabs, mine, orbits, groups, halves, lines, per, orb_per) = plan
    levels, _ = elimination_levels(slabs)
    gains, kept = stored[0], stored[1:]
    solved = kept[7].shape
    return pl.pallas_call(
        functools.partial(lesser_kernel, plan),
        out_shape=jax.ShapeDtypeStruct((groups, lines, 2, mine, per, orb_per, solved[-1] // 2), F32),
        in_specs=[pl.BlockSpec(memory_space=pltpu.SMEM)]
        + vmem_specs(1)
        + [pl.BlockSpec(memory_space=pl.ANY)] * len(kept),
        out_specs=pl.BlockSpec(memory_space=pltpu.VMEM),
        scratch_shapes=[pltpu.VMEM(array.shape, F32) for array in kept]
        + [pltpu.VMEM(solved, F32), pltpu.VMEM(solved, F32), pltpu.SemaphoreType.DMA((6 * len(levels) + 4,))],
        compiler_params=pltpu.CompilerParams(vmem_limit_bytes=VMEM_LIMIT),
        name="solve_lesser",
    )(where, gains, *kept)


def correlate_kernel(order, power_ref, got_ref, out_ref):
    count = len(order)
    window = 8
    scale = 1.0 / count
    for start in range(0, count, window):
        span = min(window, count - start)
        acc_re = [None] * span
        acc_im = [None] * span
        reach = count - start
        lead = {}
        for energy in range(reach):
            sender, place = order[energy]
            power = power_ref[sender, place, 0]
            for w in range(span):
                at = energy + start + w
                if at >= count:
                    continue
                if at not in lead:
                    s2, p2 = order[at]
                    lead[at] = (got_ref[s2, 0, p2, 0], got_ref[s2, 1, p2, 0])
                re, im = lead[at]
                acc_re[w] = re * power if acc_re[w] is None else acc_re[w] + re * power
                acc_im[w] = im * power if acc_im[w] is None else acc_im[w] + im * power
        for w in range(span):
            out_ref[0, start + w, 0] = acc_re[w] * scale
            out_ref[1, start + w, 0] = acc_im[w] * scale


def correlate(power, got, order):
    senders, kinds, mine, per, rows, columns = got.shape
    count = len(order)
    return pl.pallas_call(
        functools.partial(correlate_kernel, order),
        grid=(per,),
        out_shape=jax.ShapeDtypeStruct((2, count, per, rows, columns), F32),
        in_specs=[
            pl.BlockSpec((senders, mine, 1, rows, columns), lambda i: (0, 0, i, 0, 0)),
            pl.BlockSpec((senders, kinds, mine, 1, rows, columns), lambda i: (0, 0, 0, i, 0, 0)),
        ],
        out_specs=pl.BlockSpec((2, count, 1, rows, columns), lambda i: (0, 0, i, 0, 0)),
        compiler_params=pltpu.CompilerParams(vmem_limit_bytes=VMEM_LIMIT),
        name="correlate",
    )(power, got)


def per_device(link_p, link_q, shift, lesser_gain, sources):
    per, _, orbits, _ = link_p.shape
    columns = sources.shape[-1]
    local = shift.shape[0]
    groups = lax.axis_size("slab")
    halves = lax.axis_size("half")
    lines = lax.axis_size("line")
    slabs = per * groups
    share = max(1, local // groups)
    mine = halves * share
    owner = lax.axis_index("slab")
    half = lax.axis_index("half")
    core = lax.axis_index("line") & 1
    where = jnp.stack([owner * local // groups, owner, core, half]).astype(jnp.int32)
    settings = jnp.concatenate([jnp.swapaxes(shift, 0, 1), jnp.swapaxes(lesser_gain, 0, 1)], axis=-1)
    settings = lax.all_gather(settings, ("slab", "half"), axis=0, tiled=True)
    factors, parcel = pack(where, link_p, link_q, sources)
    pieces = [factors, sources, settings]
    fetched = [lax.ppermute(parcel, "slab", [(g, g ^ k) for g in range(groups)]) for k in range(1, groups)]
    siblings = [(j, j ^ 1) for j in range(lines)]
    for piece in fetched:
        pieces.append(piece)
        pieces.append(lax.ppermute(piece, "line", siblings))
    plan = (slabs, mine, orbits, groups, halves, lines, per, orbits // (halves * lines))
    power, *stored = solve_retarded(where, pieces, plan, columns)

    def spread(array):
        array = array.reshape((groups * lines,) + array.shape[2:])
        return lax.all_to_all(array, ("slab", "line"), split_axis=0, concat_axis=0, tiled=True)

    power = spread(power)
    got = spread(solve_lesser(where, stored, plan))
    order = []
    for energy in range(halves * lines * local):
        group, row = energy // local, energy % local
        if local >= groups:
            holder, place = row // share, row % share
        else:
            holder, place = -(-row * groups // local), 0
        order.append((holder * lines + group % lines, (group // lines) * share + place))
    return correlate(power, got, tuple(order))


def solution(mesh):
    slab_size, energy_size = mesh.devices.shape
    halves = HALVES if energy_size % (2 * HALVES) == 0 else 1
    split = jax.sharding.Mesh(
        mesh.devices.reshape(slab_size, halves, energy_size // halves), ("slab", "half", "line")
    )
    placed = (
        P("slab", None, None, None),
        P("slab", None, None, None),
        P(("half", "line"), "slab", None),
        P(("half", "line"), "slab", None),
        P("slab", None, None, None),
    )
    return jax.shard_map(
        per_device,
        mesh=split,
        in_specs=placed,
        out_specs=P(None, None, "slab", ("half", "line"), None),
        check_vma=False,
    )
```

```python
import functools

import jax
import jax.numpy as jnp
from jax import lax
from jax.experimental import pallas as pl
from jax.experimental.pallas import tpu as pltpu
from jax.sharding import PartitionSpec as P

F32 = jnp.float32
BF16 = jnp.bfloat16
VMEM_LIMIT = 56 * 1024 * 1024
LEAST = 0.0095
CLOSE = 1e-3
STRIDE = 4
HALVES = 2


def elimination_levels(count):
    levels = []
    chain = list(range(count))
    while len(chain) > 1:
        level = []
        for place in range(0, len(chain), 2):
            left = chain[place - 1] if place > 0 else None
            right = chain[place + 1] if place + 1 < len(chain) else None
            level.append((chain[place], left, right))
        levels.append(level)
        chain = chain[1::2]
    return levels, chain[0]


def split(x, count):
    parts = []
    for place in range(count):
        part = x.astype(BF16)
        parts.append(part)
        if place + 1 < count:
            x = x - part.astype(F32)
    return parts


def half_roll(x):
    return pltpu.roll(x, x.shape[1] // 2, 1)


def turned(block, count):
    half = block.shape[1] // 2
    top = split(block, count)
    if half % 128 == 0:
        bottom = [jnp.concatenate([-part[:, half:], part[:, :half]], axis=1) for part in top]
    else:
        low = lax.broadcasted_iota(jnp.int32, block.shape, 1) < half
        rolled = half_roll(block)
        bottom = split(jnp.where(low, -rolled, rolled), count)
    return [jnp.concatenate([one, two], axis=0) for one, two in zip(top, bottom)]


def wide(x):
    half = x.shape[0] // 2
    return jnp.concatenate([x[:half], x[half:]], axis=1)


def tall(x):
    half = x.shape[1] // 2
    return jnp.concatenate([x[:, :half], x[:, half:]], axis=0)


def above(blocks, count):
    parts = [turned(block, count) for block in blocks]
    if len(parts) == 1:
        return parts[0]
    return [jnp.concatenate([part[k] for part in parts], axis=0) for k in range(count)]


def times(a, right, contract=0):
    left = split(a, len(right))
    if len(right) == 3:
        left = [left[0], left[1], left[0], left[1], left[0], left[2]]
        right = [right[0], right[0], right[1], right[1], right[2], right[0]]
    else:
        left = [left[0], left[1], left[0]]
        right = [right[0], right[0], right[1]]
    return lax.dot_general(
        jnp.concatenate(left, axis=1),
        jnp.concatenate(right, axis=contract),
        (((1,), (contract,)), ((), ())),
        preferred_element_type=F32,
    )


def invert_batch(mat_ref, inv_ref, members, top):
    shape = mat_ref.shape[1:]
    count = shape[0]
    lane = lax.broadcasted_iota(jnp.int32, shape, 1)
    sub = lax.broadcasted_iota(jnp.int32, shape, 0)
    eye = jnp.where(lane == sub, 1.0, 0.0).astype(F32)
    total = top + LEAST

    def factor_of(reach):
        squared = reach * reach
        gain = 2.0 / (2.0 - squared)
        return gain, 0.5 * squared * gain

    def steps(xs, ts, reach, number):
        for step in range(number):
            gain, reach = factor_of(reach)
            bases = [(2.0 * eye - t) * gain for t in ts]
            if step + 1 < number:
                pairs = [times(jnp.concatenate([x, t], axis=0), turned(base, 2)) for x, t, base in zip(xs, ts, bases)]
                xs = [pair[:count] for pair in pairs]
                ts = [pair[count:] for pair in pairs]
            else:
                xs = [times(x, turned(base, 2)) for x, base in zip(xs, bases)]
        for m, x in zip(members, xs):
            inv_ref[m] = x
        return reach

    reach = (top - LEAST) / total
    start = 2.0 / total
    gain, reach = factor_of(reach)
    ts = [mat_ref[m] * start for m in members]
    bases = [(2.0 * eye - t) * gain for t in ts]
    xs = [base * start for base in bases]
    ts = [times(base, turned(t, 2)) for t, base in zip(ts, bases)]
    reach = steps(xs, ts, reach, STRIDE - 1)

    def body(reach):
        xs = [inv_ref[m] for m in members]
        ts = [times(mat_ref[m], turned(x, 2)) for m, x in zip(members, xs)]
        return steps(xs, ts, reach, STRIDE)

    lax.while_loop(lambda reach: reach > CLOSE, body, reach)
    xs = [inv_ref[m] for m in members]
    rests = [eye - times(mat_ref[m], turned(x, 3)) for m, x in zip(members, xs)]
    for m, x, rest in zip(members, xs, rests):
        inv_ref[m] = x + times(x, turned(rest, 2))


def slots(levels, root):
    order = [node for level in levels for node, _, _ in level] + [root]
    return {node: place for place, node in enumerate(order)}


def link_places(slabs, mine, levels):
    places = {}
    for s in range(slabs - 1):
        for e in range(mine):
            places[(0, s, s + 1, e)] = (True, s)
    spare = 0
    for depth, level in enumerate(levels):
        for node, left, right in level:
            if left is not None and right is not None:
                for e in range(mine):
                    places[(depth + 1, left, right, e)] = (False, spare)
                    spare += 1
    return places, spare


def climb(levels, spot, mine, w1, w2, sol, finished):
    for level in reversed(levels):
        for node, left, right in level:
            for e in range(mine):
                m = spot[node] * mine + e
                steps, sides = [], []
                if left is not None:
                    steps.append(w1[m])
                    sides.append(wide(sol[spot[left] * mine + e]))
                if right is not None:
                    steps.append(w2[m])
                    sides.append(wide(sol[spot[right] * mine + e]))
                steps = steps[0] if len(steps) == 1 else jnp.concatenate(steps, axis=1)
                sol[m] = sol[m] - tall(times(steps, above(sides, 2)))
        finished([node for node, _, _ in level])


def orbitals_of(ref, m, half, halves, orbits):
    count = orbits // halves
    found = [ref[m, 0:count, :], ref[m, orbits : orbits + count, :]]
    for h in range(1, halves):
        found = [
            jnp.where(half == h, ref[m, low + h * count : low + (h + 1) * count, :], kept)
            for low, kept in zip((0, orbits), found)
        ]
    return found


def retarded_kernel(plan, where_ref, *refs):
    (slabs, mine, orbits, groups, halves, lines, per, orb_per) = plan
    factors_ref, src_ref = refs[:2]
    own_settings = refs[2 : 2 + halves]
    refs = refs[2 + halves :]
    peers = refs[: 2 * (groups - 1)]
    refs = refs[2 * (groups - 1) :]
    local = own_settings[0].shape[1]
    power_ref, gains, outs = refs[0], refs[1], refs[2:10]
    inv, w1, w2, up1, dn1, up2, dn2, sol, data, mat, rhs, sems = refs[10:]
    stores = (inv, w1, w2, up1, dn1, up2, dn2, sol)
    copies = []

    def copy_out(which, low_place, high_place):
        part = pl.ds(low_place, high_place - low_place)
        copy = pltpu.make_async_copy(stores[which].at[part], outs[which].at[part], sems.at[len(copies)])
        copy.start()
        copies.append(copy)

    width = 2 * orbits
    columns = src_ref.shape[-1]
    share = mine // halves
    levels, root = elimination_levels(slabs)
    spot = slots(levels, root)
    places, _ = link_places(slabs, mine, levels)
    lane = lax.broadcasted_iota(jnp.int32, (orbits, width), 1)
    sub = lax.broadcasted_iota(jnp.int32, (orbits, width), 0)
    diag_lane = lane == sub
    first, owner, core, half = where_ref[0], where_ref[1], where_ref[2], where_ref[3]

    for i in range(per):
        at = owner * per + i
        data[at, 0:width, :] = factors_ref[i]
        data[at, width : width + orbits, :] = src_ref[i, 0]
        data[at, width + orbits : 2 * width, :] = src_ref[i, 1]
        for h in range(halves):
            data[at, 2 * width + h * local : 2 * width + (h + 1) * local, :] = own_settings[h][i]
    for k in range(1, groups):
        mine_half, other_half = peers[2 * (k - 1)], peers[2 * (k - 1) + 1]
        for i in range(per):
            at = (owner ^ k) * per + i
            data[at, pl.ds(pl.multiple_of(core * width, width), width), :] = mine_half[i, 0:width, :]
            data[at, pl.ds(pl.multiple_of((1 - core) * width, width), width), :] = other_half[i, 0:width, :]
            data[at, 2 * width : 2 * width + halves * local, :] = mine_half[i, width : width + halves * local, :]

    pps, qqs = [], []
    for s in range(slabs):
        both = data[s, 0:width, :]
        with_p = times(both, turned(both[:orbits], 3), 1)
        with_q = times(both, turned(both[orbits:], 3), 1)
        pps.append(with_p[:orbits])
        qqs.append(with_q[orbits:])
        if s > 0:
            up1[s - 1] = -with_q[:orbits]
            dn1[s - 1] = -with_p[orbits:]
    largest = None
    for s in range(slabs):
        base = qqs[s]
        if s + 1 < slabs:
            base = base + pps[s + 1]
        if s == 0:
            base = base + pps[0]
        for e in range(mine):
            row = 2 * width + ((e // share) ^ half) * local + first + e % share
            settings = data[s, pl.ds(row, 1), :]
            m = spot[s] * mine + e
            gains[m] = settings
            block = base + jnp.where(diag_lane, settings, 0.0)
            mat[m] = block
            rhs[m] = data[s, width : 2 * width, :]
            sums = jnp.sum(jnp.abs(block), axis=0, keepdims=True)
            largest = sums if largest is None else jnp.maximum(largest, sums)
    top = 1.01 * jnp.max(largest + half_roll(largest))
    copy_out(3, 0, slabs - 1)
    copy_out(4, 0, slabs - 1)

    def held(key):
        basic, place = places[key]
        return (up1, dn1, place) if basic else (up2, dn2, place)

    low = lane < orbits

    def real_rows(z):
        return jnp.concatenate([jnp.where(low, z, -z), half_roll(z)], axis=0)

    def packed(t, right):
        top, bottom = t[:orbits], t[orbits:]
        return jnp.where(low, half_roll(top), bottom) if right else jnp.where(low, top, half_roll(bottom))

    def around(depth, node, left, right, e):
        to_left = to_right = jnp.zeros((orbits, width), F32)
        inward = []
        if left is not None:
            ups, downs, place = held((depth, left, node, e))
            to_left = downs[place]
            inward.append(real_rows(ups[place]))
        if right is not None:
            ups, downs, place = held((depth, node, right, e))
            to_right = ups[place]
            inward.append(real_rows(downs[place]))
        outward = jnp.concatenate(
            [jnp.where(low, to_left, half_roll(to_right)), jnp.where(low, half_roll(to_left), to_right)], axis=0
        )
        return outward, inward[0] if len(inward) == 1 else jnp.concatenate(inward, axis=0)

    def settle(depth, node, left, right, e, step, inward):
        m = spot[node] * mine + e
        links_step, rhs_step = step[:, :width], step[:, width:]
        sol[m] = rhs_step
        change = times(inward, split(step, 3))
        if left is not None:
            w1[m] = packed(links_step, False)
            ml = spot[left] * mine + e
            mat[ml] = mat[ml] - packed(change[:width, :width], False)
            rhs[ml] = rhs[ml] - change[:width, width:]
        if right is not None:
            w2[m] = packed(links_step, True)
            mr = spot[right] * mine + e
            mat[mr] = mat[mr] - packed(change[-width:, :width], True)
            rhs[mr] = rhs[mr] - change[-width:, width:]
        if left is not None and right is not None:
            ups, downs, place = held((depth + 1, left, right, e))
            ups[place] = -packed(change[:width, :width], True)
            downs[place] = -packed(change[width:, :width], False)

    for depth, level in enumerate(levels):
        invert_batch(mat, inv, [spot[node] * mine + e for node, _, _ in level for e in range(mine)], top)
        for node, left, right in level:
            if depth == 0:
                outward, inward = around(depth, node, left, right, 0)
                right_parts = split(jnp.concatenate([outward, rhs[spot[node] * mine]], axis=1), 3)
                inverses = [real_rows(inv[spot[node] * mine + e]) for e in range(mine)]
                step = times(jnp.concatenate(inverses, axis=0), right_parts)
                for e in range(mine):
                    settle(depth, node, left, right, e, step[e * width : (e + 1) * width], inward)
                continue
            for e in range(mine):
                m = spot[node] * mine + e
                outward, inward = around(depth, node, left, right, e)
                step = times(real_rows(inv[m]), split(jnp.concatenate([outward, rhs[m]], axis=1), 3))
                settle(depth, node, left, right, e, step, inward)
        span = [spot[node] * mine for node, _, _ in level]
        for which in range(3):
            copy_out(which, span[0], span[-1] + mine)
        made = [places[(depth + 1, l, r, e)][1] for _, l, r in level if l is not None and r is not None for e in range(mine)]
        if made:
            copy_out(5, made[0], made[-1] + 1)
            copy_out(6, made[0], made[-1] + 1)
    invert_batch(mat, inv, [spot[root] * mine + e for e in range(mine)], top)
    for e in range(mine):
        m = spot[root] * mine + e
        sol[m] = tall(times(inv[m], turned(wide(rhs[m]), 3)))
    copy_out(0, spot[root] * mine, (spot[root] + 1) * mine)

    def finished(nodes):
        copy_out(7, spot[nodes[0]] * mine, (spot[nodes[-1]] + 1) * mine)
        for s in nodes:
            for e in range(mine):
                xr, xi = orbitals_of(sol, spot[s] * mine + e, half, halves, orbits)
                power = xr * xr + xi * xi
                for j in range(lines):
                    power_ref[s // per, j, e, s % per, :, :] = power[j * orb_per : (j + 1) * orb_per, :]

    finished([root])
    climb(levels, spot, mine, w1, w2, sol, finished)
    for copy in copies:
        copy.wait()


def lesser_kernel(plan, where_ref, gains, *refs):
    (slabs, mine, orbits, groups, halves, lines, per, orb_per) = plan
    stores, out_ref = refs[:8], refs[8]
    inv, w1, w2, up1, dn1, up2, dn2, ret, rhs, sol, sems = refs[9:]
    held = (inv, w1, w2, up1, dn1, up2, dn2, ret)
    half = where_ref[3]
    width = 2 * orbits
    levels, root = elimination_levels(slabs)
    spot = slots(levels, root)
    places, _ = link_places(slabs, mine, levels)
    fetches = {}

    def fetch(which, depth, low_place, high_place):
        part = pl.ds(low_place, high_place - low_place)
        copy = pltpu.make_async_copy(stores[which].at[part], held[which].at[part], sems.at[len(fetches)])
        copy.start()
        fetches[(which, depth)] = copy

    spans = []
    for level in levels:
        span = [spot[node] * mine for node, _, _ in level]
        spans.append((span[0], span[-1] + mine))
    spans.append((spot[root] * mine, (spot[root] + 1) * mine))
    for depth, span in enumerate(spans):
        fetch(7, depth, *span)
        fetch(0, depth, *span)
        if depth == 0:
            fetch(3, 0, 0, slabs - 1)
            fetch(4, 0, 0, slabs - 1)
        elif depth < len(levels):
            level = levels[depth - 1]
            made = [places[(depth, l, r, e)][1] for _, l, r in level if l is not None and r is not None for e in range(mine)]
            if made:
                fetch(5, depth, made[0], made[-1] + 1)
                fetch(6, depth, made[0], made[-1] + 1)
    for depth in range(len(levels) - 1, -1, -1):
        fetch(1, depth, *spans[depth])
        fetch(2, depth, *spans[depth])
    for depth in range(len(spans)):
        fetches[(7, depth)].wait()
    lane = lax.broadcasted_iota(jnp.int32, (orbits, width), 1)
    sub = lax.broadcasted_iota(jnp.int32, (orbits, width), 0)
    gain_lane = lane == sub + orbits
    for m in range(slabs * mine):
        gain = jnp.sum(jnp.where(gain_lane, gains[m], 0.0), axis=1, keepdims=True)
        rhs[m] = wide(ret[m]) * gain
    for depth, level in enumerate(levels):
        for which in (0, 3, 4, 5, 6):
            if (which, depth) in fetches:
                fetches[(which, depth)].wait()
        for node, left, right in level:
            for e in range(mine):
                m = spot[node] * mine + e
                step = times(inv[m], turned(rhs[m], 3))
                sol[m] = tall(step)
                sides = []
                if left is not None:
                    basic, place = places[(depth, left, node, e)]
                    sides.append((up1 if basic else up2)[place])
                if right is not None:
                    basic, place = places[(depth, node, right, e)]
                    sides.append((dn1 if basic else dn2)[place])
                change = times(sides[0] if len(sides) == 1 else jnp.concatenate(sides, axis=0), turned(step, 3))
                if left is not None:
                    ml = spot[left] * mine + e
                    rhs[ml] = rhs[ml] - change[:orbits]
                if right is not None:
                    mr = spot[right] * mine + e
                    rhs[mr] = rhs[mr] - change[-orbits:]
    fetches[(0, len(levels))].wait()
    for e in range(mine):
        m = spot[root] * mine + e
        sol[m] = tall(times(inv[m], turned(rhs[m], 3)))
    for depth in range(len(levels)):
        fetches[(1, depth)].wait()
        fetches[(2, depth)].wait()
    climb(levels, spot, mine, w1, w2, sol, lambda nodes: None)
    for s in range(slabs):
        for e in range(mine):
            m = spot[s] * mine + e
            xr, xi = orbitals_of(ret, m, half, halves, orbits)
            yr, yi = orbitals_of(sol, m, half, halves, orbits)
            re = xr * yr + xi * yi
            im = xr * yi - xi * yr
            for j in range(lines):
                rows = slice(j * orb_per, (j + 1) * orb_per)
                out_ref[s // per, j, 0, e, s % per, :, :] = re[rows, :]
                out_ref[s // per, j, 1, e, s % per, :, :] = im[rows, :]


def pack_kernel(where_ref, p_ref, q_ref, src_ref, *refs):
    settings, (factors_ref, parcel_ref) = refs[:-2], refs[-2:]
    per, _, orbits, _ = p_ref.shape
    width = 2 * orbits
    local = settings[0].shape[1]
    core = where_ref[2]
    for i in range(per):
        factors_ref[i, 0:orbits, :] = jnp.concatenate([p_ref[i, 0], p_ref[i, 1]], axis=1)
        factors_ref[i, orbits:width, :] = jnp.concatenate([q_ref[i, 0], q_ref[i, 1]], axis=1)
        for h, setting in enumerate(settings):
            parcel_ref[i, width + h * local : width + (h + 1) * local, :] = setting[i]

    @pl.when(core == 0)
    def _():
        parcel_ref[:, 0:width, :] = factors_ref[...]

    @pl.when(core != 0)
    def _():
        for i in range(per):
            parcel_ref[i, 0:orbits, :] = src_ref[i, 0]
            parcel_ref[i, orbits:width, :] = src_ref[i, 1]


def pack(where, link_p, link_q, sources, settings):
    per, _, orbits, _ = link_p.shape
    width = 2 * orbits
    rows = width + len(settings) * settings[0].shape[1]
    return pl.pallas_call(
        pack_kernel,
        out_shape=[
            jax.ShapeDtypeStruct((per, width, width), F32),
            jax.ShapeDtypeStruct((per, rows, sources.shape[-1]), F32),
        ],
        in_specs=[pl.BlockSpec(memory_space=pltpu.SMEM)] + vmem_specs(3 + len(settings)),
        out_specs=vmem_specs(2),
        compiler_params=pltpu.CompilerParams(vmem_limit_bytes=VMEM_LIMIT),
        name="pack_parcel",
    )(where, link_p, link_q, sources, *settings)


def vmem_specs(count):
    return [pl.BlockSpec(memory_space=pltpu.VMEM)] * count


def solve_retarded(where, pieces, plan, columns):
    (slabs, mine, orbits, groups, halves, lines, per, orb_per) = plan
    width = 2 * orbits
    nodes = slabs * mine
    levels, _ = elimination_levels(slabs)
    _, fills = link_places(slabs, mine, levels)
    kept = [
        (nodes, orbits, width),
        (nodes, orbits, width),
        (nodes, orbits, width),
        (slabs - 1, orbits, width),
        (slabs - 1, orbits, width),
        (fills, orbits, width),
        (fills, orbits, width),
        (nodes, width, columns),
    ]
    shapes = [(groups, lines, mine, per, orb_per, columns), (nodes, 1, width)] + kept
    return pl.pallas_call(
        functools.partial(retarded_kernel, plan),
        out_shape=[jax.ShapeDtypeStruct(shape, F32) for shape in shapes],
        in_specs=[pl.BlockSpec(memory_space=pltpu.SMEM)] + vmem_specs(len(pieces)),
        out_specs=vmem_specs(2) + [pl.BlockSpec(memory_space=pl.ANY)] * len(kept),
        scratch_shapes=[pltpu.VMEM(shape, F32) for shape in kept]
        + [
            pltpu.VMEM((slabs, 2 * width + halves * pieces[2].shape[1], columns), F32),
            pltpu.VMEM((nodes, orbits, width), F32),
            pltpu.VMEM((nodes, width, columns), F32),
            pltpu.SemaphoreType.DMA((6 * len(levels) + 4,)),
        ],
        compiler_params=pltpu.CompilerParams(vmem_limit_bytes=VMEM_LIMIT),
        name="solve_retarded",
    )(where, *pieces)


def solve_lesser(where, stored, plan):
    (slabs, mine, orbits, groups, halves, lines, per, orb_per) = plan
    levels, _ = elimination_levels(slabs)
    gains, kept = stored[0], stored[1:]
    solved = kept[7].shape
    return pl.pallas_call(
        functools.partial(lesser_kernel, plan),
        out_shape=jax.ShapeDtypeStruct((groups, lines, 2, mine, per, orb_per, solved[-1]), F32),
        in_specs=[pl.BlockSpec(memory_space=pltpu.SMEM)]
        + vmem_specs(1)
        + [pl.BlockSpec(memory_space=pl.ANY)] * len(kept),
        out_specs=pl.BlockSpec(memory_space=pltpu.VMEM),
        scratch_shapes=[pltpu.VMEM(array.shape, F32) for array in kept]
        + [pltpu.VMEM((solved[0], solved[1] // 2, 2 * solved[2]), F32), pltpu.VMEM(solved, F32), pltpu.SemaphoreType.DMA((6 * len(levels) + 4,))],
        compiler_params=pltpu.CompilerParams(vmem_limit_bytes=VMEM_LIMIT),
        name="solve_lesser",
    )(where, gains, *kept)


def correlate_kernel(order, power_ref, got_ref, out_ref):
    count = len(order)
    window = 8
    scale = 1.0 / count
    for start in range(0, count, window):
        span = min(window, count - start)
        acc_re = [None] * span
        acc_im = [None] * span
        reach = count - start
        lead = {}
        for energy in range(reach):
            sender, place = order[energy]
            power = power_ref[sender, place, 0]
            for w in range(span):
                at = energy + start + w
                if at >= count:
                    continue
                if at not in lead:
                    s2, p2 = order[at]
                    lead[at] = (got_ref[s2, 0, p2, 0], got_ref[s2, 1, p2, 0])
                re, im = lead[at]
                acc_re[w] = re * power if acc_re[w] is None else acc_re[w] + re * power
                acc_im[w] = im * power if acc_im[w] is None else acc_im[w] + im * power
        for w in range(span):
            out_ref[0, start + w, 0] = acc_re[w] * scale
            out_ref[1, start + w, 0] = acc_im[w] * scale


def correlate(power, got, order):
    senders, kinds, mine, per, rows, columns = got.shape
    count = len(order)
    return pl.pallas_call(
        functools.partial(correlate_kernel, order),
        grid=(per,),
        out_shape=jax.ShapeDtypeStruct((2, count, per, rows, columns), F32),
        in_specs=[
            pl.BlockSpec((senders, mine, 1, rows, columns), lambda i: (0, 0, i, 0, 0)),
            pl.BlockSpec((senders, kinds, mine, 1, rows, columns), lambda i: (0, 0, 0, i, 0, 0)),
        ],
        out_specs=pl.BlockSpec((2, count, 1, rows, columns), lambda i: (0, 0, i, 0, 0)),
        compiler_params=pltpu.CompilerParams(vmem_limit_bytes=VMEM_LIMIT),
        name="correlate",
    )(power, got)


def per_device(link_p, link_q, shift, lesser_gain, sources):
    per, _, orbits, _ = link_p.shape
    columns = sources.shape[-1]
    local = shift.shape[0]
    groups = lax.axis_size("slab")
    halves = lax.axis_size("half")
    lines = lax.axis_size("line")
    slabs = per * groups
    share = max(1, local // groups)
    mine = halves * share
    owner = lax.axis_index("slab")
    half = lax.axis_index("half")
    core = lax.axis_index("line") & 1
    where = jnp.stack([owner * local // groups, owner, core, half]).astype(jnp.int32)
    settings = jnp.concatenate([jnp.swapaxes(shift, 0, 1), jnp.swapaxes(lesser_gain, 0, 1)], axis=-1)
    swaps = [[(a, a ^ h) for a in range(halves)] for h in range(1, halves)]
    settings = [settings] + [lax.ppermute(settings, "half", swap) for swap in swaps]
    factors, parcel = pack(where, link_p, link_q, sources, settings)
    pieces = [factors, sources, *settings]
    fetched = [lax.ppermute(parcel, "slab", [(g, g ^ k) for g in range(groups)]) for k in range(1, groups)]
    siblings = [(j, j ^ 1) for j in range(lines)]
    for piece in fetched:
        pieces.append(piece)
        pieces.append(lax.ppermute(piece, "line", siblings))
    plan = (slabs, mine, orbits, groups, halves, lines, per, orbits // (halves * lines))
    power, *stored = solve_retarded(where, pieces, plan, columns)

    def spread(array):
        array = array.reshape((groups * lines,) + array.shape[2:])
        return lax.all_to_all(array, ("slab", "line"), split_axis=0, concat_axis=0, tiled=True)

    power = spread(power)
    got = spread(solve_lesser(where, stored, plan))
    order = []
    for energy in range(halves * lines * local):
        group, row = energy // local, energy % local
        if local >= groups:
            holder, place = row // share, row % share
        else:
            holder, place = -(-row * groups // local), 0
        order.append((holder * lines + group % lines, (group // lines) * share + place))
    return correlate(power, got, tuple(order))


def solution(mesh):
    slab_size, energy_size = mesh.devices.shape
    halves = HALVES if energy_size % (2 * HALVES) == 0 else 1
    split = jax.sharding.Mesh(
        mesh.devices.reshape(slab_size, halves, energy_size // halves), ("slab", "half", "line")
    )
    placed = (
        P("slab", None, None, None),
        P("slab", None, None, None),
        P(("half", "line"), "slab", None),
        P(("half", "line"), "slab", None),
        P("slab", None, None, None),
    )
    return jax.shard_map(
        per_device,
        mesh=split,
        in_specs=placed,
        out_specs=P(None, None, "slab", ("half", "line"), None),
        check_vma=False,
    )
```

```python
import functools

import jax
import jax.numpy as jnp
from jax import lax
from jax.experimental import pallas as pl
from jax.experimental.pallas import tpu as pltpu
from jax.sharding import PartitionSpec as P

F32 = jnp.float32
BF16 = jnp.bfloat16
VMEM_LIMIT = 56 * 1024 * 1024
LEAST = 0.0095
CLOSE = 1e-3
STRIDE = 4
GROUP = 12
HALVES = 2


def elimination_levels(count):
    levels = []
    chain = list(range(count))
    while len(chain) > 1:
        level = []
        for place in range(0, len(chain), 2):
            left = chain[place - 1] if place > 0 else None
            right = chain[place + 1] if place + 1 < len(chain) else None
            level.append((chain[place], left, right))
        levels.append(level)
        chain = chain[1::2]
    return levels, chain[0]


def split(x, count):
    parts = []
    for place in range(count):
        part = x.astype(BF16)
        parts.append(part)
        if place + 1 < count:
            x = x - part.astype(F32)
    return parts


def half_roll(x):
    return pltpu.roll(x, x.shape[1] // 2, 1)


def turned(block, count):
    half = block.shape[1] // 2
    top = split(block, count)
    if half % 128 == 0:
        bottom = [jnp.concatenate([-part[:, half:], part[:, :half]], axis=1) for part in top]
    else:
        low = lax.broadcasted_iota(jnp.int32, block.shape, 1) < half
        rolled = half_roll(block)
        bottom = split(jnp.where(low, -rolled, rolled), count)
    return [jnp.concatenate([one, two], axis=0) for one, two in zip(top, bottom)]


def wide(x):
    half = x.shape[0] // 2
    return jnp.concatenate([x[:half], x[half:]], axis=1)


def tall(x):
    half = x.shape[1] // 2
    return jnp.concatenate([x[:, :half], x[:, half:]], axis=0)


def above(blocks, count):
    parts = [turned(block, count) for block in blocks]
    if len(parts) == 1:
        return parts[0]
    return [jnp.concatenate([part[k] for part in parts], axis=0) for k in range(count)]


def times(a, right, contract=0):
    left = split(a, len(right))
    if len(right) == 3:
        left = [left[0], left[1], left[0], left[1], left[0], left[2]]
        right = [right[0], right[0], right[1], right[1], right[2], right[0]]
    else:
        left = [left[0], left[1], left[0]]
        right = [right[0], right[0], right[1]]
    return lax.dot_general(
        jnp.concatenate(left, axis=1),
        jnp.concatenate(right, axis=contract),
        (((1,), (contract,)), ((), ())),
        preferred_element_type=F32,
    )


def over_energies(mine, many, work):
    if many and mine > 2 and mine % 2 == 0:

        def two(place, unused):
            work([2 * place, 2 * place + 1])
            return 0

        lax.fori_loop(0, mine // 2, two, 0)
    else:
        work(list(range(mine)))


def invert_batch(mat_ref, inv_ref, near_ref, first, number, top):
    size = next(size for size in range(min(number, GROUP), 0, -1) if number % size == 0)
    if size == number:
        invert_group(mat_ref, inv_ref, near_ref, range(first, first + number), top)
    else:

        def group(place, unused):
            begin = first + place * size
            invert_group(mat_ref, inv_ref, near_ref, [begin + n for n in range(size)], top)
            return 0

        lax.fori_loop(0, number // size, group, 0)


def invert_group(mat_ref, inv_ref, near_ref, members, top):
    shape = mat_ref.shape[1:]
    count = shape[0]
    lane = lax.broadcasted_iota(jnp.int32, shape, 1)
    sub = lax.broadcasted_iota(jnp.int32, shape, 0)
    eye = jnp.where(lane == sub, 1.0, 0.0).astype(F32)
    total = top + LEAST

    def factor_of(reach):
        squared = reach * reach
        gain = 2.0 / (2.0 - squared)
        return gain, 0.5 * squared * gain

    def pair_step(unused, reach):
        gain, after = factor_of(reach)
        ts = [near_ref[m] for m in members]
        both = [jnp.concatenate([inv_ref[m], t], axis=0) for m, t in zip(members, ts)]
        pairs = [times(x, turned((2.0 * eye - t) * gain, 2)) for x, t in zip(both, ts)]
        for m, pair in zip(members, pairs):
            inv_ref[m] = pair[:count]
            near_ref[m] = pair[count:]
        return after

    def cycle(state):
        number, reach = state
        reach = lax.fori_loop(0, number, pair_step, reach)
        gain, after = factor_of(reach)
        xs = [times(inv_ref[m], turned((2.0 * eye - near_ref[m]) * gain, 2)) for m in members]
        for m, x in zip(members, xs):
            inv_ref[m] = x

        @pl.when(after > CLOSE)
        def _():
            ts = [times(mat_ref[m], turned(inv_ref[m], 2)) for m in members]
            for m, t in zip(members, ts):
                near_ref[m] = t

        return jnp.int32(STRIDE - 1), after

    start = 2.0 / total
    gain, reach = factor_of((top - LEAST) / total)
    ts = [mat_ref[m] * start for m in members]
    bases = [(2.0 * eye - t) * gain for t in ts]
    products = [times(t, turned(base, 2)) for t, base in zip(ts, bases)]
    for m, base, product in zip(members, bases, products):
        inv_ref[m] = base * start
        near_ref[m] = product
    lax.while_loop(lambda state: state[1] > CLOSE, cycle, (jnp.int32(STRIDE - 2), reach))
    xs = [inv_ref[m] for m in members]
    rests = [eye - times(mat_ref[m], turned(x, 3)) for m, x in zip(members, xs)]
    for m, x, rest in zip(members, xs, rests):
        inv_ref[m] = x + times(x, turned(rest, 2))


def slots(levels, root):
    order = [node for level in levels for node, _, _ in level] + [root]
    return {node: place for place, node in enumerate(order)}


def link_places(slabs, mine, levels):
    places = {}
    for s in range(slabs - 1):
        for e in range(mine):
            places[(0, s, s + 1, e)] = (True, s)
    spare = 0
    for depth, level in enumerate(levels):
        for node, left, right in level:
            if left is not None and right is not None:
                for e in range(mine):
                    places[(depth + 1, left, right, e)] = (False, spare)
                    spare += 1
    return places, spare


def climb(levels, spot, mine, w1, w2, sol, finished):
    for level in reversed(levels):

        def work(energies, level=level):
            values = []
            for node, left, right in level:
                for e in energies:
                    m = spot[node] * mine + e
                    steps, sides = [], []
                    if left is not None:
                        steps.append(w1[m])
                        sides.append(wide(sol[spot[left] * mine + e]))
                    if right is not None:
                        steps.append(w2[m])
                        sides.append(wide(sol[spot[right] * mine + e]))
                    steps = steps[0] if len(steps) == 1 else jnp.concatenate(steps, axis=1)
                    values.append((m, sol[m] - tall(times(steps, above(sides, 2)))))
            for m, value in values:
                sol[m] = value

        over_energies(mine, len(level) > 2, work)
        finished([node for node, _, _ in level])


def orbitals_of(ref, m, half, halves, orbits):
    count = orbits // halves
    found = [ref[m, 0:count, :], ref[m, orbits : orbits + count, :]]
    for h in range(1, halves):
        found = [
            jnp.where(half == h, ref[m, low + h * count : low + (h + 1) * count, :], kept)
            for low, kept in zip((0, orbits), found)
        ]
    return found


def retarded_kernel(plan, where_ref, *refs):
    (slabs, mine, orbits, groups, halves, lines, per, orb_per) = plan
    factors_ref, src_ref = refs[:2]
    own_settings = refs[2 : 2 + halves]
    refs = refs[2 + halves :]
    peers = refs[: 2 * (groups - 1)]
    refs = refs[2 * (groups - 1) :]
    local = own_settings[0].shape[1]
    power_ref, gains, outs = refs[0], refs[1], refs[2:10]
    inv, w1, w2, up1, dn1, up2, dn2, sol, data, mat, rhs, near, sems = refs[10:]
    stores = (inv, w1, w2, up1, dn1, up2, dn2, sol)
    copies = []

    def copy_out(which, low_place, high_place):
        part = pl.ds(low_place, high_place - low_place)
        copy = pltpu.make_async_copy(stores[which].at[part], outs[which].at[part], sems.at[len(copies)])
        copy.start()
        copies.append(copy)

    width = 2 * orbits
    columns = src_ref.shape[-1]
    share = mine // halves
    levels, root = elimination_levels(slabs)
    spot = slots(levels, root)
    places, _ = link_places(slabs, mine, levels)
    lane = lax.broadcasted_iota(jnp.int32, (orbits, width), 1)
    sub = lax.broadcasted_iota(jnp.int32, (orbits, width), 0)
    diag_lane = lane == sub
    first, owner, core, half = where_ref[0], where_ref[1], where_ref[2], where_ref[3]

    for i in range(per):
        at = owner * per + i
        data[at, 0:width, :] = factors_ref[i]
        data[at, width : width + orbits, :] = src_ref[i, 0]
        data[at, width + orbits : 2 * width, :] = src_ref[i, 1]
        for h in range(halves):
            data[at, 2 * width + h * local : 2 * width + (h + 1) * local, :] = own_settings[h][i]
    for k in range(1, groups):
        mine_half, other_half = peers[2 * (k - 1)], peers[2 * (k - 1) + 1]
        for i in range(per):
            at = (owner ^ k) * per + i
            data[at, pl.ds(pl.multiple_of(core * width, width), width), :] = mine_half[i, 0:width, :]
            data[at, pl.ds(pl.multiple_of((1 - core) * width, width), width), :] = other_half[i, 0:width, :]
            data[at, 2 * width : 2 * width + halves * local, :] = mine_half[i, width : width + halves * local, :]

    pps, qqs = [], []
    for s in range(slabs):
        both = data[s, 0:width, :]
        with_p = times(both, turned(both[:orbits], 3), 1)
        with_q = times(both, turned(both[orbits:], 3), 1)
        pps.append(with_p[:orbits])
        qqs.append(with_q[orbits:])
        if s > 0:
            up1[s - 1] = -with_q[:orbits]
            dn1[s - 1] = -with_p[orbits:]
    largest = None
    for s in range(slabs):
        base = qqs[s]
        if s + 1 < slabs:
            base = base + pps[s + 1]
        if s == 0:
            base = base + pps[0]
        for e in range(mine):
            row = 2 * width + ((e // share) ^ half) * local + first + e % share
            settings = data[s, pl.ds(row, 1), :]
            m = spot[s] * mine + e
            gains[m] = settings
            block = base + jnp.where(diag_lane, settings, 0.0)
            mat[m] = block
            rhs[m] = data[s, width : 2 * width, :]
            sums = jnp.sum(jnp.abs(block), axis=0, keepdims=True)
            largest = sums if largest is None else jnp.maximum(largest, sums)
    top = 1.01 * jnp.max(largest + half_roll(largest))
    copy_out(3, 0, slabs - 1)
    copy_out(4, 0, slabs - 1)

    def held(key):
        basic, place = places[key]
        return (up1, dn1, place) if basic else (up2, dn2, place)

    low = lane < orbits

    def real_rows(z):
        return jnp.concatenate([jnp.where(low, z, -z), half_roll(z)], axis=0)

    def packed(t, right):
        top, bottom = t[:orbits], t[orbits:]
        return jnp.where(low, half_roll(top), bottom) if right else jnp.where(low, top, half_roll(bottom))

    def around(depth, node, left, right, e):
        to_left = to_right = jnp.zeros((orbits, width), F32)
        inward = []
        if left is not None:
            ups, downs, place = held((depth, left, node, e))
            to_left = downs[place]
            inward.append(real_rows(ups[place]))
        if right is not None:
            ups, downs, place = held((depth, node, right, e))
            to_right = ups[place]
            inward.append(real_rows(downs[place]))
        outward = jnp.concatenate(
            [jnp.where(low, to_left, half_roll(to_right)), jnp.where(low, half_roll(to_left), to_right)], axis=0
        )
        return outward, inward[0] if len(inward) == 1 else jnp.concatenate(inward, axis=0)

    def settle(depth, node, left, right, e, step, inward):
        m = spot[node] * mine + e
        links_step, rhs_step = step[:, :width], step[:, width:]
        sol[m] = rhs_step
        change = times(inward, split(step, 3))
        if left is not None:
            w1[m] = packed(links_step, False)
            ml = spot[left] * mine + e
            mat[ml] = mat[ml] - packed(change[:width, :width], False)
            rhs[ml] = rhs[ml] - change[:width, width:]
        if right is not None:
            w2[m] = packed(links_step, True)
            mr = spot[right] * mine + e
            mat[mr] = mat[mr] - packed(change[-width:, :width], True)
            rhs[mr] = rhs[mr] - change[-width:, width:]
        if left is not None and right is not None:
            ups, downs, place = held((depth + 1, left, right, e))
            ups[place] = -packed(change[:width, :width], True)
            downs[place] = -packed(change[width:, :width], False)

    for depth, level in enumerate(levels):
        invert_batch(mat, inv, near, spot[level[0][0]] * mine, len(level) * mine, top)
        for node, left, right in level:
            if depth == 0:
                outward, inward = around(depth, node, left, right, 0)
                right_parts = split(jnp.concatenate([outward, rhs[spot[node] * mine]], axis=1), 3)
                inverses = [real_rows(inv[spot[node] * mine + e]) for e in range(mine)]
                step = times(jnp.concatenate(inverses, axis=0), right_parts)
                for e in range(mine):
                    settle(depth, node, left, right, e, step[e * width : (e + 1) * width], inward)
                continue
            for e in range(mine):
                m = spot[node] * mine + e
                outward, inward = around(depth, node, left, right, e)
                step = times(real_rows(inv[m]), split(jnp.concatenate([outward, rhs[m]], axis=1), 3))
                settle(depth, node, left, right, e, step, inward)
        span = [spot[node] * mine for node, _, _ in level]
        for which in range(3):
            copy_out(which, span[0], span[-1] + mine)
        made = [places[(depth + 1, l, r, e)][1] for _, l, r in level if l is not None and r is not None for e in range(mine)]
        if made:
            copy_out(5, made[0], made[-1] + 1)
            copy_out(6, made[0], made[-1] + 1)
    invert_batch(mat, inv, near, spot[root] * mine, mine, top)
    for e in range(mine):
        m = spot[root] * mine + e
        sol[m] = tall(times(inv[m], turned(wide(rhs[m]), 3)))
    copy_out(0, spot[root] * mine, (spot[root] + 1) * mine)

    def finished(nodes):
        copy_out(7, spot[nodes[0]] * mine, (spot[nodes[-1]] + 1) * mine)
        for s in nodes:
            for e in range(mine):
                xr, xi = orbitals_of(sol, spot[s] * mine + e, half, halves, orbits)
                power = xr * xr + xi * xi
                for j in range(lines):
                    power_ref[s // per, j, e, s % per, :, :] = power[j * orb_per : (j + 1) * orb_per, :]

    finished([root])
    climb(levels, spot, mine, w1, w2, sol, finished)
    for copy in copies:
        copy.wait()


def lesser_kernel(plan, where_ref, gains, *refs):
    (slabs, mine, orbits, groups, halves, lines, per, orb_per) = plan
    stores, out_ref = refs[:8], refs[8]
    inv, w1, w2, up1, dn1, up2, dn2, ret, rhs, sol, sems = refs[9:]
    held = (inv, w1, w2, up1, dn1, up2, dn2, ret)
    half = where_ref[3]
    width = 2 * orbits
    levels, root = elimination_levels(slabs)
    spot = slots(levels, root)
    places, _ = link_places(slabs, mine, levels)
    fetches = {}

    def fetch(which, depth, low_place, high_place):
        part = pl.ds(low_place, high_place - low_place)
        copy = pltpu.make_async_copy(stores[which].at[part], held[which].at[part], sems.at[len(fetches)])
        copy.start()
        fetches[(which, depth)] = copy

    spans = []
    for level in levels:
        span = [spot[node] * mine for node, _, _ in level]
        spans.append((span[0], span[-1] + mine))
    spans.append((spot[root] * mine, (spot[root] + 1) * mine))
    for depth, span in enumerate(spans):
        fetch(7, depth, *span)
        fetch(0, depth, *span)
        if depth == 0:
            fetch(3, 0, 0, slabs - 1)
            fetch(4, 0, 0, slabs - 1)
        elif depth < len(levels):
            level = levels[depth - 1]
            made = [places[(depth, l, r, e)][1] for _, l, r in level if l is not None and r is not None for e in range(mine)]
            if made:
                fetch(5, depth, made[0], made[-1] + 1)
                fetch(6, depth, made[0], made[-1] + 1)
    for depth in range(len(levels) - 1, -1, -1):
        fetch(1, depth, *spans[depth])
        fetch(2, depth, *spans[depth])
    for depth in range(len(spans)):
        fetches[(7, depth)].wait()
    lane = lax.broadcasted_iota(jnp.int32, (orbits, width), 1)
    sub = lax.broadcasted_iota(jnp.int32, (orbits, width), 0)
    gain_lane = lane == sub + orbits
    for m in range(slabs * mine):
        gain = jnp.sum(jnp.where(gain_lane, gains[m], 0.0), axis=1, keepdims=True)
        rhs[m] = wide(ret[m]) * gain
    for depth, level in enumerate(levels):
        for which in (0, 3, 4, 5, 6):
            if (which, depth) in fetches:
                fetches[(which, depth)].wait()

        def work(energies, depth=depth, level=level):
            items = [(node, left, right, e) for node, left, right in level for e in energies]
            steps = [times(inv[spot[node] * mine + e], turned(rhs[spot[node] * mine + e], 3)) for node, _, _, e in items]
            changes = []
            for (node, left, right, e), step in zip(items, steps):
                sides = []
                if left is not None:
                    basic, place = places[(depth, left, node, 0)]
                    sides.append(up1[place] if basic else up2[place + e])
                if right is not None:
                    basic, place = places[(depth, node, right, 0)]
                    sides.append(dn1[place] if basic else dn2[place + e])
                sides = sides[0] if len(sides) == 1 else jnp.concatenate(sides, axis=0)
                changes.append(times(sides, turned(step, 3)))
            for (node, left, right, e), step, change in zip(items, steps, changes):
                sol[spot[node] * mine + e] = tall(step)
                if left is not None:
                    ml = spot[left] * mine + e
                    rhs[ml] = rhs[ml] - change[:orbits]
                if right is not None:
                    mr = spot[right] * mine + e
                    rhs[mr] = rhs[mr] - change[-orbits:]

        over_energies(mine, len(level) > 2, work)
    fetches[(0, len(levels))].wait()
    for e in range(mine):
        m = spot[root] * mine + e
        sol[m] = tall(times(inv[m], turned(rhs[m], 3)))
    for depth in range(len(levels)):
        fetches[(1, depth)].wait()
        fetches[(2, depth)].wait()
    climb(levels, spot, mine, w1, w2, sol, lambda nodes: None)
    for s in range(slabs):
        for e in range(mine):
            m = spot[s] * mine + e
            xr, xi = orbitals_of(ret, m, half, halves, orbits)
            yr, yi = orbitals_of(sol, m, half, halves, orbits)
            re = xr * yr + xi * yi
            im = xr * yi - xi * yr
            for j in range(lines):
                rows = slice(j * orb_per, (j + 1) * orb_per)
                out_ref[s // per, j, 0, e, s % per, :, :] = re[rows, :]
                out_ref[s // per, j, 1, e, s % per, :, :] = im[rows, :]


def pack_kernel(where_ref, p_ref, q_ref, src_ref, *refs):
    settings, (factors_ref, parcel_ref) = refs[:-2], refs[-2:]
    per, _, orbits, _ = p_ref.shape
    width = 2 * orbits
    local = settings[0].shape[1]
    core = where_ref[2]
    for i in range(per):
        factors_ref[i, 0:orbits, :] = jnp.concatenate([p_ref[i, 0], p_ref[i, 1]], axis=1)
        factors_ref[i, orbits:width, :] = jnp.concatenate([q_ref[i, 0], q_ref[i, 1]], axis=1)
        for h, setting in enumerate(settings):
            parcel_ref[i, width + h * local : width + (h + 1) * local, :] = setting[i]

    @pl.when(core == 0)
    def _():
        parcel_ref[:, 0:width, :] = factors_ref[...]

    @pl.when(core != 0)
    def _():
        for i in range(per):
            parcel_ref[i, 0:orbits, :] = src_ref[i, 0]
            parcel_ref[i, orbits:width, :] = src_ref[i, 1]


def pack(where, link_p, link_q, sources, settings):
    per, _, orbits, _ = link_p.shape
    width = 2 * orbits
    rows = width + len(settings) * settings[0].shape[1]
    return pl.pallas_call(
        pack_kernel,
        out_shape=[
            jax.ShapeDtypeStruct((per, width, width), F32),
            jax.ShapeDtypeStruct((per, rows, sources.shape[-1]), F32),
        ],
        in_specs=[pl.BlockSpec(memory_space=pltpu.SMEM)] + vmem_specs(3 + len(settings)),
        out_specs=vmem_specs(2),
        compiler_params=pltpu.CompilerParams(vmem_limit_bytes=VMEM_LIMIT),
        name="pack_parcel",
    )(where, link_p, link_q, sources, *settings)


def vmem_specs(count):
    return [pl.BlockSpec(memory_space=pltpu.VMEM)] * count


def solve_retarded(where, pieces, plan, columns):
    (slabs, mine, orbits, groups, halves, lines, per, orb_per) = plan
    width = 2 * orbits
    nodes = slabs * mine
    levels, _ = elimination_levels(slabs)
    _, fills = link_places(slabs, mine, levels)
    kept = [
        (nodes, orbits, width),
        (nodes, orbits, width),
        (nodes, orbits, width),
        (slabs - 1, orbits, width),
        (slabs - 1, orbits, width),
        (fills, orbits, width),
        (fills, orbits, width),
        (nodes, width, columns),
    ]
    shapes = [(groups, lines, mine, per, orb_per, columns), (nodes, 1, width)] + kept
    return pl.pallas_call(
        functools.partial(retarded_kernel, plan),
        out_shape=[jax.ShapeDtypeStruct(shape, F32) for shape in shapes],
        in_specs=[pl.BlockSpec(memory_space=pltpu.SMEM)] + vmem_specs(len(pieces)),
        out_specs=vmem_specs(2) + [pl.BlockSpec(memory_space=pl.ANY)] * len(kept),
        scratch_shapes=[pltpu.VMEM(shape, F32) for shape in kept]
        + [
            pltpu.VMEM((slabs, 2 * width + halves * pieces[2].shape[1], columns), F32),
            pltpu.VMEM((nodes, orbits, width), F32),
            pltpu.VMEM((nodes, width, columns), F32),
            pltpu.VMEM((nodes, orbits, width), F32),
            pltpu.SemaphoreType.DMA((6 * len(levels) + 4,)),
        ],
        compiler_params=pltpu.CompilerParams(vmem_limit_bytes=VMEM_LIMIT),
        name="solve_retarded",
    )(where, *pieces)


def solve_lesser(where, stored, plan):
    (slabs, mine, orbits, groups, halves, lines, per, orb_per) = plan
    levels, _ = elimination_levels(slabs)
    gains, kept = stored[0], stored[1:]
    solved = kept[7].shape
    return pl.pallas_call(
        functools.partial(lesser_kernel, plan),
        out_shape=jax.ShapeDtypeStruct((groups, lines, 2, mine, per, orb_per, solved[-1]), F32),
        in_specs=[pl.BlockSpec(memory_space=pltpu.SMEM)]
        + vmem_specs(1)
        + [pl.BlockSpec(memory_space=pl.ANY)] * len(kept),
        out_specs=pl.BlockSpec(memory_space=pltpu.VMEM),
        scratch_shapes=[pltpu.VMEM(array.shape, F32) for array in kept]
        + [pltpu.VMEM((solved[0], solved[1] // 2, 2 * solved[2]), F32), pltpu.VMEM(solved, F32), pltpu.SemaphoreType.DMA((6 * len(levels) + 4,))],
        compiler_params=pltpu.CompilerParams(vmem_limit_bytes=VMEM_LIMIT),
        name="solve_lesser",
    )(where, gains, *kept)


def correlate_kernel(order, power_ref, got_ref, out_ref):
    count = len(order)
    window = 8
    scale = 1.0 / count
    for start in range(0, count, window):
        span = min(window, count - start)
        acc_re = [None] * span
        acc_im = [None] * span
        reach = count - start
        lead = {}
        for energy in range(reach):
            sender, place = order[energy]
            power = power_ref[sender, place, 0]
            for w in range(span):
                at = energy + start + w
                if at >= count:
                    continue
                if at not in lead:
                    s2, p2 = order[at]
                    lead[at] = (got_ref[s2, 0, p2, 0], got_ref[s2, 1, p2, 0])
                re, im = lead[at]
                acc_re[w] = re * power if acc_re[w] is None else acc_re[w] + re * power
                acc_im[w] = im * power if acc_im[w] is None else acc_im[w] + im * power
        for w in range(span):
            out_ref[0, start + w, 0] = acc_re[w] * scale
            out_ref[1, start + w, 0] = acc_im[w] * scale


def correlate(power, got, order):
    senders, kinds, mine, per, rows, columns = got.shape
    count = len(order)
    return pl.pallas_call(
        functools.partial(correlate_kernel, order),
        grid=(per,),
        out_shape=jax.ShapeDtypeStruct((2, count, per, rows, columns), F32),
        in_specs=[
            pl.BlockSpec((senders, mine, 1, rows, columns), lambda i: (0, 0, i, 0, 0)),
            pl.BlockSpec((senders, kinds, mine, 1, rows, columns), lambda i: (0, 0, 0, i, 0, 0)),
        ],
        out_specs=pl.BlockSpec((2, count, 1, rows, columns), lambda i: (0, 0, i, 0, 0)),
        compiler_params=pltpu.CompilerParams(vmem_limit_bytes=VMEM_LIMIT),
        name="correlate",
    )(power, got)


def per_device(link_p, link_q, shift, lesser_gain, sources):
    per, _, orbits, _ = link_p.shape
    columns = sources.shape[-1]
    local = shift.shape[0]
    groups = lax.axis_size("slab")
    halves = lax.axis_size("half")
    lines = lax.axis_size("line")
    slabs = per * groups
    share = max(1, local // groups)
    mine = halves * share
    owner = lax.axis_index("slab")
    half = lax.axis_index("half")
    core = lax.axis_index("line") & 1
    where = jnp.stack([owner * local // groups, owner, core, half]).astype(jnp.int32)
    settings = jnp.concatenate([jnp.swapaxes(shift, 0, 1), jnp.swapaxes(lesser_gain, 0, 1)], axis=-1)
    swaps = [[(a, a ^ h) for a in range(halves)] for h in range(1, halves)]
    settings = [settings] + [lax.ppermute(settings, "half", swap) for swap in swaps]
    factors, parcel = pack(where, link_p, link_q, sources, settings)
    pieces = [factors, sources, *settings]
    fetched = [lax.ppermute(parcel, "slab", [(g, g ^ k) for g in range(groups)]) for k in range(1, groups)]
    siblings = [(j, j ^ 1) for j in range(lines)]
    for piece in fetched:
        pieces.append(piece)
        pieces.append(lax.ppermute(piece, "line", siblings))
    plan = (slabs, mine, orbits, groups, halves, lines, per, orbits // (halves * lines))
    power, *stored = solve_retarded(where, pieces, plan, columns)

    def spread(array):
        array = array.reshape((groups * lines,) + array.shape[2:])
        return lax.all_to_all(array, ("slab", "line"), split_axis=0, concat_axis=0, tiled=True)

    power = spread(power)
    got = spread(solve_lesser(where, stored, plan))
    order = []
    for energy in range(halves * lines * local):
        group, row = energy // local, energy % local
        if local >= groups:
            holder, place = row // share, row % share
        else:
            holder, place = -(-row * groups // local), 0
        order.append((holder * lines + group % lines, (group // lines) * share + place))
    return correlate(power, got, tuple(order))


def solution(mesh):
    slab_size, energy_size = mesh.devices.shape
    halves = HALVES if energy_size % (2 * HALVES) == 0 else 1
    split = jax.sharding.Mesh(
        mesh.devices.reshape(slab_size, halves, energy_size // halves), ("slab", "half", "line")
    )
    placed = (
        P("slab", None, None, None),
        P("slab", None, None, None),
        P(("half", "line"), "slab", None),
        P(("half", "line"), "slab", None),
        P("slab", None, None, None),
    )
    return jax.shard_map(
        per_device,
        mesh=split,
        in_specs=placed,
        out_specs=P(None, None, "slab", ("half", "line"), None),
        check_vma=False,
    )
```

```python
import functools

import jax
import jax.numpy as jnp
from jax import lax
from jax.experimental import pallas as pl
from jax.experimental.pallas import tpu as pltpu
from jax.sharding import PartitionSpec as P

F32 = jnp.float32
BF16 = jnp.bfloat16
VMEM_LIMIT = 56 * 1024 * 1024
LEAST = 0.0095
CLOSE = 1e-3
STRIDE = 4
GROUP = 8
HALVES = 2


def elimination_levels(count):
    levels = []
    chain = list(range(count))
    while len(chain) > 1:
        level = []
        for place in range(0, len(chain), 2):
            left = chain[place - 1] if place > 0 else None
            right = chain[place + 1] if place + 1 < len(chain) else None
            level.append((chain[place], left, right))
        levels.append(level)
        chain = chain[1::2]
    return levels, chain[0]


def split(x, count):
    parts = []
    for place in range(count):
        part = x.astype(BF16)
        parts.append(part)
        if place + 1 < count:
            x = x - part.astype(F32)
    return parts


def half_roll(x):
    return pltpu.roll(x, x.shape[1] // 2, 1)


def turned(block, count):
    half = block.shape[1] // 2
    top = split(block, count)
    if half % 128 == 0:
        bottom = [jnp.concatenate([-part[:, half:], part[:, :half]], axis=1) for part in top]
    else:
        low = lax.broadcasted_iota(jnp.int32, block.shape, 1) < half
        rolled = half_roll(block)
        bottom = split(jnp.where(low, -rolled, rolled), count)
    return [jnp.concatenate([one, two], axis=0) for one, two in zip(top, bottom)]


def wide(x):
    half = x.shape[0] // 2
    return jnp.concatenate([x[:half], x[half:]], axis=1)


def tall(x):
    half = x.shape[1] // 2
    return jnp.concatenate([x[:, :half], x[:, half:]], axis=0)


def above(blocks, count):
    parts = [turned(block, count) for block in blocks]
    if len(parts) == 1:
        return parts[0]
    return [jnp.concatenate([part[k] for part in parts], axis=0) for k in range(count)]


def times(a, right, contract=0):
    left = split(a, len(right))
    if len(right) == 3:
        left = [left[0], left[1], left[0], left[1], left[0], left[2]]
        right = [right[0], right[0], right[1], right[1], right[2], right[0]]
    else:
        left = [left[0], left[1], left[0]]
        right = [right[0], right[0], right[1]]
    return lax.dot_general(
        jnp.concatenate(left, axis=1),
        jnp.concatenate(right, axis=contract),
        (((1,), (contract,)), ((), ())),
        preferred_element_type=F32,
    )


def over_energies(mine, many, work):
    if many and mine > 2 and mine % 2 == 0:

        def two(place, unused):
            work([2 * place, 2 * place + 1])
            return 0

        lax.fori_loop(0, mine // 2, two, 0)
    else:
        work(list(range(mine)))


def invert_batch(mat_ref, inv_ref, first, number, top):
    size = next(size for size in range(min(number, GROUP), 0, -1) if number % size == 0)
    if size == number:
        invert_group(mat_ref, inv_ref, range(first, first + number), top)
    else:

        def group(place, unused):
            begin = first + place * size
            invert_group(mat_ref, inv_ref, [begin + n for n in range(size)], top)
            return 0

        lax.fori_loop(0, number // size, group, 0)


def invert_group(mat_ref, inv_ref, members, top):
    shape = mat_ref.shape[1:]
    count = shape[0]
    lane = lax.broadcasted_iota(jnp.int32, shape, 1)
    sub = lax.broadcasted_iota(jnp.int32, shape, 0)
    eye = jnp.where(lane == sub, 1.0, 0.0).astype(F32)
    total = top + LEAST

    def factor_of(reach):
        squared = reach * reach
        gain = 2.0 / (2.0 - squared)
        return gain, 0.5 * squared * gain

    def steps(xs, ts, reach, number):
        for step in range(number):
            gain, reach = factor_of(reach)
            bases = [(2.0 * eye - t) * gain for t in ts]
            if step + 1 < number:
                pairs = [times(jnp.concatenate([x, t], axis=0), turned(base, 2)) for x, t, base in zip(xs, ts, bases)]
                xs = [pair[:count] for pair in pairs]
                ts = [pair[count:] for pair in pairs]
            else:
                xs = [times(x, turned(base, 2)) for x, base in zip(xs, bases)]
        for m, x in zip(members, xs):
            inv_ref[m] = x
        return reach

    start = 2.0 / total
    gain, reach = factor_of((top - LEAST) / total)
    ts = [mat_ref[m] * start for m in members]
    bases = [(2.0 * eye - t) * gain for t in ts]
    xs = [base * start for base in bases]
    ts = [times(t, turned(base, 2)) for t, base in zip(ts, bases)]
    reach = steps(xs, ts, reach, STRIDE - 1)

    def cycle(reach):
        xs = [inv_ref[m] for m in members]
        ts = [times(mat_ref[m], turned(x, 2)) for m, x in zip(members, xs)]
        return steps(xs, ts, reach, STRIDE)

    lax.while_loop(lambda reach: reach > CLOSE, cycle, reach)
    xs = [inv_ref[m] for m in members]
    rests = [eye - times(mat_ref[m], turned(x, 3)) for m, x in zip(members, xs)]
    for m, x, rest in zip(members, xs, rests):
        inv_ref[m] = x + times(x, turned(rest, 2))


def slots(levels, root):
    order = [node for level in levels for node, _, _ in level] + [root]
    return {node: place for place, node in enumerate(order)}


def link_places(slabs, mine, levels):
    places = {}
    for s in range(slabs - 1):
        for e in range(mine):
            places[(0, s, s + 1, e)] = (True, s)
    spare = 0
    for depth, level in enumerate(levels):
        for node, left, right in level:
            if left is not None and right is not None:
                for e in range(mine):
                    places[(depth + 1, left, right, e)] = (False, spare)
                    spare += 1
    return places, spare


def climb(levels, spot, mine, w1, w2, sol, finished):
    for level in reversed(levels):

        def work(energies, level=level):
            values = []
            for node, left, right in level:
                for e in energies:
                    m = spot[node] * mine + e
                    steps, sides = [], []
                    if left is not None:
                        steps.append(w1[m])
                        sides.append(wide(sol[spot[left] * mine + e]))
                    if right is not None:
                        steps.append(w2[m])
                        sides.append(wide(sol[spot[right] * mine + e]))
                    steps = steps[0] if len(steps) == 1 else jnp.concatenate(steps, axis=1)
                    values.append((m, sol[m] - tall(times(steps, above(sides, 2)))))
            for m, value in values:
                sol[m] = value

        over_energies(mine, len(level) > 2, work)
        finished([node for node, _, _ in level])


def orbitals_of(ref, m, half, halves, orbits):
    count = orbits // halves
    found = [ref[m, 0:count, :], ref[m, orbits : orbits + count, :]]
    for h in range(1, halves):
        found = [
            jnp.where(half == h, ref[m, low + h * count : low + (h + 1) * count, :], kept)
            for low, kept in zip((0, orbits), found)
        ]
    return found


def retarded_kernel(plan, where_ref, *refs):
    (slabs, mine, orbits, groups, halves, lines, per, orb_per) = plan
    factors_ref, src_ref, settings_ref = refs[:3]
    peers = refs[3 : 3 + 2 * (groups - 1)]
    refs = refs[3 + 2 * (groups - 1) :]
    others, refs = refs[: halves - 1], refs[halves - 1 :]
    local = settings_ref.shape[1]
    power_ref, gains, outs = refs[0], refs[1], refs[2:10]
    inv, w1, w2, up1, dn1, up2, dn2, sol, data, mat, rhs, hold, sems = refs[10:]
    stores = (inv, w1, w2, up1, dn1, up2, dn2, sol)
    copies = []

    def copy_out(which, low_place, high_place):
        part = pl.ds(low_place, high_place - low_place)
        copy = pltpu.make_async_copy(stores[which].at[part], outs[which].at[part], sems.at[len(copies)])
        copy.start()
        copies.append(copy)

    width = 2 * orbits
    columns = src_ref.shape[-1]
    share = mine // halves
    levels, root = elimination_levels(slabs)
    spot = slots(levels, root)
    places, _ = link_places(slabs, mine, levels)
    lane = lax.broadcasted_iota(jnp.int32, (orbits, width), 1)
    sub = lax.broadcasted_iota(jnp.int32, (orbits, width), 0)
    diag_lane = lane == sub
    first, owner, core, half = where_ref[0], where_ref[1], where_ref[2], where_ref[3]

    for i in range(per):
        at = owner * per + i
        data[at, 0:width, :] = factors_ref[i]
        data[at, width : width + orbits, :] = src_ref[i, 0]
        data[at, width + orbits : 2 * width, :] = src_ref[i, 1]
        data[at, 2 * width : 2 * width + local, :] = settings_ref[i]
    for k in range(1, groups):
        mine_half, other_half = peers[2 * (k - 1)], peers[2 * (k - 1) + 1]
        for i in range(per):
            at = (owner ^ k) * per + i
            data[at, pl.ds(pl.multiple_of(core * width, width), width), :] = mine_half[i, 0:width, :]
            data[at, pl.ds(pl.multiple_of((1 - core) * width, width), width), :] = other_half[i, 0:width, :]
            data[at, 2 * width : 2 * width + local, :] = mine_half[i, width : width + local, :]
    for h in range(1, halves):
        for k in range(groups):
            for i in range(per):
                at = (owner ^ k) * per + i
                data[at, 2 * width + h * local : 2 * width + (h + 1) * local, :] = others[h - 1][k * per + i]

    pps, qqs = [], []
    for s in range(slabs):
        both = data[s, 0:width, :]
        with_p = times(both, turned(both[:orbits], 3), 1)
        with_q = times(both, turned(both[orbits:], 3), 1)
        pps.append(with_p[:orbits])
        qqs.append(with_q[orbits:])
        if s > 0:
            up1[s - 1] = -with_q[:orbits]
            dn1[s - 1] = -with_p[orbits:]
    largest = None
    for s in range(slabs):
        base = qqs[s]
        if s + 1 < slabs:
            base = base + pps[s + 1]
        if s == 0:
            base = base + pps[0]
        for e in range(mine):
            row = 2 * width + ((e // share) ^ half) * local + first + e % share
            settings = data[s, pl.ds(row, 1), :]
            m = spot[s] * mine + e
            gains[m] = settings
            block = base + jnp.where(diag_lane, settings, 0.0)
            mat[m] = block
            rhs[m] = data[s, width : 2 * width, :]
            sums = jnp.sum(jnp.abs(block), axis=0, keepdims=True)
            largest = sums if largest is None else jnp.maximum(largest, sums)
    top = 1.01 * jnp.max(largest + half_roll(largest))
    copy_out(3, 0, slabs - 1)
    copy_out(4, 0, slabs - 1)

    def held(depth, left, right, e):
        basic, place = places[(depth, left, right, 0)]
        return (up1, dn1, place) if basic else (up2, dn2, place + e)

    low = lane < orbits

    def real_rows(z):
        return jnp.concatenate([jnp.where(low, z, -z), half_roll(z)], axis=0)

    def packed(t, right):
        top, bottom = t[:orbits], t[orbits:]
        return jnp.where(low, half_roll(top), bottom) if right else jnp.where(low, top, half_roll(bottom))

    def around(depth, node, left, right, e):
        to_left = to_right = jnp.zeros((orbits, width), F32)
        inward = []
        if left is not None:
            ups, downs, place = held(depth, left, node, e)
            to_left = downs[place]
            inward.append(real_rows(ups[place]))
        if right is not None:
            ups, downs, place = held(depth, node, right, e)
            to_right = ups[place]
            inward.append(real_rows(downs[place]))
        outward = jnp.concatenate(
            [jnp.where(low, to_left, half_roll(to_right)), jnp.where(low, half_roll(to_left), to_right)], axis=0
        )
        return outward, inward[0] if len(inward) == 1 else jnp.concatenate(inward, axis=0)

    def settle(depth, node, left, right, e, step, inward):
        m = spot[node] * mine + e
        links_step, rhs_step = step[:, :width], step[:, width:]
        sol[m] = rhs_step
        change = times(inward, split(step, 3))
        if left is not None:
            w1[m] = packed(links_step, False)
            ml = spot[left] * mine + e
            mat[ml] = mat[ml] - packed(change[:width, :width], False)
            rhs[ml] = rhs[ml] - change[:width, width:]
        if right is not None:
            w2[m] = packed(links_step, True)
            mr = spot[right] * mine + e
            mat[mr] = mat[mr] - packed(change[-width:, :width], True)
            rhs[mr] = rhs[mr] - change[-width:, width:]
        if left is not None and right is not None:
            ups, downs, place = held(depth + 1, left, right, e)
            ups[place] = -packed(change[:width, :width], True)
            downs[place] = -packed(change[width:, :width], False)

    for depth, level in enumerate(levels):
        invert_batch(mat, inv, spot[level[0][0]] * mine, len(level) * mine, top)
        if depth == 0:
            for node, left, right in level:
                at = spot[node] * mine
                outward, _ = around(depth, node, left, right, 0)
                inverses = [real_rows(inv[at + e]) for e in range(mine)]
                right_parts = split(jnp.concatenate([outward, rhs[at]], axis=1), 3)
                step = times(jnp.concatenate(inverses, axis=0), right_parts)
                for e in range(mine):
                    hold[at + e] = step[e * width : (e + 1) * width]

        def work(energies, depth=depth, level=level):
            found = []
            for node, left, right in level:
                for e in energies:
                    m = spot[node] * mine + e
                    outward, inward = around(depth, node, left, right, e)
                    if depth == 0:
                        step = hold[m]
                    else:
                        step = times(real_rows(inv[m]), split(jnp.concatenate([outward, rhs[m]], axis=1), 3))
                    found.append((node, left, right, e, step, inward))
            for node, left, right, e, step, inward in found:
                settle(depth, node, left, right, e, step, inward)

        over_energies(mine, len(level) > 2, work)
        span = [spot[node] * mine for node, _, _ in level]
        for which in range(3):
            copy_out(which, span[0], span[-1] + mine)
        made = [places[(depth + 1, l, r, e)][1] for _, l, r in level if l is not None and r is not None for e in range(mine)]
        if made:
            copy_out(5, made[0], made[-1] + 1)
            copy_out(6, made[0], made[-1] + 1)
    invert_batch(mat, inv, spot[root] * mine, mine, top)
    for e in range(mine):
        m = spot[root] * mine + e
        sol[m] = tall(times(inv[m], turned(wide(rhs[m]), 3)))
    copy_out(0, spot[root] * mine, (spot[root] + 1) * mine)

    def finished(nodes):
        copy_out(7, spot[nodes[0]] * mine, (spot[nodes[-1]] + 1) * mine)
        for s in nodes:
            for e in range(mine):
                xr, xi = orbitals_of(sol, spot[s] * mine + e, half, halves, orbits)
                power = xr * xr + xi * xi
                for j in range(lines):
                    power_ref[s // per, j, e, s % per, :, :] = power[j * orb_per : (j + 1) * orb_per, :]

    finished([root])
    climb(levels, spot, mine, w1, w2, sol, finished)
    for copy in copies:
        copy.wait()


def lesser_kernel(plan, where_ref, gains, *refs):
    (slabs, mine, orbits, groups, halves, lines, per, orb_per) = plan
    stores, out_ref = refs[:8], refs[8]
    inv, w1, w2, up1, dn1, up2, dn2, ret, rhs, sol, sems = refs[9:]
    held = (inv, w1, w2, up1, dn1, up2, dn2, ret)
    half = where_ref[3]
    width = 2 * orbits
    levels, root = elimination_levels(slabs)
    spot = slots(levels, root)
    places, _ = link_places(slabs, mine, levels)
    fetches = {}

    def fetch(which, depth, low_place, high_place):
        part = pl.ds(low_place, high_place - low_place)
        copy = pltpu.make_async_copy(stores[which].at[part], held[which].at[part], sems.at[len(fetches)])
        copy.start()
        fetches[(which, depth)] = copy

    spans = []
    for level in levels:
        span = [spot[node] * mine for node, _, _ in level]
        spans.append((span[0], span[-1] + mine))
    spans.append((spot[root] * mine, (spot[root] + 1) * mine))
    for depth, span in enumerate(spans):
        fetch(7, depth, *span)
        fetch(0, depth, *span)
        if depth == 0:
            fetch(3, 0, 0, slabs - 1)
            fetch(4, 0, 0, slabs - 1)
        elif depth < len(levels):
            level = levels[depth - 1]
            made = [places[(depth, l, r, e)][1] for _, l, r in level if l is not None and r is not None for e in range(mine)]
            if made:
                fetch(5, depth, made[0], made[-1] + 1)
                fetch(6, depth, made[0], made[-1] + 1)
    for depth in range(len(levels) - 1, -1, -1):
        fetch(1, depth, *spans[depth])
        fetch(2, depth, *spans[depth])
    for depth in range(len(spans)):
        fetches[(7, depth)].wait()
    lane = lax.broadcasted_iota(jnp.int32, (orbits, width), 1)
    sub = lax.broadcasted_iota(jnp.int32, (orbits, width), 0)
    gain_lane = lane == sub + orbits
    for m in range(slabs * mine):
        gain = jnp.sum(jnp.where(gain_lane, gains[m], 0.0), axis=1, keepdims=True)
        rhs[m] = wide(ret[m]) * gain
    for depth, level in enumerate(levels):
        for which in (0, 3, 4, 5, 6):
            if (which, depth) in fetches:
                fetches[(which, depth)].wait()

        def work(energies, depth=depth, level=level):
            items = [(node, left, right, e) for node, left, right in level for e in energies]
            steps = [times(inv[spot[node] * mine + e], turned(rhs[spot[node] * mine + e], 3)) for node, _, _, e in items]
            changes = []
            for (node, left, right, e), step in zip(items, steps):
                sides = []
                if left is not None:
                    basic, place = places[(depth, left, node, 0)]
                    sides.append(up1[place] if basic else up2[place + e])
                if right is not None:
                    basic, place = places[(depth, node, right, 0)]
                    sides.append(dn1[place] if basic else dn2[place + e])
                sides = sides[0] if len(sides) == 1 else jnp.concatenate(sides, axis=0)
                changes.append(times(sides, turned(step, 3)))
            for (node, left, right, e), step, change in zip(items, steps, changes):
                sol[spot[node] * mine + e] = tall(step)
                if left is not None:
                    ml = spot[left] * mine + e
                    rhs[ml] = rhs[ml] - change[:orbits]
                if right is not None:
                    mr = spot[right] * mine + e
                    rhs[mr] = rhs[mr] - change[-orbits:]

        over_energies(mine, len(level) > 1, work)
    fetches[(0, len(levels))].wait()
    for e in range(mine):
        m = spot[root] * mine + e
        sol[m] = tall(times(inv[m], turned(rhs[m], 3)))
    for depth in range(len(levels)):
        fetches[(1, depth)].wait()
        fetches[(2, depth)].wait()
    climb(levels, spot, mine, w1, w2, sol, lambda nodes: None)
    for s in range(slabs):
        for e in range(mine):
            m = spot[s] * mine + e
            xr, xi = orbitals_of(ret, m, half, halves, orbits)
            yr, yi = orbitals_of(sol, m, half, halves, orbits)
            re = xr * yr + xi * yi
            im = xr * yi - xi * yr
            for j in range(lines):
                rows = slice(j * orb_per, (j + 1) * orb_per)
                out_ref[s // per, j, 0, e, s % per, :, :] = re[rows, :]
                out_ref[s // per, j, 1, e, s % per, :, :] = im[rows, :]


def pack_kernel(where_ref, p_ref, q_ref, src_ref, shift_ref, gain_ref, factors_ref, settings_ref, parcel_ref):
    per, _, orbits, _ = p_ref.shape
    width = 2 * orbits
    local = shift_ref.shape[1]
    core = where_ref[2]
    for i in range(per):
        settings = jnp.concatenate([shift_ref[i], gain_ref[i]], axis=1)
        settings_ref[i] = settings
        parcel_ref[i, width : width + local, :] = settings
        factors_ref[i, 0:orbits, :] = jnp.concatenate([p_ref[i, 0], p_ref[i, 1]], axis=1)
        factors_ref[i, orbits:width, :] = jnp.concatenate([q_ref[i, 0], q_ref[i, 1]], axis=1)

    @pl.when(core == 0)
    def _():
        parcel_ref[:, 0:width, :] = factors_ref[...]

    @pl.when(core != 0)
    def _():
        for i in range(per):
            parcel_ref[i, 0:orbits, :] = src_ref[i, 0]
            parcel_ref[i, orbits:width, :] = src_ref[i, 1]


def pack(where, link_p, link_q, sources, shift, lesser_gain):
    per, _, orbits, _ = link_p.shape
    width = 2 * orbits
    local = shift.shape[1]
    shapes = [(per, width, width), (per, local, width), (per, width + local, sources.shape[-1])]
    return pl.pallas_call(
        pack_kernel,
        out_shape=[jax.ShapeDtypeStruct(shape, F32) for shape in shapes],
        in_specs=[pl.BlockSpec(memory_space=pltpu.SMEM)] + vmem_specs(5),
        out_specs=vmem_specs(3),
        compiler_params=pltpu.CompilerParams(vmem_limit_bytes=VMEM_LIMIT),
        name="pack_parcel",
    )(where, link_p, link_q, sources, shift, lesser_gain)


def vmem_specs(count):
    return [pl.BlockSpec(memory_space=pltpu.VMEM)] * count


def solve_retarded(where, pieces, plan, columns):
    (slabs, mine, orbits, groups, halves, lines, per, orb_per) = plan
    width = 2 * orbits
    nodes = slabs * mine
    levels, _ = elimination_levels(slabs)
    _, fills = link_places(slabs, mine, levels)
    kept = [
        (nodes, orbits, width),
        (nodes, orbits, width),
        (nodes, orbits, width),
        (slabs - 1, orbits, width),
        (slabs - 1, orbits, width),
        (fills, orbits, width),
        (fills, orbits, width),
        (nodes, width, columns),
    ]
    shapes = [(groups, lines, mine, per, orb_per, columns), (nodes, 1, width)] + kept
    return pl.pallas_call(
        functools.partial(retarded_kernel, plan),
        out_shape=[jax.ShapeDtypeStruct(shape, F32) for shape in shapes],
        in_specs=[pl.BlockSpec(memory_space=pltpu.SMEM)] + vmem_specs(len(pieces)),
        out_specs=vmem_specs(2) + [pl.BlockSpec(memory_space=pl.ANY)] * len(kept),
        scratch_shapes=[pltpu.VMEM(shape, F32) for shape in kept]
        + [
            pltpu.VMEM((slabs, 2 * width + halves * pieces[2].shape[1], columns), F32),
            pltpu.VMEM((nodes, orbits, width), F32),
            pltpu.VMEM((nodes, width, columns), F32),
            pltpu.VMEM((len(levels[0]) * mine, width, 2 * width), F32),
            pltpu.SemaphoreType.DMA((6 * len(levels) + 4,)),
        ],
        compiler_params=pltpu.CompilerParams(vmem_limit_bytes=VMEM_LIMIT),
        name="solve_retarded",
    )(where, *pieces)


def solve_lesser(where, stored, plan):
    (slabs, mine, orbits, groups, halves, lines, per, orb_per) = plan
    levels, _ = elimination_levels(slabs)
    gains, kept = stored[0], stored[1:]
    solved = kept[7].shape
    return pl.pallas_call(
        functools.partial(lesser_kernel, plan),
        out_shape=jax.ShapeDtypeStruct((groups, lines, 2, mine, per, orb_per, solved[-1]), F32),
        in_specs=[pl.BlockSpec(memory_space=pltpu.SMEM)]
        + vmem_specs(1)
        + [pl.BlockSpec(memory_space=pl.ANY)] * len(kept),
        out_specs=pl.BlockSpec(memory_space=pltpu.VMEM),
        scratch_shapes=[pltpu.VMEM(array.shape, F32) for array in kept]
        + [pltpu.VMEM((solved[0], solved[1] // 2, 2 * solved[2]), F32), pltpu.VMEM(solved, F32), pltpu.SemaphoreType.DMA((6 * len(levels) + 4,))],
        compiler_params=pltpu.CompilerParams(vmem_limit_bytes=VMEM_LIMIT),
        name="solve_lesser",
    )(where, gains, *kept)


def correlate_kernel(order, power_ref, got_ref, out_ref):
    count = len(order)
    window = 8
    scale = 1.0 / count
    for start in range(0, count, window):
        span = min(window, count - start)
        acc_re = [None] * span
        acc_im = [None] * span
        reach = count - start
        lead = {}
        for energy in range(reach):
            sender, place = order[energy]
            power = power_ref[sender, place, 0]
            for w in range(span):
                at = energy + start + w
                if at >= count:
                    continue
                if at not in lead:
                    s2, p2 = order[at]
                    lead[at] = (got_ref[s2, 0, p2, 0], got_ref[s2, 1, p2, 0])
                re, im = lead[at]
                acc_re[w] = re * power if acc_re[w] is None else acc_re[w] + re * power
                acc_im[w] = im * power if acc_im[w] is None else acc_im[w] + im * power
        for w in range(span):
            out_ref[0, start + w, 0] = acc_re[w] * scale
            out_ref[1, start + w, 0] = acc_im[w] * scale


def correlate(power, got, order):
    senders, kinds, mine, per, rows, columns = got.shape
    count = len(order)
    return pl.pallas_call(
        functools.partial(correlate_kernel, order),
        grid=(per,),
        out_shape=jax.ShapeDtypeStruct((2, count, per, rows, columns), F32),
        in_specs=[
            pl.BlockSpec((senders, mine, 1, rows, columns), lambda i: (0, 0, i, 0, 0)),
            pl.BlockSpec((senders, kinds, mine, 1, rows, columns), lambda i: (0, 0, 0, i, 0, 0)),
        ],
        out_specs=pl.BlockSpec((2, count, 1, rows, columns), lambda i: (0, 0, i, 0, 0)),
        compiler_params=pltpu.CompilerParams(vmem_limit_bytes=VMEM_LIMIT),
        name="correlate",
    )(power, got)


def per_device(link_p, link_q, shift, lesser_gain, sources):
    per, _, orbits, _ = link_p.shape
    columns = sources.shape[-1]
    local = shift.shape[0]
    groups = lax.axis_size("slab")
    halves = lax.axis_size("half")
    lines = lax.axis_size("line")
    slabs = per * groups
    share = max(1, local // groups)
    mine = halves * share
    owner = lax.axis_index("slab")
    half = lax.axis_index("half")
    core = lax.axis_index("line") & 1
    where = jnp.stack([owner * local // groups, owner, core, half]).astype(jnp.int32)
    factors, settings, parcel = pack(
        where, link_p, link_q, sources, jnp.swapaxes(shift, 0, 1), jnp.swapaxes(lesser_gain, 0, 1)
    )
    pieces = [factors, sources, settings]
    fetched = [lax.ppermute(parcel, "slab", [(g, g ^ k) for g in range(groups)]) for k in range(1, groups)]
    siblings = [(j, j ^ 1) for j in range(lines)]
    for piece in fetched:
        pieces.append(piece)
        pieces.append(lax.ppermute(piece, "line", siblings))
    known = jnp.concatenate([settings] + [piece[:, 2 * orbits :] for piece in fetched], axis=0)
    for h in range(1, halves):
        pieces.append(lax.ppermute(known, "half", [(a, a ^ h) for a in range(halves)]))
    plan = (slabs, mine, orbits, groups, halves, lines, per, orbits // (halves * lines))
    power, *stored = solve_retarded(where, pieces, plan, columns)

    def spread(array):
        array = array.reshape((groups * lines,) + array.shape[2:])
        return lax.all_to_all(array, ("slab", "line"), split_axis=0, concat_axis=0, tiled=True)

    power = spread(power)
    got = spread(solve_lesser(where, stored, plan))
    order = []
    for energy in range(halves * lines * local):
        group, row = energy // local, energy % local
        if local >= groups:
            holder, place = row // share, row % share
        else:
            holder, place = -(-row * groups // local), 0
        order.append((holder * lines + group % lines, (group // lines) * share + place))
    return correlate(power, got, tuple(order))


def solution(mesh):
    slab_size, energy_size = mesh.devices.shape
    halves = HALVES if energy_size % (2 * HALVES) == 0 else 1
    split = jax.sharding.Mesh(
        mesh.devices.reshape(slab_size, halves, energy_size // halves), ("slab", "half", "line")
    )
    placed = (
        P("slab", None, None, None),
        P("slab", None, None, None),
        P(("half", "line"), "slab", None),
        P(("half", "line"), "slab", None),
        P("slab", None, None, None),
    )
    return jax.shard_map(
        per_device,
        mesh=split,
        in_specs=placed,
        out_specs=P(None, None, "slab", ("half", "line"), None),
        check_vma=False,
    )
```

```python
import functools

import jax
import jax.numpy as jnp
from jax import lax
from jax.experimental import pallas as pl
from jax.experimental.pallas import tpu as pltpu
from jax.sharding import PartitionSpec as P

F32 = jnp.float32
BF16 = jnp.bfloat16
VMEM_LIMIT = 56 * 1024 * 1024
LEAST = 0.0095
CLOSE = 1e-3
STRIDE = 4
GROUP = 24
ASSEMBLED = 3
HALVES = 2


def elimination_levels(count):
    levels = []
    chain = list(range(count))
    while len(chain) > 1:
        level = []
        for place in range(0, len(chain), 2):
            left = chain[place - 1] if place > 0 else None
            right = chain[place + 1] if place + 1 < len(chain) else None
            level.append((chain[place], left, right))
        levels.append(level)
        chain = chain[1::2]
    return levels, chain[0]


def split(x, count):
    parts = []
    for place in range(count):
        part = x.astype(BF16)
        parts.append(part)
        if place + 1 < count:
            x = x - part.astype(F32)
    return parts


def half_roll(x):
    return pltpu.roll(x, x.shape[1] // 2, 1)


def turned(block, count):
    half = block.shape[1] // 2
    top = split(block, count)
    if half % 128 == 0:
        bottom = [jnp.concatenate([-part[:, half:], part[:, :half]], axis=1) for part in top]
    else:
        low = lax.broadcasted_iota(jnp.int32, block.shape, 1) < half
        rolled = half_roll(block)
        bottom = split(jnp.where(low, -rolled, rolled), count)
    return [jnp.concatenate([one, two], axis=0) for one, two in zip(top, bottom)]


def wide(x):
    half = x.shape[0] // 2
    return jnp.concatenate([x[:half], x[half:]], axis=1)


def tall(x):
    half = x.shape[1] // 2
    return jnp.concatenate([x[:, :half], x[:, half:]], axis=0)


def above(blocks, count):
    parts = [turned(block, count) for block in blocks]
    if len(parts) == 1:
        return parts[0]
    return [jnp.concatenate([part[k] for part in parts], axis=0) for k in range(count)]


def times(a, right, contract=0):
    left = split(a, len(right))
    if len(right) == 3:
        left = [left[0], left[1], left[0], left[1], left[0], left[2]]
        right = [right[0], right[0], right[1], right[1], right[2], right[0]]
    else:
        left = [left[0], left[1], left[0]]
        right = [right[0], right[0], right[1]]
    return lax.dot_general(
        jnp.concatenate(left, axis=1),
        jnp.concatenate(right, axis=contract),
        (((1,), (contract,)), ((), ())),
        preferred_element_type=F32,
    )


def over_energies(mine, many, work):
    if many and mine > 2 and mine % 2 == 0:

        def two(place, unused):
            work([2 * place, 2 * place + 1])
            return 0

        lax.fori_loop(0, mine // 2, two, 0)
    else:
        work(list(range(mine)))


def invert_batch(mat_ref, inv_ref, first, number, top):
    size = next(size for size in range(min(number, GROUP), 0, -1) if number % size == 0)
    if size == number:
        invert_group(mat_ref, inv_ref, range(first, first + number), top)
    else:

        def group(place, unused):
            begin = first + place * size
            invert_group(mat_ref, inv_ref, [begin + n for n in range(size)], top)
            return 0

        lax.fori_loop(0, number // size, group, 0)


def invert_group(mat_ref, inv_ref, members, top):
    shape = mat_ref.shape[1:]
    count = shape[0]
    lane = lax.broadcasted_iota(jnp.int32, shape, 1)
    sub = lax.broadcasted_iota(jnp.int32, shape, 0)
    eye = jnp.where(lane == sub, 1.0, 0.0).astype(F32)
    total = top + LEAST

    def factor_of(reach):
        squared = reach * reach
        gain = 2.0 / (2.0 - squared)
        return gain, 0.5 * squared * gain

    def steps(xs, ts, reach, number):
        for step in range(number):
            gain, reach = factor_of(reach)
            bases = [(2.0 * eye - t) * gain for t in ts]
            if step + 1 < number:
                pairs = [times(jnp.concatenate([x, t], axis=0), turned(base, 2)) for x, t, base in zip(xs, ts, bases)]
                xs = [pair[:count] for pair in pairs]
                ts = [pair[count:] for pair in pairs]
            else:
                xs = [times(x, turned(base, 2)) for x, base in zip(xs, bases)]
        for m, x in zip(members, xs):
            inv_ref[m] = x
        return reach

    start = 2.0 / total
    gain, reach = factor_of((top - LEAST) / total)
    ts = [mat_ref[m] * start for m in members]
    bases = [(2.0 * eye - t) * gain for t in ts]
    xs = [base * start for base in bases]
    ts = [times(t, turned(base, 2)) for t, base in zip(ts, bases)]
    reach = steps(xs, ts, reach, STRIDE - 1)

    def cycle(reach):
        xs = [inv_ref[m] for m in members]
        ts = [times(mat_ref[m], turned(x, 2)) for m, x in zip(members, xs)]
        return steps(xs, ts, reach, STRIDE)

    lax.while_loop(lambda reach: reach > CLOSE, cycle, reach)
    xs = [inv_ref[m] for m in members]
    rests = [eye - times(mat_ref[m], turned(x, 3)) for m, x in zip(members, xs)]
    for m, x, rest in zip(members, xs, rests):
        inv_ref[m] = x + times(x, turned(rest, 2))


def slots(levels, root):
    order = [node for level in levels for node, _, _ in level] + [root]
    return {node: place for place, node in enumerate(order)}


def link_places(slabs, mine, levels):
    places = {}
    for s in range(slabs - 1):
        for e in range(mine):
            places[(0, s, s + 1, e)] = (True, s)
    spare = 0
    for depth, level in enumerate(levels):
        for node, left, right in level:
            if left is not None and right is not None:
                for e in range(mine):
                    places[(depth + 1, left, right, e)] = (False, spare)
                    spare += 1
    return places, spare


def climb(levels, spot, mine, w1, w2, sol, finished):
    for level in reversed(levels):

        def work(energies, level=level):
            values = []
            for node, left, right in level:
                for e in energies:
                    m = spot[node] * mine + e
                    steps, sides = [], []
                    if left is not None:
                        steps.append(w1[m])
                        sides.append(wide(sol[spot[left] * mine + e]))
                    if right is not None:
                        steps.append(w2[m])
                        sides.append(wide(sol[spot[right] * mine + e]))
                    steps = steps[0] if len(steps) == 1 else jnp.concatenate(steps, axis=1)
                    values.append((m, sol[m] - tall(times(steps, above(sides, 2)))))
            for m, value in values:
                sol[m] = value

        over_energies(mine, len(level) > 2, work)
        finished([node for node, _, _ in level])


def orbitals_of(ref, m, half, halves, orbits):
    count = orbits // halves
    found = [ref[m, 0:count, :], ref[m, orbits : orbits + count, :]]
    for h in range(1, halves):
        found = [
            jnp.where(half == h, ref[m, low + h * count : low + (h + 1) * count, :], kept)
            for low, kept in zip((0, orbits), found)
        ]
    return found


def retarded_kernel(plan, where_ref, *refs):
    (slabs, mine, orbits, groups, halves, lines, per, orb_per) = plan
    factors_ref, src_ref, settings_ref = refs[:3]
    peers = refs[3 : 3 + 2 * (groups - 1)]
    refs = refs[3 + 2 * (groups - 1) :]
    others, refs = refs[: halves - 1], refs[halves - 1 :]
    local = settings_ref.shape[1]
    power_ref, gains, outs = refs[0], refs[1], refs[2:10]
    inv, w1, w2, up1, dn1, up2, dn2, sol, data, mat, rhs, hold, sems = refs[10:]
    stores = (inv, w1, w2, up1, dn1, up2, dn2, sol)
    copies = []

    def copy_out(which, low_place, high_place):
        part = pl.ds(low_place, high_place - low_place)
        copy = pltpu.make_async_copy(stores[which].at[part], outs[which].at[part], sems.at[len(copies)])
        copy.start()
        copies.append(copy)

    width = 2 * orbits
    columns = src_ref.shape[-1]
    share = mine // halves
    levels, root = elimination_levels(slabs)
    spot = slots(levels, root)
    places, _ = link_places(slabs, mine, levels)
    lane = lax.broadcasted_iota(jnp.int32, (orbits, width), 1)
    sub = lax.broadcasted_iota(jnp.int32, (orbits, width), 0)
    diag_lane = lane == sub
    first, owner, core, half = where_ref[0], where_ref[1], where_ref[2], where_ref[3]

    for i in range(per):
        at = owner * per + i
        data[at, 0:width, :] = factors_ref[i]
        data[at, width : width + orbits, :] = src_ref[i, 0]
        data[at, width + orbits : 2 * width, :] = src_ref[i, 1]
        data[at, 2 * width : 2 * width + local, :] = settings_ref[i]
    for k in range(1, groups):
        mine_half, other_half = peers[2 * (k - 1)], peers[2 * (k - 1) + 1]
        for i in range(per):
            at = (owner ^ k) * per + i
            data[at, pl.ds(pl.multiple_of(core * width, width), width), :] = mine_half[i, 0:width, :]
            data[at, pl.ds(pl.multiple_of((1 - core) * width, width), width), :] = other_half[i, 0:width, :]
            data[at, 2 * width : 2 * width + local, :] = mine_half[i, width : width + local, :]
    for h in range(1, halves):
        for k in range(groups):
            for i in range(per):
                at = (owner ^ k) * per + i
                data[at, 2 * width + h * local : 2 * width + (h + 1) * local, :] = others[h - 1][k * per + i]

    def assemble(s, unused):
        both = data[s, 0:width, :]
        with_p = times(both, turned(both[:orbits], 3), 1)
        with_q = times(both, turned(both[orbits:], 3), 1)
        hold[s, 0:orbits, 0:width] = with_p[:orbits]
        hold[s, orbits:width, 0:width] = with_q[orbits:]
        before = jnp.maximum(s - 1, 0)
        up1[before] = -with_q[:orbits]
        dn1[before] = -with_p[orbits:]
        return 0

    def assemble_some(place, unused):
        for n in range(ASSEMBLED):
            assemble(place * ASSEMBLED + n, 0)
        return 0

    lax.fori_loop(0, slabs // ASSEMBLED, assemble_some, 0)
    for s in range(slabs // ASSEMBLED * ASSEMBLED, slabs):
        assemble(s, 0)
    largest = largest_shift = None
    for s in range(slabs):
        base = hold[s, orbits:width, 0:width]
        if s + 1 < slabs:
            base = base + hold[s + 1, 0:orbits, 0:width]
        if s == 0:
            base = base + hold[0, 0:orbits, 0:width]
        squares = base * base
        sums = jnp.sum(jnp.sqrt(squares + half_roll(squares)), axis=0, keepdims=True)
        largest = sums if largest is None else jnp.maximum(largest, sums)
        for e in range(mine):
            row = 2 * width + ((e // share) ^ half) * local + first + e % share
            settings = data[s, pl.ds(row, 1), :]
            m = spot[s] * mine + e
            gains[m] = settings
            mat[m] = base + jnp.where(diag_lane, settings, 0.0)
            rhs[m] = data[s, width : 2 * width, :]
            largest_shift = settings if largest_shift is None else jnp.maximum(largest_shift, settings)
    shift_lane = lax.broadcasted_iota(jnp.int32, largest_shift.shape, 1) < orbits
    top = 1.01 * jnp.max(largest + jnp.max(jnp.where(shift_lane, largest_shift, 0.0)))
    copy_out(3, 0, slabs - 1)
    copy_out(4, 0, slabs - 1)

    def held(depth, left, right, e):
        basic, place = places[(depth, left, right, 0)]
        return (up1, dn1, place) if basic else (up2, dn2, place + e)

    low = lane < orbits

    def real_rows(z):
        return jnp.concatenate([jnp.where(low, z, -z), half_roll(z)], axis=0)

    def packed(t, right):
        top, bottom = t[:orbits], t[orbits:]
        return jnp.where(low, half_roll(top), bottom) if right else jnp.where(low, top, half_roll(bottom))

    def around(depth, node, left, right, e):
        to_left = to_right = jnp.zeros((orbits, width), F32)
        inward = []
        if left is not None:
            ups, downs, place = held(depth, left, node, e)
            to_left = downs[place]
            inward.append(real_rows(ups[place]))
        if right is not None:
            ups, downs, place = held(depth, node, right, e)
            to_right = ups[place]
            inward.append(real_rows(downs[place]))
        outward = jnp.concatenate(
            [jnp.where(low, to_left, half_roll(to_right)), jnp.where(low, half_roll(to_left), to_right)], axis=0
        )
        return outward, inward[0] if len(inward) == 1 else jnp.concatenate(inward, axis=0)

    def settle(depth, node, left, right, e, step, inward):
        m = spot[node] * mine + e
        links_step, rhs_step = step[:, :width], step[:, width:]
        sol[m] = rhs_step
        change = times(inward, split(step, 3))
        if left is not None:
            w1[m] = packed(links_step, False)
            ml = spot[left] * mine + e
            mat[ml] = mat[ml] - packed(change[:width, :width], False)
            rhs[ml] = rhs[ml] - change[:width, width:]
        if right is not None:
            w2[m] = packed(links_step, True)
            mr = spot[right] * mine + e
            mat[mr] = mat[mr] - packed(change[-width:, :width], True)
            rhs[mr] = rhs[mr] - change[-width:, width:]
        if left is not None and right is not None:
            ups, downs, place = held(depth + 1, left, right, e)
            ups[place] = -packed(change[:width, :width], True)
            downs[place] = -packed(change[width:, :width], False)

    for depth, level in enumerate(levels):
        invert_batch(mat, inv, spot[level[0][0]] * mine, len(level) * mine, top)
        if depth == 0:
            for node, left, right in level:
                at = spot[node] * mine
                outward, _ = around(depth, node, left, right, 0)
                inverses = [real_rows(inv[at + e]) for e in range(mine)]
                right_parts = split(jnp.concatenate([outward, rhs[at]], axis=1), 3)
                step = times(jnp.concatenate(inverses, axis=0), right_parts)
                for e in range(mine):
                    hold[at + e] = step[e * width : (e + 1) * width]

        def work(energies, depth=depth, level=level):
            found = []
            for node, left, right in level:
                for e in energies:
                    m = spot[node] * mine + e
                    outward, inward = around(depth, node, left, right, e)
                    if depth == 0:
                        step = hold[m]
                    else:
                        step = times(real_rows(inv[m]), split(jnp.concatenate([outward, rhs[m]], axis=1), 3))
                    found.append((node, left, right, e, step, inward))
            for node, left, right, e, step, inward in found:
                settle(depth, node, left, right, e, step, inward)

        over_energies(mine, len(level) > 2, work)
        span = [spot[node] * mine for node, _, _ in level]
        for which in range(3):
            copy_out(which, span[0], span[-1] + mine)
        made = [places[(depth + 1, l, r, e)][1] for _, l, r in level if l is not None and r is not None for e in range(mine)]
        if made:
            copy_out(5, made[0], made[-1] + 1)
            copy_out(6, made[0], made[-1] + 1)
    invert_batch(mat, inv, spot[root] * mine, mine, top)
    for e in range(mine):
        m = spot[root] * mine + e
        sol[m] = tall(times(inv[m], turned(wide(rhs[m]), 3)))
    copy_out(0, spot[root] * mine, (spot[root] + 1) * mine)

    def finished(nodes):
        copy_out(7, spot[nodes[0]] * mine, (spot[nodes[-1]] + 1) * mine)

    def deliver(e, unused):
        for s in range(slabs):
            xr, xi = orbitals_of(sol, spot[s] * mine + e, half, halves, orbits)
            power = xr * xr + xi * xi
            for j in range(lines):
                power_ref[s // per, j, e, s % per, :, :] = power[j * orb_per : (j + 1) * orb_per, :]
        return 0

    finished([root])
    climb(levels, spot, mine, w1, w2, sol, finished)
    lax.fori_loop(0, mine, deliver, 0)
    for copy in copies:
        copy.wait()


def lesser_kernel(plan, where_ref, gains, *refs):
    (slabs, mine, orbits, groups, halves, lines, per, orb_per) = plan
    stores, out_ref = refs[:8], refs[8]
    inv, w1, w2, up1, dn1, up2, dn2, ret, rhs, sol, sems = refs[9:]
    held = (inv, w1, w2, up1, dn1, up2, dn2, ret)
    half = where_ref[3]
    width = 2 * orbits
    levels, root = elimination_levels(slabs)
    spot = slots(levels, root)
    places, _ = link_places(slabs, mine, levels)
    fetches = {}

    def fetch(which, depth, low_place, high_place):
        part = pl.ds(low_place, high_place - low_place)
        copy = pltpu.make_async_copy(stores[which].at[part], held[which].at[part], sems.at[len(fetches)])
        copy.start()
        fetches[(which, depth)] = copy

    spans = []
    for level in levels:
        span = [spot[node] * mine for node, _, _ in level]
        spans.append((span[0], span[-1] + mine))
    spans.append((spot[root] * mine, (spot[root] + 1) * mine))
    for depth, span in enumerate(spans):
        fetch(7, depth, *span)
        fetch(0, depth, *span)
        if depth == 0:
            fetch(3, 0, 0, slabs - 1)
            fetch(4, 0, 0, slabs - 1)
        elif depth < len(levels):
            level = levels[depth - 1]
            made = [places[(depth, l, r, e)][1] for _, l, r in level if l is not None and r is not None for e in range(mine)]
            if made:
                fetch(5, depth, made[0], made[-1] + 1)
                fetch(6, depth, made[0], made[-1] + 1)
    for depth in range(len(levels) - 1, -1, -1):
        fetch(1, depth, *spans[depth])
        fetch(2, depth, *spans[depth])
    for depth in range(len(spans)):
        fetches[(7, depth)].wait()
    lane = lax.broadcasted_iota(jnp.int32, (orbits, width), 1)
    sub = lax.broadcasted_iota(jnp.int32, (orbits, width), 0)
    gain_lane = lane == sub + orbits

    def scale(s, unused):
        for e in range(mine):
            m = s * mine + e
            gain = jnp.sum(jnp.where(gain_lane, gains[m], 0.0), axis=1, keepdims=True)
            rhs[m] = wide(ret[m]) * gain
        return 0

    lax.fori_loop(0, slabs, scale, 0)
    for depth, level in enumerate(levels):
        for which in (0, 3, 4, 5, 6):
            if (which, depth) in fetches:
                fetches[(which, depth)].wait()

        def work(energies, depth=depth, level=level):
            items = [(node, left, right, e) for node, left, right in level for e in energies]
            steps = [times(inv[spot[node] * mine + e], turned(rhs[spot[node] * mine + e], 3)) for node, _, _, e in items]
            changes = []
            for (node, left, right, e), step in zip(items, steps):
                sides = []
                if left is not None:
                    basic, place = places[(depth, left, node, 0)]
                    sides.append(up1[place] if basic else up2[place + e])
                if right is not None:
                    basic, place = places[(depth, node, right, 0)]
                    sides.append(dn1[place] if basic else dn2[place + e])
                sides = sides[0] if len(sides) == 1 else jnp.concatenate(sides, axis=0)
                changes.append(times(sides, turned(step, 3)))
            for (node, left, right, e), step, change in zip(items, steps, changes):
                sol[spot[node] * mine + e] = tall(step)
                if left is not None:
                    ml = spot[left] * mine + e
                    rhs[ml] = rhs[ml] - change[:orbits]
                if right is not None:
                    mr = spot[right] * mine + e
                    rhs[mr] = rhs[mr] - change[-orbits:]

        over_energies(mine, len(level) > 1, work)
    fetches[(0, len(levels))].wait()
    for e in range(mine):
        m = spot[root] * mine + e
        sol[m] = tall(times(inv[m], turned(rhs[m], 3)))
    for depth in range(len(levels)):
        fetches[(1, depth)].wait()
        fetches[(2, depth)].wait()
    climb(levels, spot, mine, w1, w2, sol, lambda nodes: None)

    def deliver(e, unused):
        for s in range(slabs):
            m = spot[s] * mine + e
            xr, xi = orbitals_of(ret, m, half, halves, orbits)
            yr, yi = orbitals_of(sol, m, half, halves, orbits)
            re = xr * yr + xi * yi
            im = xr * yi - xi * yr
            for j in range(lines):
                rows = slice(j * orb_per, (j + 1) * orb_per)
                out_ref[s // per, j, 0, e, s % per, :, :] = re[rows, :]
                out_ref[s // per, j, 1, e, s % per, :, :] = im[rows, :]
        return 0

    lax.fori_loop(0, mine, deliver, 0)


def pack_kernel(where_ref, p_ref, q_ref, src_ref, shift_ref, gain_ref, factors_ref, settings_ref, parcel_ref):
    per, _, orbits, _ = p_ref.shape
    width = 2 * orbits
    local = shift_ref.shape[1]
    core = where_ref[2]
    for i in range(per):
        settings = jnp.concatenate([shift_ref[i], gain_ref[i]], axis=1)
        settings_ref[i] = settings
        parcel_ref[i, width : width + local, :] = settings
        factors_ref[i, 0:orbits, :] = jnp.concatenate([p_ref[i, 0], p_ref[i, 1]], axis=1)
        factors_ref[i, orbits:width, :] = jnp.concatenate([q_ref[i, 0], q_ref[i, 1]], axis=1)

    @pl.when(core == 0)
    def _():
        parcel_ref[:, 0:width, :] = factors_ref[...]

    @pl.when(core != 0)
    def _():
        for i in range(per):
            parcel_ref[i, 0:orbits, :] = src_ref[i, 0]
            parcel_ref[i, orbits:width, :] = src_ref[i, 1]


def pack(where, link_p, link_q, sources, shift, lesser_gain):
    per, _, orbits, _ = link_p.shape
    width = 2 * orbits
    local = shift.shape[1]
    shapes = [(per, width, width), (per, local, width), (per, width + local, sources.shape[-1])]
    return pl.pallas_call(
        pack_kernel,
        out_shape=[jax.ShapeDtypeStruct(shape, F32) for shape in shapes],
        in_specs=[pl.BlockSpec(memory_space=pltpu.SMEM)] + vmem_specs(5),
        out_specs=vmem_specs(3),
        compiler_params=pltpu.CompilerParams(vmem_limit_bytes=VMEM_LIMIT),
        name="pack_parcel",
    )(where, link_p, link_q, sources, shift, lesser_gain)


def vmem_specs(count):
    return [pl.BlockSpec(memory_space=pltpu.VMEM)] * count


def solve_retarded(where, pieces, plan, columns):
    (slabs, mine, orbits, groups, halves, lines, per, orb_per) = plan
    width = 2 * orbits
    nodes = slabs * mine
    levels, _ = elimination_levels(slabs)
    _, fills = link_places(slabs, mine, levels)
    kept = [
        (nodes, orbits, width),
        (nodes, orbits, width),
        (nodes, orbits, width),
        (slabs - 1, orbits, width),
        (slabs - 1, orbits, width),
        (fills, orbits, width),
        (fills, orbits, width),
        (nodes, width, columns),
    ]
    shapes = [(groups, lines, mine, per, orb_per, columns), (nodes, 1, width)] + kept
    return pl.pallas_call(
        functools.partial(retarded_kernel, plan),
        out_shape=[jax.ShapeDtypeStruct(shape, F32) for shape in shapes],
        in_specs=[pl.BlockSpec(memory_space=pltpu.SMEM)] + vmem_specs(len(pieces)),
        out_specs=vmem_specs(2) + [pl.BlockSpec(memory_space=pl.ANY)] * len(kept),
        scratch_shapes=[pltpu.VMEM(shape, F32) for shape in kept]
        + [
            pltpu.VMEM((slabs, 2 * width + halves * pieces[2].shape[1], columns), F32),
            pltpu.VMEM((nodes, orbits, width), F32),
            pltpu.VMEM((nodes, width, columns), F32),
            pltpu.VMEM((len(levels[0]) * mine, width, 2 * width), F32),
            pltpu.SemaphoreType.DMA((6 * len(levels) + 4,)),
        ],
        compiler_params=pltpu.CompilerParams(vmem_limit_bytes=VMEM_LIMIT),
        name="solve_retarded",
    )(where, *pieces)


def solve_lesser(where, stored, plan):
    (slabs, mine, orbits, groups, halves, lines, per, orb_per) = plan
    levels, _ = elimination_levels(slabs)
    gains, kept = stored[0], stored[1:]
    solved = kept[7].shape
    return pl.pallas_call(
        functools.partial(lesser_kernel, plan),
        out_shape=jax.ShapeDtypeStruct((groups, lines, 2, mine, per, orb_per, solved[-1]), F32),
        in_specs=[pl.BlockSpec(memory_space=pltpu.SMEM)]
        + vmem_specs(1)
        + [pl.BlockSpec(memory_space=pl.ANY)] * len(kept),
        out_specs=pl.BlockSpec(memory_space=pltpu.VMEM),
        scratch_shapes=[pltpu.VMEM(array.shape, F32) for array in kept]
        + [pltpu.VMEM((solved[0], solved[1] // 2, 2 * solved[2]), F32), pltpu.VMEM(solved, F32), pltpu.SemaphoreType.DMA((6 * len(levels) + 4,))],
        compiler_params=pltpu.CompilerParams(vmem_limit_bytes=VMEM_LIMIT),
        name="solve_lesser",
    )(where, gains, *kept)


def correlate_kernel(order, power_ref, got_ref, out_ref):
    count = len(order)
    window = 8
    scale = 1.0 / count
    for start in range(0, count, window):
        span = min(window, count - start)
        acc_re = [None] * span
        acc_im = [None] * span
        reach = count - start
        lead = {}
        for energy in range(reach):
            sender, place = order[energy]
            power = power_ref[sender, place, 0]
            for w in range(span):
                at = energy + start + w
                if at >= count:
                    continue
                if at not in lead:
                    s2, p2 = order[at]
                    lead[at] = (got_ref[s2, 0, p2, 0], got_ref[s2, 1, p2, 0])
                re, im = lead[at]
                acc_re[w] = re * power if acc_re[w] is None else acc_re[w] + re * power
                acc_im[w] = im * power if acc_im[w] is None else acc_im[w] + im * power
        for w in range(span):
            out_ref[0, start + w, 0] = acc_re[w] * scale
            out_ref[1, start + w, 0] = acc_im[w] * scale


def correlate(power, got, order):
    senders, kinds, mine, per, rows, columns = got.shape
    count = len(order)
    return pl.pallas_call(
        functools.partial(correlate_kernel, order),
        grid=(per,),
        out_shape=jax.ShapeDtypeStruct((2, count, per, rows, columns), F32),
        in_specs=[
            pl.BlockSpec((senders, mine, 1, rows, columns), lambda i: (0, 0, i, 0, 0)),
            pl.BlockSpec((senders, kinds, mine, 1, rows, columns), lambda i: (0, 0, 0, i, 0, 0)),
        ],
        out_specs=pl.BlockSpec((2, count, 1, rows, columns), lambda i: (0, 0, i, 0, 0)),
        compiler_params=pltpu.CompilerParams(vmem_limit_bytes=VMEM_LIMIT),
        name="correlate",
    )(power, got)


def per_device(link_p, link_q, shift, lesser_gain, sources):
    per, _, orbits, _ = link_p.shape
    columns = sources.shape[-1]
    local = shift.shape[0]
    groups = lax.axis_size("slab")
    halves = lax.axis_size("half")
    lines = lax.axis_size("line")
    slabs = per * groups
    share = max(1, local // groups)
    mine = halves * share
    owner = lax.axis_index("slab")
    half = lax.axis_index("half")
    core = lax.axis_index("line") & 1
    where = jnp.stack([owner * local // groups, owner, core, half]).astype(jnp.int32)
    factors, settings, parcel = pack(
        where, link_p, link_q, sources, jnp.swapaxes(shift, 0, 1), jnp.swapaxes(lesser_gain, 0, 1)
    )
    pieces = [factors, sources, settings]
    fetched = [lax.ppermute(parcel, "slab", [(g, g ^ k) for g in range(groups)]) for k in range(1, groups)]
    siblings = [(j, j ^ 1) for j in range(lines)]
    for piece in fetched:
        pieces.append(piece)
        pieces.append(lax.ppermute(piece, "line", siblings))
    known = jnp.concatenate([settings] + [piece[:, 2 * orbits :] for piece in fetched], axis=0)
    for h in range(1, halves):
        pieces.append(lax.ppermute(known, "half", [(a, a ^ h) for a in range(halves)]))
    plan = (slabs, mine, orbits, groups, halves, lines, per, orbits // (halves * lines))
    power, *stored = solve_retarded(where, pieces, plan, columns)

    def spread(array):
        array = array.reshape((groups * lines,) + array.shape[2:])
        return lax.all_to_all(array, ("slab", "line"), split_axis=0, concat_axis=0, tiled=True)

    power = spread(power)
    got = spread(solve_lesser(where, stored, plan))
    order = []
    for energy in range(halves * lines * local):
        group, row = energy // local, energy % local
        if local >= groups:
            holder, place = row // share, row % share
        else:
            holder, place = -(-row * groups // local), 0
        order.append((holder * lines + group % lines, (group // lines) * share + place))
    return correlate(power, got, tuple(order))


def solution(mesh):
    slab_size, energy_size = mesh.devices.shape
    halves = HALVES if energy_size % (2 * HALVES) == 0 else 1
    split = jax.sharding.Mesh(
        mesh.devices.reshape(slab_size, halves, energy_size // halves), ("slab", "half", "line")
    )
    placed = (
        P("slab", None, None, None),
        P("slab", None, None, None),
        P(("half", "line"), "slab", None),
        P(("half", "line"), "slab", None),
        P("slab", None, None, None),
    )
    return jax.shard_map(
        per_device,
        mesh=split,
        in_specs=placed,
        out_specs=P(None, None, "slab", ("half", "line"), None),
        check_vma=False,
    )
```

```python
import functools

import jax
import jax.numpy as jnp
from jax import lax
from jax.experimental import pallas as pl
from jax.experimental.pallas import tpu as pltpu
from jax.sharding import PartitionSpec as P

F32 = jnp.float32
BF16 = jnp.bfloat16
VMEM_LIMIT = 56 * 1024 * 1024
LEAST = 0.0095
CLOSE = 1e-3
STRIDE = 4
GROUP = 24
ASSEMBLED = 3
HALVES = 2


def elimination_levels(count):
    levels = []
    chain = list(range(count))
    while len(chain) > 1:
        level = []
        for place in range(0, len(chain), 2):
            left = chain[place - 1] if place > 0 else None
            right = chain[place + 1] if place + 1 < len(chain) else None
            level.append((chain[place], left, right))
        levels.append(level)
        chain = chain[1::2]
    return levels, chain[0]


def split(x, count):
    parts = []
    for place in range(count):
        part = x.astype(BF16)
        parts.append(part)
        if place + 1 < count:
            x = x - part.astype(F32)
    return parts


def half_roll(x):
    return pltpu.roll(x, x.shape[1] // 2, 1)


def turned(block, count):
    half = block.shape[1] // 2
    top = split(block, count)
    if half % 128 == 0:
        bottom = [jnp.concatenate([-part[:, half:], part[:, :half]], axis=1) for part in top]
    else:
        low = lax.broadcasted_iota(jnp.int32, block.shape, 1) < half
        rolled = half_roll(block)
        bottom = split(jnp.where(low, -rolled, rolled), count)
    return [jnp.concatenate([one, two], axis=0) for one, two in zip(top, bottom)]


def wide(x):
    half = x.shape[0] // 2
    return jnp.concatenate([x[:half], x[half:]], axis=1)


def tall(x):
    half = x.shape[1] // 2
    return jnp.concatenate([x[:, :half], x[:, half:]], axis=0)


def above(blocks, count):
    parts = [turned(block, count) for block in blocks]
    if len(parts) == 1:
        return parts[0]
    return [jnp.concatenate([part[k] for part in parts], axis=0) for k in range(count)]


def times(a, right, contract=0):
    left = split(a, len(right))
    if len(right) == 3:
        left = [left[0], left[1], left[0], left[1], left[0], left[2]]
        right = [right[0], right[0], right[1], right[1], right[2], right[0]]
    else:
        left = [left[0], left[1], left[0]]
        right = [right[0], right[0], right[1]]
    return lax.dot_general(
        jnp.concatenate(left, axis=1),
        jnp.concatenate(right, axis=contract),
        (((1,), (contract,)), ((), ())),
        preferred_element_type=F32,
    )


def over_energies(mine, many, work):
    if many and mine > 2 and mine % 2 == 0:

        def two(place, unused):
            work([2 * place, 2 * place + 1])
            return 0

        lax.fori_loop(0, mine // 2, two, 0)
    else:
        work(list(range(mine)))


def invert_batch(mat_ref, inv_ref, first, number, top):
    size = next(size for size in range(min(number, GROUP), 0, -1) if number % size == 0)
    if size == number:
        invert_group(mat_ref, inv_ref, range(first, first + number), top)
    else:

        def group(place, unused):
            begin = first + place * size
            invert_group(mat_ref, inv_ref, [begin + n for n in range(size)], top)
            return 0

        lax.fori_loop(0, number // size, group, 0)


def invert_group(mat_ref, inv_ref, members, top):
    shape = mat_ref.shape[1:]
    count = shape[0]
    lane = lax.broadcasted_iota(jnp.int32, shape, 1)
    sub = lax.broadcasted_iota(jnp.int32, shape, 0)
    eye = jnp.where(lane == sub, 1.0, 0.0).astype(F32)
    total = top + LEAST

    def factor_of(reach):
        squared = reach * reach
        gain = 2.0 / (2.0 - squared)
        return gain, 0.5 * squared * gain

    def steps(xs, ts, reach, number):
        for step in range(number):
            gain, reach = factor_of(reach)
            bases = [(2.0 * eye - t) * gain for t in ts]
            if step + 1 < number:
                pairs = [times(jnp.concatenate([x, t], axis=0), turned(base, 2)) for x, t, base in zip(xs, ts, bases)]
                xs = [pair[:count] for pair in pairs]
                ts = [pair[count:] for pair in pairs]
            else:
                xs = [times(x, turned(base, 2)) for x, base in zip(xs, bases)]
        for m, x in zip(members, xs):
            inv_ref[m] = x
        return reach

    start = 2.0 / total
    gain, reach = factor_of((top - LEAST) / total)
    ts = [mat_ref[m] * start for m in members]
    bases = [(2.0 * eye - t) * gain for t in ts]
    xs = [base * start for base in bases]
    ts = [times(t, turned(base, 2)) for t, base in zip(ts, bases)]
    reach = steps(xs, ts, reach, STRIDE - 1)

    def cycle(reach):
        xs = [inv_ref[m] for m in members]
        ts = [times(mat_ref[m], turned(x, 2)) for m, x in zip(members, xs)]
        return steps(xs, ts, reach, STRIDE)

    lax.while_loop(lambda reach: reach > CLOSE, cycle, reach)
    xs = [inv_ref[m] for m in members]
    rests = [eye - times(mat_ref[m], turned(x, 3)) for m, x in zip(members, xs)]
    for m, x, rest in zip(members, xs, rests):
        inv_ref[m] = x + times(x, turned(rest, 2))


def slots(levels, root):
    order = [node for level in levels for node, _, _ in level] + [root]
    return {node: place for place, node in enumerate(order)}


def link_places(slabs, mine, levels):
    places = {}
    for s in range(slabs - 1):
        for e in range(mine):
            places[(0, s, s + 1, e)] = (True, s)
    spare = 0
    for depth, level in enumerate(levels):
        for node, left, right in level:
            if left is not None and right is not None:
                for e in range(mine):
                    places[(depth + 1, left, right, e)] = (False, spare)
                    spare += 1
    return places, spare


def climb(levels, spot, mine, w1, w2, sol, finished):
    for level in reversed(levels):

        def work(energies, level=level):
            values = []
            for node, left, right in level:
                for e in energies:
                    m = spot[node] * mine + e
                    steps, sides = [], []
                    if left is not None:
                        steps.append(w1[m])
                        sides.append(wide(sol[spot[left] * mine + e]))
                    if right is not None:
                        steps.append(w2[m])
                        sides.append(wide(sol[spot[right] * mine + e]))
                    steps = steps[0] if len(steps) == 1 else jnp.concatenate(steps, axis=1)
                    values.append((m, sol[m] - tall(times(steps, above(sides, 2)))))
            for m, value in values:
                sol[m] = value

        over_energies(mine, len(level) > 2, work)
        finished([node for node, _, _ in level])


def orbitals_of(ref, m, half, halves, orbits):
    count = orbits // halves
    found = [ref[m, 0:count, :], ref[m, orbits : orbits + count, :]]
    for h in range(1, halves):
        found = [
            jnp.where(half == h, ref[m, low + h * count : low + (h + 1) * count, :], kept)
            for low, kept in zip((0, orbits), found)
        ]
    return found


def retarded_kernel(plan, where_ref, *refs):
    (slabs, mine, orbits, groups, halves, lines, per, orb_per) = plan
    factors_ref, src_ref, settings_ref = refs[:3]
    peers = refs[3 : 3 + 2 * (groups - 1)]
    refs = refs[3 + 2 * (groups - 1) :]
    others, refs = refs[: halves - 1], refs[halves - 1 :]
    local = settings_ref.shape[1]
    power_ref, gains, outs = refs[0], refs[1], refs[2:10]
    inv, w1, w2, up1, dn1, up2, dn2, sol, data, mat, rhs, hold, sems = refs[10:]
    stores = (inv, w1, w2, up1, dn1, up2, dn2, sol)
    copies = []

    def copy_out(which, low_place, high_place):
        part = pl.ds(low_place, high_place - low_place)
        copy = pltpu.make_async_copy(stores[which].at[part], outs[which].at[part], sems.at[len(copies)])
        copy.start()
        copies.append(copy)

    width = 2 * orbits
    columns = src_ref.shape[-1]
    share = mine // halves
    levels, root = elimination_levels(slabs)
    spot = slots(levels, root)
    places, _ = link_places(slabs, mine, levels)
    lane = lax.broadcasted_iota(jnp.int32, (orbits, width), 1)
    sub = lax.broadcasted_iota(jnp.int32, (orbits, width), 0)
    diag_lane = lane == sub
    first, owner, core, half = where_ref[0], where_ref[1], where_ref[2], where_ref[3]

    for i in range(per):
        at = owner * per + i
        data[at, 0:width, :] = factors_ref[i]
        data[at, width : width + orbits, :] = src_ref[i, 0]
        data[at, width + orbits : 2 * width, :] = src_ref[i, 1]
        data[at, 2 * width : 2 * width + local, :] = settings_ref[i]
    for k in range(1, groups):
        mine_half, other_half = peers[2 * (k - 1)], peers[2 * (k - 1) + 1]
        for i in range(per):
            at = (owner ^ k) * per + i
            data[at, pl.ds(pl.multiple_of(core * width, width), width), :] = mine_half[i, 0:width, :]
            data[at, pl.ds(pl.multiple_of((1 - core) * width, width), width), :] = other_half[i, 0:width, :]
            data[at, 2 * width : 2 * width + local, :] = mine_half[i, width : width + local, :]
    for h in range(1, halves):
        for k in range(groups):
            for i in range(per):
                at = (owner ^ k) * per + i
                data[at, 2 * width + h * local : 2 * width + (h + 1) * local, :] = others[h - 1][k * per + i]

    def assemble(s, unused):
        both = data[s, 0:width, :]
        with_p = times(both, turned(both[:orbits], 3), 1)
        with_q = times(both, turned(both[orbits:], 3), 1)
        hold[s, 0:orbits, 0:width] = with_p[:orbits]
        hold[s, orbits:width, 0:width] = with_q[orbits:]
        before = jnp.maximum(s - 1, 0)
        up1[before] = -with_q[:orbits]
        dn1[before] = -with_p[orbits:]
        return 0

    def assemble_some(place, unused):
        for n in range(ASSEMBLED):
            assemble(place * ASSEMBLED + n, 0)
        return 0

    lax.fori_loop(0, slabs // ASSEMBLED, assemble_some, 0)
    for s in range(slabs // ASSEMBLED * ASSEMBLED, slabs):
        assemble(s, 0)
    largest = largest_shift = None
    for s in range(slabs):
        base = hold[s, orbits:width, 0:width]
        if s + 1 < slabs:
            base = base + hold[s + 1, 0:orbits, 0:width]
        if s == 0:
            base = base + hold[0, 0:orbits, 0:width]
        squares = base * base
        sums = jnp.sum(jnp.sqrt(squares + half_roll(squares)), axis=0, keepdims=True)
        largest = sums if largest is None else jnp.maximum(largest, sums)
        for e in range(mine):
            row = 2 * width + ((e // share) ^ half) * local + first + e % share
            settings = data[s, pl.ds(row, 1), :]
            m = spot[s] * mine + e
            gains[m] = settings
            mat[m] = base + jnp.where(diag_lane, settings, 0.0)
            rhs[m] = data[s, width : 2 * width, :]
            largest_shift = settings if largest_shift is None else jnp.maximum(largest_shift, settings)
    shift_lane = lax.broadcasted_iota(jnp.int32, largest_shift.shape, 1) < orbits
    top = 1.01 * jnp.max(largest + jnp.max(jnp.where(shift_lane, largest_shift, 0.0)))
    copy_out(3, 0, slabs - 1)
    copy_out(4, 0, slabs - 1)

    def held(depth, left, right, e):
        basic, place = places[(depth, left, right, 0)]
        return (up1, dn1, place) if basic else (up2, dn2, place + e)

    low = lane < orbits

    def real_rows(z):
        return jnp.concatenate([jnp.where(low, z, -z), half_roll(z)], axis=0)

    def packed(t, right):
        top, bottom = t[:orbits], t[orbits:]
        return jnp.where(low, half_roll(top), bottom) if right else jnp.where(low, top, half_roll(bottom))

    def around(depth, node, left, right, e):
        to_left = to_right = jnp.zeros((orbits, width), F32)
        inward = []
        if left is not None:
            ups, downs, place = held(depth, left, node, e)
            to_left = downs[place]
            inward.append(real_rows(ups[place]))
        if right is not None:
            ups, downs, place = held(depth, node, right, e)
            to_right = ups[place]
            inward.append(real_rows(downs[place]))
        outward = jnp.concatenate(
            [jnp.where(low, to_left, half_roll(to_right)), jnp.where(low, half_roll(to_left), to_right)], axis=0
        )
        return outward, inward[0] if len(inward) == 1 else jnp.concatenate(inward, axis=0)

    def settle(depth, node, left, right, e, step, inward):
        m = spot[node] * mine + e
        links_step, rhs_step = step[:, :width], step[:, width:]
        sol[m] = rhs_step
        change = times(inward, split(step, 3))
        if left is not None:
            w1[m] = packed(links_step, False)
            ml = spot[left] * mine + e
            mat[ml] = mat[ml] - packed(change[:width, :width], False)
            rhs[ml] = rhs[ml] - change[:width, width:]
        if right is not None:
            w2[m] = packed(links_step, True)
            mr = spot[right] * mine + e
            mat[mr] = mat[mr] - packed(change[-width:, :width], True)
            rhs[mr] = rhs[mr] - change[-width:, width:]
        if left is not None and right is not None:
            ups, downs, place = held(depth + 1, left, right, e)
            ups[place] = -packed(change[:width, :width], True)
            downs[place] = -packed(change[width:, :width], False)

    for depth, level in enumerate(levels):
        invert_batch(mat, inv, spot[level[0][0]] * mine, len(level) * mine, top)
        if depth == 0:
            for node, left, right in level:
                at = spot[node] * mine
                outward, _ = around(depth, node, left, right, 0)
                inverses = [real_rows(inv[at + e]) for e in range(mine)]
                right_parts = split(jnp.concatenate([outward, rhs[at]], axis=1), 3)
                step = times(jnp.concatenate(inverses, axis=0), right_parts)
                for e in range(mine):
                    hold[at + e] = step[e * width : (e + 1) * width]

        def work(energies, depth=depth, level=level):
            found = []
            for node, left, right in level:
                for e in energies:
                    m = spot[node] * mine + e
                    outward, inward = around(depth, node, left, right, e)
                    if depth == 0:
                        step = hold[m]
                    else:
                        step = times(real_rows(inv[m]), split(jnp.concatenate([outward, rhs[m]], axis=1), 3))
                    found.append((node, left, right, e, step, inward))
            for node, left, right, e, step, inward in found:
                settle(depth, node, left, right, e, step, inward)

        over_energies(mine, len(level) > 2, work)
        span = [spot[node] * mine for node, _, _ in level]
        for which in range(3):
            copy_out(which, span[0], span[-1] + mine)
        made = [places[(depth + 1, l, r, e)][1] for _, l, r in level if l is not None and r is not None for e in range(mine)]
        if made:
            copy_out(5, made[0], made[-1] + 1)
            copy_out(6, made[0], made[-1] + 1)
    invert_batch(mat, inv, spot[root] * mine, mine, top)
    for e in range(mine):
        m = spot[root] * mine + e
        sol[m] = tall(times(inv[m], turned(wide(rhs[m]), 3)))
    copy_out(0, spot[root] * mine, (spot[root] + 1) * mine)

    def finished(nodes):
        copy_out(7, spot[nodes[0]] * mine, (spot[nodes[-1]] + 1) * mine)

    def deliver(e, unused):
        for s in range(slabs):
            xr, xi = orbitals_of(sol, spot[s] * mine + e, half, halves, orbits)
            power = xr * xr + xi * xi
            for j in range(lines):
                power_ref[s // per, j, e, s % per, :, :] = power[j * orb_per : (j + 1) * orb_per, :]
        return 0

    finished([root])
    climb(levels, spot, mine, w1, w2, sol, finished)
    lax.fori_loop(0, mine, deliver, 0)
    for copy in copies:
        copy.wait()


def lesser_kernel(plan, where_ref, gains, *refs):
    (slabs, mine, orbits, groups, halves, lines, per, orb_per) = plan
    stores, out_ref = refs[:8], refs[8]
    inv, w1, w2, up1, dn1, up2, dn2, ret, rhs, sol, sems = refs[9:]
    held = (inv, w1, w2, up1, dn1, up2, dn2, ret)
    half = where_ref[3]
    width = 2 * orbits
    levels, root = elimination_levels(slabs)
    spot = slots(levels, root)
    places, _ = link_places(slabs, mine, levels)
    fetches = {}

    def fetch(which, depth, low_place, high_place):
        part = pl.ds(low_place, high_place - low_place)
        copy = pltpu.make_async_copy(stores[which].at[part], held[which].at[part], sems.at[len(fetches)])
        copy.start()
        fetches[(which, depth)] = copy

    spans = []
    for level in levels:
        span = [spot[node] * mine for node, _, _ in level]
        spans.append((span[0], span[-1] + mine))
    spans.append((spot[root] * mine, (spot[root] + 1) * mine))
    for depth, span in enumerate(spans):
        fetch(7, depth, *span)
        fetch(0, depth, *span)
        if depth == 0:
            fetch(3, 0, 0, slabs - 1)
            fetch(4, 0, 0, slabs - 1)
        elif depth < len(levels):
            level = levels[depth - 1]
            made = [places[(depth, l, r, e)][1] for _, l, r in level if l is not None and r is not None for e in range(mine)]
            if made:
                fetch(5, depth, made[0], made[-1] + 1)
                fetch(6, depth, made[0], made[-1] + 1)
    for depth in range(len(levels) - 1, -1, -1):
        fetch(1, depth, *spans[depth])
        fetch(2, depth, *spans[depth])
    for depth in range(len(spans)):
        fetches[(7, depth)].wait()
    lane = lax.broadcasted_iota(jnp.int32, (orbits, width), 1)
    sub = lax.broadcasted_iota(jnp.int32, (orbits, width), 0)
    gain_lane = lane == sub + orbits

    def scale(s, unused):
        for e in range(mine):
            m = s * mine + e
            gain = jnp.sum(jnp.where(gain_lane, gains[m], 0.0), axis=1, keepdims=True)
            rhs[m] = wide(ret[m]) * gain
        return 0

    lax.fori_loop(0, slabs, scale, 0)
    for depth, level in enumerate(levels):
        for which in (0, 3, 4, 5, 6):
            if (which, depth) in fetches:
                fetches[(which, depth)].wait()

        def work(energies, depth=depth, level=level):
            items = [(node, left, right, e) for node, left, right in level for e in energies]
            steps = [times(inv[spot[node] * mine + e], turned(rhs[spot[node] * mine + e], 2)) for node, _, _, e in items]
            changes = []
            for (node, left, right, e), step in zip(items, steps):
                sides = []
                if left is not None:
                    basic, place = places[(depth, left, node, 0)]
                    sides.append(up1[place] if basic else up2[place + e])
                if right is not None:
                    basic, place = places[(depth, node, right, 0)]
                    sides.append(dn1[place] if basic else dn2[place + e])
                sides = sides[0] if len(sides) == 1 else jnp.concatenate(sides, axis=0)
                changes.append(times(sides, turned(step, 2)))
            for (node, left, right, e), step, change in zip(items, steps, changes):
                sol[spot[node] * mine + e] = tall(step)
                if left is not None:
                    ml = spot[left] * mine + e
                    rhs[ml] = rhs[ml] - change[:orbits]
                if right is not None:
                    mr = spot[right] * mine + e
                    rhs[mr] = rhs[mr] - change[-orbits:]

        over_energies(mine, len(level) > 1, work)
    fetches[(0, len(levels))].wait()
    for e in range(mine):
        m = spot[root] * mine + e
        sol[m] = tall(times(inv[m], turned(rhs[m], 2)))
    for depth in range(len(levels)):
        fetches[(1, depth)].wait()
        fetches[(2, depth)].wait()
    climb(levels, spot, mine, w1, w2, sol, lambda nodes: None)

    def deliver(e, unused):
        for s in range(slabs):
            m = spot[s] * mine + e
            xr, xi = orbitals_of(ret, m, half, halves, orbits)
            yr, yi = orbitals_of(sol, m, half, halves, orbits)
            re = xr * yr + xi * yi
            im = xr * yi - xi * yr
            for j in range(lines):
                rows = slice(j * orb_per, (j + 1) * orb_per)
                out_ref[s // per, j, 0, e, s % per, :, :] = re[rows, :]
                out_ref[s // per, j, 1, e, s % per, :, :] = im[rows, :]
        return 0

    lax.fori_loop(0, mine, deliver, 0)


def pack_kernel(where_ref, p_ref, q_ref, src_ref, shift_ref, gain_ref, factors_ref, settings_ref, parcel_ref):
    per, _, orbits, _ = p_ref.shape
    width = 2 * orbits
    local = shift_ref.shape[1]
    core = where_ref[2]
    for i in range(per):
        settings = jnp.concatenate([shift_ref[i], gain_ref[i]], axis=1)
        settings_ref[i] = settings
        parcel_ref[i, width : width + local, :] = settings
        factors_ref[i, 0:orbits, :] = jnp.concatenate([p_ref[i, 0], p_ref[i, 1]], axis=1)
        factors_ref[i, orbits:width, :] = jnp.concatenate([q_ref[i, 0], q_ref[i, 1]], axis=1)

    @pl.when(core == 0)
    def _():
        parcel_ref[:, 0:width, :] = factors_ref[...]

    @pl.when(core != 0)
    def _():
        for i in range(per):
            parcel_ref[i, 0:orbits, :] = src_ref[i, 0]
            parcel_ref[i, orbits:width, :] = src_ref[i, 1]


def pack(where, link_p, link_q, sources, shift, lesser_gain):
    per, _, orbits, _ = link_p.shape
    width = 2 * orbits
    local = shift.shape[1]
    shapes = [(per, width, width), (per, local, width), (per, width + local, sources.shape[-1])]
    return pl.pallas_call(
        pack_kernel,
        out_shape=[jax.ShapeDtypeStruct(shape, F32) for shape in shapes],
        in_specs=[pl.BlockSpec(memory_space=pltpu.SMEM)] + vmem_specs(5),
        out_specs=vmem_specs(3),
        compiler_params=pltpu.CompilerParams(vmem_limit_bytes=VMEM_LIMIT),
        name="pack_parcel",
    )(where, link_p, link_q, sources, shift, lesser_gain)


def vmem_specs(count):
    return [pl.BlockSpec(memory_space=pltpu.VMEM)] * count


def solve_retarded(where, pieces, plan, columns):
    (slabs, mine, orbits, groups, halves, lines, per, orb_per) = plan
    width = 2 * orbits
    nodes = slabs * mine
    levels, _ = elimination_levels(slabs)
    _, fills = link_places(slabs, mine, levels)
    kept = [
        (nodes, orbits, width),
        (nodes, orbits, width),
        (nodes, orbits, width),
        (slabs - 1, orbits, width),
        (slabs - 1, orbits, width),
        (fills, orbits, width),
        (fills, orbits, width),
        (nodes, width, columns),
    ]
    shapes = [(groups, lines, mine, per, orb_per, columns), (nodes, 1, width)] + kept
    return pl.pallas_call(
        functools.partial(retarded_kernel, plan),
        out_shape=[jax.ShapeDtypeStruct(shape, F32) for shape in shapes],
        in_specs=[pl.BlockSpec(memory_space=pltpu.SMEM)] + vmem_specs(len(pieces)),
        out_specs=vmem_specs(2) + [pl.BlockSpec(memory_space=pl.ANY)] * len(kept),
        scratch_shapes=[pltpu.VMEM(shape, F32) for shape in kept]
        + [
            pltpu.VMEM((slabs, 2 * width + halves * pieces[2].shape[1], columns), F32),
            pltpu.VMEM((nodes, orbits, width), F32),
            pltpu.VMEM((nodes, width, columns), F32),
            pltpu.VMEM((len(levels[0]) * mine, width, 2 * width), F32),
            pltpu.SemaphoreType.DMA((6 * len(levels) + 4,)),
        ],
        compiler_params=pltpu.CompilerParams(vmem_limit_bytes=VMEM_LIMIT),
        name="solve_retarded",
    )(where, *pieces)


def solve_lesser(where, stored, plan):
    (slabs, mine, orbits, groups, halves, lines, per, orb_per) = plan
    levels, _ = elimination_levels(slabs)
    gains, kept = stored[0], stored[1:]
    solved = kept[7].shape
    return pl.pallas_call(
        functools.partial(lesser_kernel, plan),
        out_shape=jax.ShapeDtypeStruct((groups, lines, 2, mine, per, orb_per, solved[-1]), F32),
        in_specs=[pl.BlockSpec(memory_space=pltpu.SMEM)]
        + vmem_specs(1)
        + [pl.BlockSpec(memory_space=pl.ANY)] * len(kept),
        out_specs=pl.BlockSpec(memory_space=pltpu.VMEM),
        scratch_shapes=[pltpu.VMEM(array.shape, F32) for array in kept]
        + [pltpu.VMEM((solved[0], solved[1] // 2, 2 * solved[2]), F32), pltpu.VMEM(solved, F32), pltpu.SemaphoreType.DMA((6 * len(levels) + 4,))],
        compiler_params=pltpu.CompilerParams(vmem_limit_bytes=VMEM_LIMIT),
        name="solve_lesser",
    )(where, gains, *kept)


def correlate_kernel(order, power_ref, got_ref, out_ref):
    count = len(order)
    window = 8
    scale = 1.0 / count
    for start in range(0, count, window):
        span = min(window, count - start)
        acc_re = [None] * span
        acc_im = [None] * span
        reach = count - start
        lead = {}
        for energy in range(reach):
            sender, place = order[energy]
            power = power_ref[sender, place, 0]
            for w in range(span):
                at = energy + start + w
                if at >= count:
                    continue
                if at not in lead:
                    s2, p2 = order[at]
                    lead[at] = (got_ref[s2, 0, p2, 0], got_ref[s2, 1, p2, 0])
                re, im = lead[at]
                acc_re[w] = re * power if acc_re[w] is None else acc_re[w] + re * power
                acc_im[w] = im * power if acc_im[w] is None else acc_im[w] + im * power
        for w in range(span):
            out_ref[0, start + w, 0] = acc_re[w] * scale
            out_ref[1, start + w, 0] = acc_im[w] * scale


def correlate(power, got, order):
    senders, kinds, mine, per, rows, columns = got.shape
    count = len(order)
    return pl.pallas_call(
        functools.partial(correlate_kernel, order),
        grid=(per,),
        out_shape=jax.ShapeDtypeStruct((2, count, per, rows, columns), F32),
        in_specs=[
            pl.BlockSpec((senders, mine, 1, rows, columns), lambda i: (0, 0, i, 0, 0)),
            pl.BlockSpec((senders, kinds, mine, 1, rows, columns), lambda i: (0, 0, 0, i, 0, 0)),
        ],
        out_specs=pl.BlockSpec((2, count, 1, rows, columns), lambda i: (0, 0, i, 0, 0)),
        compiler_params=pltpu.CompilerParams(vmem_limit_bytes=VMEM_LIMIT),
        name="correlate",
    )(power, got)


def per_device(link_p, link_q, shift, lesser_gain, sources):
    per, _, orbits, _ = link_p.shape
    columns = sources.shape[-1]
    local = shift.shape[0]
    groups = lax.axis_size("slab")
    halves = lax.axis_size("half")
    lines = lax.axis_size("line")
    slabs = per * groups
    share = max(1, local // groups)
    mine = halves * share
    owner = lax.axis_index("slab")
    half = lax.axis_index("half")
    core = lax.axis_index("line") & 1
    where = jnp.stack([owner * local // groups, owner, core, half]).astype(jnp.int32)
    factors, settings, parcel = pack(
        where, link_p, link_q, sources, jnp.swapaxes(shift, 0, 1), jnp.swapaxes(lesser_gain, 0, 1)
    )
    pieces = [factors, sources, settings]
    fetched = [lax.ppermute(parcel, "slab", [(g, g ^ k) for g in range(groups)]) for k in range(1, groups)]
    siblings = [(j, j ^ 1) for j in range(lines)]
    for piece in fetched:
        pieces.append(piece)
        pieces.append(lax.ppermute(piece, "line", siblings))
    known = jnp.concatenate([settings] + [piece[:, 2 * orbits :] for piece in fetched], axis=0)
    for h in range(1, halves):
        pieces.append(lax.ppermute(known, "half", [(a, a ^ h) for a in range(halves)]))
    plan = (slabs, mine, orbits, groups, halves, lines, per, orbits // (halves * lines))
    power, *stored = solve_retarded(where, pieces, plan, columns)

    def spread(array):
        array = array.reshape((groups * lines,) + array.shape[2:])
        return lax.all_to_all(array, ("slab", "line"), split_axis=0, concat_axis=0, tiled=True)

    power = spread(power)
    got = spread(solve_lesser(where, stored, plan))
    order = []
    for energy in range(halves * lines * local):
        group, row = energy // local, energy % local
        if local >= groups:
            holder, place = row // share, row % share
        else:
            holder, place = -(-row * groups // local), 0
        order.append((holder * lines + group % lines, (group // lines) * share + place))
    return correlate(power, got, tuple(order))


def solution(mesh):
    slab_size, energy_size = mesh.devices.shape
    halves = HALVES if energy_size % (2 * HALVES) == 0 else 1
    split = jax.sharding.Mesh(
        mesh.devices.reshape(slab_size, halves, energy_size // halves), ("slab", "half", "line")
    )
    placed = (
        P("slab", None, None, None),
        P("slab", None, None, None),
        P(("half", "line"), "slab", None),
        P(("half", "line"), "slab", None),
        P("slab", None, None, None),
    )
    return jax.shard_map(
        per_device,
        mesh=split,
        in_specs=placed,
        out_specs=P(None, None, "slab", ("half", "line"), None),
        check_vma=False,
    )
```
